256 devices in a mesh: dp: 32 (over y, x, core), seq: 8 (over z).
Axes of the slice: x: 4, y: 4, z: 8, core: 2. Of those that a mesh axis runs over, the one named last changes fastest.
Arguments:
- hidden_in: bfloat16 [32, 8, 128, 4096], P('dp', 'seq'), may hold values from -6 to 6
- queries: bfloat16 [32, 8, 128, 4096], P('dp', 'seq'), may hold values from -110 to 110
- keys: bfloat16 [32, 8, 128, 512], P('dp', 'seq'), may hold values from -4.5 to 4.5
- values: bfloat16 [32, 8, 128, 512], P('dp', 'seq'), may hold values from -6 to 6
- out_grad: bfloat16 [32, 8, 128, 4096], P('dp', 'seq'), may hold values from -6 to 6
- parents: int32 [32, 8], P('dp', 'seq'), may hold values from 0 to 6, as said below
- counts: int32 [32, 8], P('dp', 'seq'), may hold values from 64 to 128, as said below
Outputs:
- query_grad: bfloat16 [32, 8, 128, 4096], P('dp', 'seq')
- key_grad: bfloat16 [32, 8, 128, 512], P('dp', 'seq')
- value_grad: bfloat16 [32, 8, 128, 512], P('dp', 'seq')
- weight_grad: float32 [4096, 512], P(('dp', 'seq'))
The draws below stay inside these ranges and needn't reach their ends.
Inputs may be any that keep to these rules, and one draw needn't show every extreme that they name: `parents`: segment 0 is its own parent; any other segment i has a parent below i; the last segment's parent is segment 8 - 2. `counts`: at least 64 tokens of each segment are live; some segment of every tree is full.
All inputs are finite; a program needn't handle non-finite values.
Results may differ from the reference program's by a relative error of at most 0.018.
Values may be sent and summed in bfloat16 or wider, within the bound.
No kernel may reach another device: no remote copies, remote signals or barrier semaphores. Data moves between devices by JAX's collectives and lax.ppermute only.
A program may use at most 64 MiB of HBM per device.

```python
import jax
import jax.numpy as jnp
from jax import lax

SEGMENT_SLOTS = 128
HQ = 32
KV_HEAD_COUNT = 4
HEAD_SIZE = 128
MODEL_FEATURES = 4096
QUERY_PER_KV = 8
TREE_SEGMENTS = 8
TREE_COUNT = 32


def shared_keys(key):
    random_base_keys = jax.random.truncated_normal(jax.random.fold_in(key, 101), -4.5, 4.5, (TREE_COUNT, TREE_SEGMENTS, SEGMENT_SLOTS, KV_HEAD_COUNT, HEAD_SIZE), jnp.float32)
    return random_base_keys


def draw_keys(key, part):
    random_base_keys = shared_keys(key)
    return random_base_keys.reshape(TREE_COUNT, TREE_SEGMENTS, SEGMENT_SLOTS, KV_HEAD_COUNT * HEAD_SIZE).astype(jnp.bfloat16)


def draw_queries(key, part):
    key = jax.random.fold_in(key, 2)
    flat_query_rows = jax.random.normal(key, (TREE_COUNT, TREE_SEGMENTS, SEGMENT_SLOTS, KV_HEAD_COUNT, QUERY_PER_KV, HEAD_SIZE), jnp.float32)
    return flat_query_rows.reshape(TREE_COUNT, TREE_SEGMENTS, SEGMENT_SLOTS, HQ * HEAD_SIZE).astype(jnp.bfloat16)


def draw_parents(key, part):
    key = jax.random.fold_in(key, 4)
    labels = jnp.arange(TREE_SEGMENTS, dtype=jnp.int32)
    random_bits = jax.random.randint(key, (TREE_COUNT, TREE_SEGMENTS), 0, 1048576)
    parent_list = random_bits % jnp.maximum(labels, 1)
    return jnp.where(labels == TREE_SEGMENTS - 1, TREE_SEGMENTS - 2, parent_list).astype(jnp.int32)


def draw_counts(key, part):
    key = jax.random.fold_in(key, 5)
    labels = jnp.arange(TREE_SEGMENTS, dtype=jnp.int32)
    live_counts = jax.random.randint(key, (TREE_COUNT, TREE_SEGMENTS), SEGMENT_SLOTS // 2, SEGMENT_SLOTS + 1)
    full_index = jax.random.randint(jax.random.fold_in(key, 6), (TREE_COUNT, 1), 0, TREE_SEGMENTS)
    return jnp.where(labels == full_index, SEGMENT_SLOTS, live_counts).astype(jnp.int32)


def strengthened(array, own_key, source, target, parts, factor):
    owner, partner = [(jnp.arange(array.shape[dim]) // (array.shape[dim] // parts)).reshape([-1 if axis == dim else 1 for axis in range(array.ndim)]) for dim in (source, target)]
    chosen = jax.random.permutation(own_key, parts)[partner]
    strong = (owner == chosen) | (owner == (partner + parts // 2) % parts)
    return jnp.where(strong, factor * array, array)


def block_scale(key, shape, split, least, top_value):
    level = 1.0
    for axis_at, parts in split:
        draws = jax.random.uniform(jax.random.fold_in(jax.random.fold_in(key, 6), axis_at), (parts,), jnp.float32, least / len(split), top_value / len(split))
        level = level * jnp.repeat(jnp.exp(draws), shape[axis_at] // parts).reshape((-1,) + (1,) * (len(shape) - 1 - axis_at))
    return level


def normal_values(stream_key, extent, deviation, most, split=(), held_as=jnp.bfloat16):
    entries = deviation * jax.random.normal(stream_key, extent, jnp.float32)
    if split:
        entries = entries * block_scale(stream_key, extent, split, -0.22, 0.18)
    return jnp.clip(entries, -most, most).astype(held_as)


def bell_draw_with(rng, extent, deviation, reach, cuts, heavy, kind=jnp.bfloat16):
    array = deviation * jax.random.normal(rng, extent, jnp.float32)
    if cuts:
        array = array * block_scale(rng, extent, cuts, -0.22, 0.18)
    return jnp.clip(strengthened(array, jax.random.fold_in(rng, 3), *heavy), -reach, reach).astype(kind)


def setup_inputs(seed: int = 0) -> dict:
    key_of = jax.random.split(jax.random.key(seed), 8)
    hidden_in = bell_draw_with(key_of[0], (TREE_COUNT, TREE_SEGMENTS, SEGMENT_SLOTS, MODEL_FEATURES), 1.0, 6.0, ((0, 32), (1, 8)), (0, 3, 32, 2.75))
    queries = draw_queries(jax.random.fold_in(key_of[7], 71), 0)
    keys = draw_keys(jax.random.fold_in(key_of[7], 71), 0)
    values = normal_values(key_of[3], (TREE_COUNT, TREE_SEGMENTS, SEGMENT_SLOTS, KV_HEAD_COUNT * HEAD_SIZE), 1.0, 6.0, ((0, 32), (1, 8)))
    out_grad = normal_values(key_of[4], (TREE_COUNT, TREE_SEGMENTS, SEGMENT_SLOTS, HQ * HEAD_SIZE), 1.0, 6.0, ((0, 32), (1, 8)))
    parents = draw_parents(jax.random.fold_in(key_of[7], 71), 0)
    counts = draw_counts(jax.random.fold_in(key_of[7], 71), 0)
    return dict(hidden_in=hidden_in, queries=queries, keys=keys, values=values, out_grad=out_grad, parents=parents, counts=counts)


NEG_FILL = -1.0e30


def strict_ancestors(parent_list):
    seg_total = parent_list.shape[0]
    labels = jnp.arange(seg_total, dtype=jnp.int32)
    current = labels
    reached = jnp.zeros((seg_total, seg_total), dtype=bool)
    for _ in range(seg_total - 1):
        current = parent_list[current].astype(jnp.int32)
        reached = reached | (current[:, None] == labels[None, :])
    return reached & (labels[:, None] != labels[None, :])


def allowed_mask(parent_list, live_counts):
    seg_total = parent_list.shape[0]
    ancestors = strict_ancestors(parent_list)
    positions = jnp.arange(SEGMENT_SLOTS, dtype=jnp.int32)
    live_tokens = (positions[None, :] < live_counts[:, None]).reshape(-1)
    seg_label = jnp.repeat(jnp.arange(seg_total, dtype=jnp.int32), SEGMENT_SLOTS)
    pos_label = jnp.tile(positions, seg_total)
    earlier = ancestors[seg_label][:, seg_label]
    same_seg = (seg_label[:, None] == seg_label[None, :]) & (pos_label[None, :] <= pos_label[:, None])
    return live_tokens[:, None] & live_tokens[None, :] & (earlier | same_seg), live_tokens


def group_grads(query_head, grad_head, key_head, value_head, allowed, live_rows):
    score_scale = 1.0 / (HEAD_SIZE ** 0.5)
    query_wide = query_head.astype(jnp.float32)
    grad_wide = grad_head.astype(jnp.float32)
    key_wide = key_head.astype(jnp.float32)
    value_wide = value_head.astype(jnp.float32)
    scores = jnp.einsum("hqd,kd->hqk", query_wide, key_wide) * score_scale
    scores = jnp.where(allowed[None], scores, NEG_FILL)
    row_top = jnp.max(scores, axis=-1, keepdims=True)
    weights = jnp.where(allowed[None], jnp.exp(scores - row_top), 0.0)
    row_total = jnp.sum(weights, axis=-1, keepdims=True)
    row_total = jnp.where(live_rows[None, :, None], row_total, 1.0)
    normed = weights / row_total
    normed_low = lax.optimization_barrier(normed.astype(jnp.bfloat16))
    attended = jnp.einsum("hqk,kd->hqd", normed_low.astype(jnp.float32), value_wide)
    row_delta = jnp.sum(grad_wide * attended, axis=-1, keepdims=True)
    grad_probs = jnp.einsum("hqd,kd->hqk", grad_wide, value_wide)
    grad_scores = lax.optimization_barrier((normed * (grad_probs - row_delta)).astype(jnp.bfloat16))
    grad_wide_scores = grad_scores.astype(jnp.float32)
    query_gradient = (jnp.einsum("hqk,kd->hqd", grad_wide_scores, key_wide) * score_scale).astype(jnp.bfloat16)
    key_gradient = jnp.einsum("hqk,hqd->kd", grad_wide_scores, query_wide) * score_scale
    value_gradient = jnp.einsum("hqk,hqd->kd", normed_low.astype(jnp.float32), grad_wide)
    return query_gradient, key_gradient, value_gradient


def tree_grads(hidden_tree, query_per_tree, key_per_tree, value_per_tree, gradient_per_tree, parent_tree, count_tree):
    token_count_total = TREE_SEGMENTS * SEGMENT_SLOTS
    allowed, live_rows = allowed_mask(parent_tree, count_tree)
    query_pieces = query_per_tree.reshape(token_count_total, KV_HEAD_COUNT, QUERY_PER_KV, HEAD_SIZE).transpose(1, 2, 0, 3)
    split_gradient = gradient_per_tree.reshape(token_count_total, KV_HEAD_COUNT, QUERY_PER_KV, HEAD_SIZE).transpose(1, 2, 0, 3)
    key_pieces = key_per_tree.reshape(token_count_total, KV_HEAD_COUNT, HEAD_SIZE).transpose(1, 0, 2)
    value_pieces = value_per_tree.reshape(token_count_total, KV_HEAD_COUNT, HEAD_SIZE).transpose(1, 0, 2)

    def one_group(pieces):
        return group_grads(pieces[0], pieces[1], pieces[2], pieces[3], allowed, live_rows)

    query_gradient, key_gradient, value_gradient = lax.map(one_group, (query_pieces, split_gradient, key_pieces, value_pieces))
    query_gradient = query_gradient.transpose(2, 0, 1, 3).reshape(TREE_SEGMENTS, SEGMENT_SLOTS, HQ * HEAD_SIZE)
    key_reduced = key_gradient.transpose(1, 0, 2).reshape(token_count_total, KV_HEAD_COUNT * HEAD_SIZE).astype(jnp.bfloat16)
    value_reduced = value_gradient.transpose(1, 0, 2).reshape(token_count_total, KV_HEAD_COUNT * HEAD_SIZE).astype(jnp.bfloat16)
    weight_component = lax.dot_general(hidden_tree.reshape(token_count_total, MODEL_FEATURES), key_reduced, (((0,), (0,)), ((), ())), preferred_element_type=jnp.float32)
    return query_gradient, key_reduced.reshape(TREE_SEGMENTS, SEGMENT_SLOTS, KV_HEAD_COUNT * HEAD_SIZE), value_reduced.reshape(TREE_SEGMENTS, SEGMENT_SLOTS, KV_HEAD_COUNT * HEAD_SIZE), weight_component


def reference(hidden_in, queries, keys, values, out_grad, parents, counts):
    def advance(running, pieces):
        query_gradient, key_reduced, value_reduced, weight_component = tree_grads(*pieces)
        return running + weight_component, (query_gradient, key_reduced, value_reduced)

    initial_sum = jnp.zeros((MODEL_FEATURES, KV_HEAD_COUNT * HEAD_SIZE), jnp.float32)
    weight_grad, outputs = lax.scan(advance, initial_sum, (hidden_in, queries, keys, values, out_grad, parents, counts))
    return outputs[0], outputs[1], outputs[2], weight_grad
```

```python
import functools
import math

import jax
import jax.numpy as jnp
from jax import lax
from jax.experimental import pallas as pl
from jax.experimental.pallas import tpu as pltpu
from jax.sharding import PartitionSpec as P

SEGMENTS = 8
SEG_LEN = 128
KV_HEADS = 4
GROUP = 8
HEAD = 128
KV_COLS = KV_HEADS * HEAD
Q_COLS = KV_HEADS * GROUP * HEAD
GROUP_COLS = GROUP * HEAD
PAIR = 2
SCALE = 1.0 / math.sqrt(HEAD)
SCALE_LOG2 = SCALE * math.log2(math.e)
NEG_FILL = -1e30
DEAD_LSE = 1e30
BF16 = jnp.bfloat16
F32 = jnp.float32

X, Y, CORES = 4, 4, 2


def dot_nt(a, b):
    return lax.dot_general(a, b, (((1,), (1,)), ((), ())), preferred_element_type=F32)


def dot_nn(a, b):
    return lax.dot_general(a, b, (((1,), (0,)), ((), ())), preferred_element_type=F32)


def dot_tn(a, b):
    return lax.dot_general(a, b, (((0,), (0,)), ((), ())), preferred_element_type=F32)


def is_ancestor(meta_ref, me, segment):
    current = me
    hit = segment < 0
    for _ in range(SEGMENTS - 1):
        current = meta_ref[current]
        hit = hit | (current == segment)
    return hit & (segment != me)


def stacked(ref, pair):
    first = pair * PAIR * HEAD
    return jnp.concatenate(
        [ref[:, first + i * HEAD : first + (i + 1) * HEAD] for i in range(PAIR)], axis=0
    )


def key_bias(live):
    position = lax.broadcasted_iota(jnp.int32, (SEG_LEN, 1), 0)
    return jnp.where(position < live, 0.0, NEG_FILL).astype(F32)


def own_bias(live):
    key_at = lax.broadcasted_iota(jnp.int32, (SEG_LEN, PAIR * SEG_LEN), 0)
    query_at = lax.broadcasted_iota(jnp.int32, (SEG_LEN, PAIR * SEG_LEN), 1) & (SEG_LEN - 1)
    return jnp.where((key_at <= query_at) & (key_at < live), 0.0, NEG_FILL).astype(F32)


def segment_id(me, offset):
    return lax.rem(me + (offset + SEGMENTS), SEGMENTS)


def stats_kernel(offsets, first, last, *refs):
    meta_ref, q_ref, g_ref = refs[:3]
    kv_refs = refs[3 : 3 + 2 * len(offsets)]
    rest = refs[3 + 2 * len(offsets) :]
    if first:
        (out_ref,) = rest
    else:
        in_ref, out_ref = rest
    me = meta_ref[2 * SEGMENTS]

    def add_segment(source_ref, k_ref, v_ref, bias, start):
        k, v = k_ref[...], v_ref[...]
        for pair in range(GROUP // PAIR):
            cols = slice(pair * PAIR * HEAD, (pair + 1) * PAIR * HEAD)
            scores = dot_nt(k, stacked(q_ref, pair)) * SCALE_LOG2 + bias
            grad_probs = dot_nt(v, stacked(g_ref, pair))
            top = jnp.max(scores, axis=0, keepdims=True)
            if not start:
                old_top = source_ref[0:1, cols]
                top = jnp.maximum(top, old_top)
            weights = jnp.exp2(scores - top)
            total = jnp.sum(weights, axis=0, keepdims=True)
            mixed = jnp.sum(weights * grad_probs, axis=0, keepdims=True)
            if not start:
                shrink = jnp.exp2(old_top - top)
                total = total + source_ref[1:2, cols] * shrink
                mixed = mixed + source_ref[2:3, cols] * shrink
            out_ref[0:1, cols] = top
            out_ref[1:2, cols] = total
            out_ref[2:3, cols] = mixed

    if first:
        add_segment(
            None, kv_refs[0], kv_refs[1], own_bias(meta_ref[SEGMENTS + me]), True
        )
    else:
        out_ref[...] = in_ref[...]
        for i, offset in enumerate(offsets):
            segment = segment_id(me, offset)

            @pl.when(is_ancestor(meta_ref, me, segment))
            def _():
                add_segment(
                    out_ref,
                    kv_refs[2 * i],
                    kv_refs[2 * i + 1],
                    key_bias(meta_ref[SEGMENTS + segment]),
                    False,
                )

    if last:
        live = meta_ref[SEGMENTS + me]
        position = lax.broadcasted_iota(jnp.int32, (1, GROUP_COLS), 1) & (SEG_LEN - 1)
        total = out_ref[1:2, :]
        row_delta = out_ref[2:3, :] / total
        lse = out_ref[0:1, :] + jnp.log2(total)
        out_ref[0:1, :] = jnp.where(position < live, lse, DEAD_LSE)
        out_ref[1:2, :] = row_delta


def grads_kernel(offsets, first, last, *refs):
    meta_ref, q_ref, g_ref, stats_ref = refs[:4]
    count = len(offsets)
    kv_refs = refs[4 : 4 + 2 * count]
    rest = refs[4 + 2 * count :]
    if first:
        acc_ref, *out_refs = rest
    elif last:
        in_ref, dq_ref, *out_refs, acc_ref = rest
    else:
        in_ref, acc_ref, *out_refs = rest
    me = meta_ref[2 * SEGMENTS]
    if first:
        acc_ref[...] = jnp.zeros_like(acc_ref)
    else:
        acc_ref[...] = in_ref[...]

    def add_segment(k_ref, v_ref, dk_ref, dv_ref, bias):
        k, v = k_ref[...], v_ref[...]
        dk = jnp.zeros((SEG_LEN, HEAD), F32)
        dv = jnp.zeros((SEG_LEN, HEAD), F32)
        for pair in range(GROUP // PAIR):
            cols = slice(pair * PAIR * HEAD, (pair + 1) * PAIR * HEAD)
            q_pair = stacked(q_ref, pair)
            g_pair = stacked(g_ref, pair)
            scores = dot_nt(k, q_pair) * SCALE_LOG2 + bias
            probs = jnp.exp2(scores - stats_ref[0:1, cols])
            grad_probs = dot_nt(v, g_pair)
            grad_scores = (probs * (grad_probs - stats_ref[1:2, cols])).astype(BF16)
            dv += dot_nn(probs.astype(BF16), g_pair)
            dk += dot_nn(grad_scores, q_pair)
            dq = dot_tn(grad_scores, k)
            for i in range(PAIR):
                head = slice((pair * PAIR + i) * HEAD, (pair * PAIR + i + 1) * HEAD)
                acc_ref[:, head] += dq[i * SEG_LEN : (i + 1) * SEG_LEN]
        dk_ref[...] = (dk * SCALE).astype(dk_ref.dtype)
        dv_ref[...] = dv.astype(dv_ref.dtype)

    for i, offset in enumerate(offsets):
        dk_ref, dv_ref = out_refs[2 * i], out_refs[2 * i + 1]
        if offset == 0:
            add_segment(
                kv_refs[2 * i], kv_refs[2 * i + 1], dk_ref, dv_ref, own_bias(meta_ref[SEGMENTS + me])
            )
        else:
            segment = segment_id(me, offset)
            seen = is_ancestor(meta_ref, me, segment)

            @pl.when(seen)
            def _():
                add_segment(
                    kv_refs[2 * i],
                    kv_refs[2 * i + 1],
                    dk_ref,
                    dv_ref,
                    key_bias(meta_ref[SEGMENTS + segment]),
                )

            @pl.when(jnp.logical_not(seen))
            def _():
                dk_ref[...] = jnp.zeros_like(dk_ref)
                dv_ref[...] = jnp.zeros_like(dv_ref)

    if last:
        dq_ref[...] = (acc_ref[...] * SCALE).astype(BF16)


SMEM_SPEC = pl.BlockSpec(memory_space=pltpu.SMEM)
Q_SPEC = pl.BlockSpec((SEG_LEN, GROUP_COLS), lambda g: (0, g))
STATS_SPEC = pl.BlockSpec((8, GROUP_COLS), lambda g: (0, g))
K_SPEC = pl.BlockSpec((SEG_LEN, HEAD), lambda g: (0, g))
V_SPEC = pl.BlockSpec((SEG_LEN, HEAD), lambda g: (0, g + KV_HEADS))
STATS_SHAPE = jax.ShapeDtypeStruct((8, Q_COLS), F32)
BLOCK_FLOPS = 2 * SEG_LEN * SEG_LEN * HEAD * KV_HEADS * GROUP


def add_stats(meta, q, g, packets, offsets, stats, last=False):
    first = stats is None
    operands = [meta, q, g]
    specs = [SMEM_SPEC, Q_SPEC, Q_SPEC]
    for packet in packets:
        operands += [packet, packet]
        specs += [K_SPEC, V_SPEC]
    if not first:
        operands.append(stats)
        specs.append(STATS_SPEC)
    return pl.pallas_call(
        functools.partial(stats_kernel, tuple(offsets), first, last),
        grid=(KV_HEADS,),
        out_shape=STATS_SHAPE,
        in_specs=specs,
        out_specs=STATS_SPEC,
        name="stats",
        cost_estimate=pl.CostEstimate(
            flops=4 * BLOCK_FLOPS * len(packets),
            bytes_accessed=4 * SEG_LEN * Q_COLS,
            transcendentals=SEG_LEN * SEG_LEN * KV_HEADS * GROUP * len(packets),
        ),
        compiler_params=pltpu.CompilerParams(vmem_limit_bytes=32 << 20),
    )(*operands)


def add_grads(meta, q, g, stats, packets, offsets, acc, out_dtype, last=False):
    first = acc is None
    operands = [meta, q, g, stats]
    specs = [SMEM_SPEC, Q_SPEC, Q_SPEC, STATS_SPEC]
    for packet in packets:
        operands += [packet, packet]
        specs += [K_SPEC, V_SPEC]
    aliases = {}
    if not first:
        if not last:
            aliases = {len(operands): 0}
        operands.append(acc)
        specs.append(Q_SPEC)
    out_shapes = [jax.ShapeDtypeStruct((SEG_LEN, Q_COLS), BF16 if last else F32)]
    out_specs = [Q_SPEC]
    for _ in packets:
        out_shapes += [jax.ShapeDtypeStruct((SEG_LEN, KV_COLS), out_dtype)] * 2
        out_specs += [K_SPEC] * 2
    outs = pl.pallas_call(
        functools.partial(grads_kernel, tuple(offsets), first, last),
        grid=(KV_HEADS,),
        out_shape=out_shapes,
        in_specs=specs,
        out_specs=out_specs,
        scratch_shapes=[pltpu.VMEM((SEG_LEN, GROUP_COLS), F32)] if last else [],
        input_output_aliases=aliases,
        name="grads",
        cost_estimate=pl.CostEstimate(
            flops=10 * BLOCK_FLOPS * len(packets),
            bytes_accessed=12 * SEG_LEN * Q_COLS,
            transcendentals=SEG_LEN * SEG_LEN * KV_HEADS * GROUP * len(packets),
        ),
        compiler_params=pltpu.CompilerParams(vmem_limit_bytes=32 << 20),
    )(*operands)
    return outs[0], [(outs[1 + 2 * i], outs[2 + 2 * i]) for i in range(len(packets))]


def shift_seq(array, k):
    return lax.ppermute(array, "seq", [(i, (i + k) % SEGMENTS) for i in range(SEGMENTS)])


def swap_cores(array):
    return lax.ppermute(array, "dp", [(i, i ^ 1) for i in range(X * Y * CORES)])


def shift_x(array, k):
    pairs = [
        ((y * X + x) * CORES + c, (y * X + (x + k) % X) * CORES + c)
        for y in range(Y)
        for x in range(X)
        for c in range(CORES)
    ]
    return lax.ppermute(array, "dp", pairs)


def tree_meta(parents, counts, me):
    slot = jnp.arange(SEGMENTS, dtype=jnp.int32)
    mine = slot == me
    row = jnp.concatenate(
        [jnp.where(mine, parents[0, 0], 0), jnp.where(mine, counts[0, 0], 0)]
    )
    near = jnp.maximum(row, jnp.maximum(shift_seq(row, 1), shift_seq(row, 7)))
    full = jnp.maximum(near, jnp.maximum(shift_seq(near, 3), shift_seq(near, 5)))
    return jnp.concatenate([full, jnp.full((SEGMENTS,), me, jnp.int32)])


def attention_grads(queries, keys, values, out_grad, parents, counts):
    me = lax.axis_index("seq")
    q = queries.reshape(SEG_LEN, Q_COLS)
    g = out_grad.reshape(SEG_LEN, Q_COLS)
    own = jnp.concatenate(
        [keys.reshape(SEG_LEN, KV_COLS), values.reshape(SEG_LEN, KV_COLS)], axis=1
    )
    meta = tree_meta(parents, counts, me)
    up, down = own, own
    packets = {0: own}
    for step in range(1, 5):
        down = shift_seq(down, -1)
        packets[step] = down
        if step < 4:
            up = shift_seq(up, 1)
            packets[-step] = up
    stats = add_stats(meta, q, g, [own], [0], None)
    for step in range(1, 4):
        stats = add_stats(
            meta, q, g, [packets[-step], packets[step]], [-step, step], stats
        )
    stats = add_stats(meta, q, g, [packets[4]], [4], stats, last=True)

    def joined(pair):
        return jnp.concatenate([pair[0].astype(F32), pair[1].astype(F32)], axis=1)

    acc, [far] = add_grads(meta, q, g, stats, [packets[4]], [4], None, BF16)
    down = shift_seq(jnp.concatenate(far, axis=1), -1)
    up = None
    for step in range(3, 0, -1):
        acc, [below, above] = add_grads(
            meta, q, g, stats, [packets[-step], packets[step]], [-step, step], acc, F32
        )
        down = shift_seq((joined(below) + down.astype(F32)).astype(BF16), -1)
        if up is None:
            up = joined(above)
        else:
            up = joined(above) + up.astype(F32)
        up = shift_seq(up.astype(BF16), 1)
    dq, [mine] = add_grads(meta, q, g, stats, [own], [0], acc, F32, last=True)
    key_grad = (
        mine[0] + down[:, :KV_COLS].astype(F32) + up[:, :KV_COLS].astype(F32)
    ).astype(BF16)
    value_grad = (
        mine[1] + down[:, KV_COLS:].astype(F32) + up[:, KV_COLS:].astype(F32)
    ).astype(BF16)
    return dq, key_grad, value_grad


def hidden_by_feature(hidden):
    dp = lax.axis_index("dp")
    core = lax.rem(dp, CORES)
    x = lax.rem(lax.div(dp, CORES), X)
    blocks = hidden.reshape(SEG_LEN, Y, X, CORES, HEAD)
    kept = lax.dynamic_index_in_dim(blocks, core, 3, keepdims=False)
    given = lax.dynamic_index_in_dim(blocks, 1 - core, 3, keepdims=False)
    both = jnp.concatenate([kept, swap_cores(given)], axis=0)
    per_x = both.transpose(2, 0, 1, 3).reshape(X, CORES * SEG_LEN, Y * HEAD)
    received = []
    for k in range(X):
        part = lax.dynamic_index_in_dim(per_x, lax.rem(x + k, X), 0, keepdims=False)
        received.append(shift_x(part, k) if k else part)
    return (
        jnp.concatenate([r[:SEG_LEN] for r in received], axis=0),
        jnp.concatenate([r[SEG_LEN:] for r in received], axis=0),
    )


def project_grad(hidden_parts, key_grad):
    tokens = jnp.concatenate(
        [key_grad] + [shift_x(key_grad, k) for k in range(1, X)], axis=0
    )
    others = swap_cores(tokens)
    partial = (dot_tn(hidden_parts[0], tokens) + dot_tn(hidden_parts[1], others)).astype(BF16)
    groups = [
        [((y * X + x) * CORES + c) * SEGMENTS + z for y in range(Y) for z in range(SEGMENTS)]
        for x in range(X)
        for c in range(CORES)
    ]
    rows = lax.all_to_all(
        partial, ("dp", "seq"), 0, 0, axis_index_groups=groups, tiled=True
    )
    return jnp.sum(rows.reshape(Y * SEGMENTS, -1, KV_COLS).astype(F32), axis=0)


def local(hidden_in, queries, keys, values, out_grad, parents, counts):
    hidden_parts = hidden_by_feature(hidden_in.reshape(SEG_LEN, -1))
    dq, key_grad, value_grad = attention_grads(queries, keys, values, out_grad, parents, counts)
    weight_grad = project_grad(hidden_parts, key_grad)
    return (
        dq.reshape(1, 1, SEG_LEN, Q_COLS),
        key_grad.reshape(1, 1, SEG_LEN, KV_COLS),
        value_grad.reshape(1, 1, SEG_LEN, KV_COLS),
        weight_grad,
    )


def solution(mesh):
    wide = P("dp", "seq", None, None)
    return jax.shard_map(
        local,
        mesh=mesh,
        in_specs=(wide, wide, wide, wide, wide, P("dp", "seq"), P("dp", "seq")),
        out_specs=(wide, wide, wide, P(("dp", "seq"), None)),
        check_vma=False,
    )
```

```python
import functools
import math

import jax
import jax.numpy as jnp
from jax import lax
from jax.experimental import pallas as pl
from jax.experimental.pallas import tpu as pltpu
from jax.sharding import PartitionSpec as P

SEGMENTS = 8
SEG_LEN = 128
KV_HEADS = 4
GROUP = 8
HEAD = 128
KV_COLS = KV_HEADS * HEAD
Q_COLS = KV_HEADS * GROUP * HEAD
GROUP_COLS = GROUP * HEAD
PAIR = 2
SCALE = 1.0 / math.sqrt(HEAD)
SCALE_LOG2 = SCALE * math.log2(math.e)
NEG_FILL = -1e30
DEAD_LSE = 1e30
LABEL_ROWS = 16
STATE = 16
BF16 = jnp.bfloat16
F32 = jnp.float32

X, Y, CORES = 4, 4, 2
SHARE = CORES * HEAD


def dot_nt(a, b):
    return lax.dot_general(a, b, (((1,), (1,)), ((), ())), preferred_element_type=F32)


def dot_nn(a, b):
    return lax.dot_general(a, b, (((1,), (0,)), ((), ())), preferred_element_type=F32)


def dot_tn(a, b):
    return lax.dot_general(a, b, (((0,), (0,)), ((), ())), preferred_element_type=F32)


def stacked(ref, pair):
    first = pair * PAIR * HEAD
    return jnp.concatenate(
        [ref[:, first + i * HEAD : first + (i + 1) * HEAD] for i in range(PAIR)], axis=0
    )


def key_bias(live):
    position = lax.broadcasted_iota(jnp.int32, (SEG_LEN, 1), 0)
    return jnp.where(position < live, 0.0, NEG_FILL).astype(F32)


def own_bias(live):
    key_at = lax.broadcasted_iota(jnp.int32, (SEG_LEN, PAIR * SEG_LEN), 0)
    query_at = lax.broadcasted_iota(jnp.int32, (SEG_LEN, PAIR * SEG_LEN), 1) & (SEG_LEN - 1)
    return jnp.where((key_at <= query_at) & (key_at < live), 0.0, NEG_FILL).astype(F32)


def climb_state(state_ref, out_ref):
    for i in range(SEGMENTS + 1):
        out_ref[i] = state_ref[i]


def stats_kernel(distances, first, last, *refs):
    if first:
        parent_ref, count_ref, q_ref, g_ref, kv_ref, out_ref, state_ref = refs
    else:
        old_ref, q_ref, g_ref = refs[:3]
        packet_refs = refs[3:-3]
        in_ref, out_ref, state_ref = refs[-3:]
    me = lax.axis_index("seq")

    def add_segment(kv_ref, bias, start):
        k, v = kv_ref[:, :HEAD], kv_ref[:, HEAD:]
        for pair in range(GROUP // PAIR):
            cols = slice(pair * PAIR * HEAD, (pair + 1) * PAIR * HEAD)
            scores = dot_nt(k, stacked(q_ref, pair)) * SCALE_LOG2 + bias
            grad_probs = dot_nt(v, stacked(g_ref, pair))
            top = jnp.max(scores, axis=0, keepdims=True)
            if not start:
                old_top = out_ref[0:1, cols]
                top = jnp.maximum(top, old_top)
            weights = jnp.exp2(scores - top)
            total = jnp.sum(weights, axis=0, keepdims=True)
            mixed = jnp.sum(weights * grad_probs, axis=0, keepdims=True)
            if not start:
                shrink = jnp.exp2(old_top - top)
                total = total + out_ref[1:2, cols] * shrink
                mixed = mixed + out_ref[2:3, cols] * shrink
            out_ref[0:1, cols] = top
            out_ref[1:2, cols] = total
            out_ref[2:3, cols] = mixed

    if first:
        live = count_ref[0, 0]
        state_ref[0] = parent_ref[0, 0]
        for i in range(1, SEGMENTS):
            state_ref[i] = 0
        state_ref[SEGMENTS] = live
        add_segment(kv_ref, own_bias(live), True)
    else:
        climb_state(old_ref, state_ref)
        out_ref[...] = in_ref[...]
        for i, distance in enumerate(distances):
            kv_ref, label_ref = packet_refs[2 * i], packet_refs[2 * i + 1]

            @pl.when(state_ref[0] == me - distance)
            def _():
                labels = label_ref[...].astype(F32)
                parent = jnp.max(labels[0:8, :]).astype(jnp.int32)
                live = jnp.max(labels[8:16, :]).astype(jnp.int32)
                state_ref[0] = parent
                state_ref[distance] = live
                add_segment(kv_ref, key_bias(live), False)

    if last:
        live = state_ref[SEGMENTS]
        position = lax.broadcasted_iota(jnp.int32, (1, GROUP_COLS), 1) & (SEG_LEN - 1)
        total = out_ref[1:2, :]
        row_delta = out_ref[2:3, :] / total
        lse = out_ref[0:1, :] + jnp.log2(total)
        out_ref[0:1, :] = jnp.where(position < live, lse, DEAD_LSE)
        out_ref[1:2, :] = row_delta


def grads_kernel(distances, first, last, *refs):
    state_ref, q_ref, g_ref, stats_ref = refs[:4]
    count = len(distances)
    kv_refs = refs[4 : 4 + count]
    rest = refs[4 + count :]
    if first:
        acc_ref, *out_refs = rest
    elif last:
        in_ref, dq_ref, *out_refs, acc_ref = rest
    else:
        in_ref, acc_ref, *out_refs = rest
    if first:
        acc_ref[...] = jnp.zeros_like(acc_ref)
    else:
        acc_ref[...] = in_ref[...]

    def add_segment(kv_ref, out_ref, bias):
        k, v = kv_ref[:, :HEAD], kv_ref[:, HEAD:]
        dk = jnp.zeros((SEG_LEN, HEAD), F32)
        dv = jnp.zeros((SEG_LEN, HEAD), F32)
        for pair in range(GROUP // PAIR):
            cols = slice(pair * PAIR * HEAD, (pair + 1) * PAIR * HEAD)
            q_pair = stacked(q_ref, pair)
            g_pair = stacked(g_ref, pair)
            scores = dot_nt(k, q_pair) * SCALE_LOG2 + bias
            probs = jnp.exp2(scores - stats_ref[0:1, cols])
            grad_probs = dot_nt(v, g_pair)
            grad_scores = (probs * (grad_probs - stats_ref[1:2, cols])).astype(BF16)
            dv += dot_nn(probs.astype(BF16), g_pair)
            dk += dot_nn(grad_scores, q_pair)
            dq = dot_tn(grad_scores, k)
            for i in range(PAIR):
                head = slice((pair * PAIR + i) * HEAD, (pair * PAIR + i + 1) * HEAD)
                acc_ref[:, head] += dq[i * SEG_LEN : (i + 1) * SEG_LEN]
        out_ref[:, :HEAD] = (dk * SCALE).astype(out_ref.dtype)
        out_ref[:, HEAD:] = dv.astype(out_ref.dtype)

    for i, distance in enumerate(distances):
        if distance == 0:
            add_segment(kv_refs[i], out_refs[i], own_bias(state_ref[SEGMENTS]))
        else:
            live = state_ref[distance]

            @pl.when(live > 0)
            def _():
                add_segment(kv_refs[i], out_refs[i], key_bias(live))

            @pl.when(live == 0)
            def _():
                out_refs[i][...] = jnp.zeros_like(out_refs[i])

    if last:
        dq_ref[...] = (acc_ref[...] * SCALE).astype(BF16)


SMEM_SPEC = pl.BlockSpec(memory_space=pltpu.SMEM)
VMEM_SPEC = pl.BlockSpec(memory_space=pltpu.VMEM)
Q_SPEC = pl.BlockSpec((SEG_LEN, GROUP_COLS), lambda g: (0, g))
STATS_SPEC = pl.BlockSpec((8, GROUP_COLS), lambda g: (0, g))
KV_SPEC = pl.BlockSpec((SEG_LEN, 2 * HEAD), lambda g: (0, g))
LABEL_SPEC = pl.BlockSpec((LABEL_ROWS, HEAD), lambda g: (SEG_LEN // LABEL_ROWS, 0))
STATS_SHAPE = jax.ShapeDtypeStruct((8, Q_COLS), F32)
STATE_SHAPE = jax.ShapeDtypeStruct((STATE,), jnp.int32)
BLOCK_FLOPS = 2 * SEG_LEN * SEG_LEN * HEAD * KV_HEADS * GROUP


def add_stats(q, g, packets, distances, state, stats, last=False):
    first = stats is None
    if first:
        operands = [*state, q, g, packets[0]]
        specs = [SMEM_SPEC, SMEM_SPEC, Q_SPEC, Q_SPEC, KV_SPEC]
    else:
        operands = [state, q, g]
        specs = [SMEM_SPEC, Q_SPEC, Q_SPEC]
        for packet in packets:
            operands += [packet, packet]
            specs += [KV_SPEC, LABEL_SPEC]
        operands.append(stats)
        specs.append(STATS_SPEC)
    stats, state = pl.pallas_call(
        functools.partial(stats_kernel, tuple(distances), first, last),
        grid=(KV_HEADS,),
        out_shape=[STATS_SHAPE, STATE_SHAPE],
        in_specs=specs,
        out_specs=[STATS_SPEC, SMEM_SPEC],
        name="stats",
        cost_estimate=pl.CostEstimate(
            flops=4 * BLOCK_FLOPS * len(packets),
            bytes_accessed=4 * SEG_LEN * Q_COLS,
            transcendentals=SEG_LEN * SEG_LEN * KV_HEADS * GROUP * len(packets),
        ),
        compiler_params=pltpu.CompilerParams(vmem_limit_bytes=32 << 20),
    )(*operands)
    return state, stats


def add_grads(state, q, g, stats, packets, distances, acc, out_dtype, last=False):
    first = acc is None
    operands = [state, q, g, stats, *packets]
    specs = [SMEM_SPEC, Q_SPEC, Q_SPEC, STATS_SPEC] + [KV_SPEC] * len(packets)
    aliases = {}
    if not first:
        if not last:
            aliases = {len(operands): 0}
        operands.append(acc)
        specs.append(Q_SPEC)
    out_shapes = [jax.ShapeDtypeStruct((SEG_LEN, Q_COLS), BF16 if last else F32)]
    out_shapes += [jax.ShapeDtypeStruct((SEG_LEN, 2 * KV_COLS), out_dtype)] * len(packets)
    acc, *parts = pl.pallas_call(
        functools.partial(grads_kernel, tuple(distances), first, last),
        grid=(KV_HEADS,),
        out_shape=out_shapes,
        in_specs=specs,
        out_specs=[Q_SPEC] + [KV_SPEC] * len(packets),
        scratch_shapes=[pltpu.VMEM((SEG_LEN, GROUP_COLS), F32)] if last else [],
        input_output_aliases=aliases,
        name="grads",
        cost_estimate=pl.CostEstimate(
            flops=10 * BLOCK_FLOPS * len(packets),
            bytes_accessed=12 * SEG_LEN * Q_COLS,
            transcendentals=SEG_LEN * SEG_LEN * KV_HEADS * GROUP * len(packets),
        ),
        compiler_params=pltpu.CompilerParams(vmem_limit_bytes=32 << 20),
    )(*operands)
    return acc, parts


def shift_seq(array, k):
    return lax.ppermute(array, "seq", [(i, (i + k) % SEGMENTS) for i in range(SEGMENTS)])


def swap_cores(array):
    return lax.ppermute(array, "dp", [(i, i ^ 1) for i in range(X * Y * CORES)])


def dp_index(y, x, core):
    return (y % Y * X + x % X) * CORES + core


def shift_xy(array, along_x, along_y):
    pairs = [
        (dp_index(y, x, c), dp_index(y + along_y, x + along_x, c))
        for y in range(Y)
        for x in range(X)
        for c in range(CORES)
    ]
    return lax.ppermute(array, "dp", pairs)


def swap_seq(array, bit):
    return lax.ppermute(array, "seq", [(i, i ^ bit) for i in range(SEGMENTS)])


def pack_kernel(parent_ref, count_ref, k_ref, v_ref, out_ref):
    for head in range(KV_HEADS):
        cols = slice(head * HEAD, (head + 1) * HEAD)
        first = 2 * head * HEAD
        out_ref[:SEG_LEN, first : first + HEAD] = k_ref[:, cols]
        out_ref[:SEG_LEN, first + HEAD : first + 2 * HEAD] = v_ref[:, cols]
    row = lax.broadcasted_iota(jnp.int32, (LABEL_ROWS, 2 * KV_COLS), 0)
    labels = jnp.where(row < LABEL_ROWS // 2, parent_ref[0, 0], count_ref[0, 0])
    out_ref[SEG_LEN:, :] = labels.astype(F32).astype(BF16)


def ring_packet(keys, values, parents, counts):
    return pl.pallas_call(
        pack_kernel,
        out_shape=jax.ShapeDtypeStruct((SEG_LEN + LABEL_ROWS, 2 * KV_COLS), BF16),
        in_specs=[SMEM_SPEC, SMEM_SPEC, VMEM_SPEC, VMEM_SPEC],
        out_specs=VMEM_SPEC,
        name="pack",
    )(parents, counts, keys, values)


def finish_kernel(mine_ref, down_ref, up_ref, key_ref, value_ref):
    for head in range(KV_HEADS):
        cols = slice(head * HEAD, (head + 1) * HEAD)
        for side, ref in enumerate((key_ref, value_ref)):
            first = (2 * head + side) * HEAD
            part = slice(first, first + HEAD)
            total = mine_ref[:, part] + (
                down_ref[:, part].astype(F32) + up_ref[:, part].astype(F32)
            )
            ref[:, cols] = total.astype(BF16)


def finish(mine, down, up):
    return pl.pallas_call(
        finish_kernel,
        out_shape=[jax.ShapeDtypeStruct((SEG_LEN, KV_COLS), BF16)] * 2,
        in_specs=[VMEM_SPEC] * 3,
        out_specs=[VMEM_SPEC] * 2,
        name="finish",
    )(mine, down, up)


def taken(array, index, axis):
    return lax.dynamic_index_in_dim(array, index, axis, keepdims=False)


def places():
    dp = lax.axis_index("dp")
    core = lax.rem(dp, CORES)
    x = lax.rem(lax.div(dp, CORES), X)
    y = lax.div(dp, CORES * X)
    return y, x, core


def deal_kernel(hidden_ref, *out_refs):
    x = places()[1]
    for k, out_ref in enumerate(out_refs):
        to = lax.rem(x + k, X)
        for y in range(Y):
            first = pl.multiple_of((y * X + to) * SHARE, SHARE)
            out_ref[:, y * SHARE : (y + 1) * SHARE] = hidden_ref[:, pl.ds(first, SHARE)]


def hidden_shifts(hidden):
    parts = pl.pallas_call(
        deal_kernel,
        out_shape=[jax.ShapeDtypeStruct((SEG_LEN, Y * SHARE), BF16)] * X,
        in_specs=[VMEM_SPEC],
        out_specs=[VMEM_SPEC] * X,
        name="deal",
        cost_estimate=pl.CostEstimate(
            flops=0, bytes_accessed=4 * SEG_LEN * Q_COLS, transcendentals=0
        ),
    )(hidden)
    return [shift_xy(part, k, 0) if k else part for k, part in enumerate(parts)]


def given_kernel(*refs):
    hidden_refs, token_refs, (out_ref,) = refs[:X], refs[X : 2 * X], refs[2 * X :]
    core = places()[2]
    tokens = jnp.concatenate([ref[...] for ref in token_refs], axis=0)
    for y in range(Y):
        first = pl.multiple_of(y * SHARE + (1 - core) * HEAD, HEAD)
        hidden = jnp.concatenate([ref[:, pl.ds(first, HEAD)] for ref in hidden_refs], axis=0)
        out_ref[y * HEAD : (y + 1) * HEAD, :] = dot_tn(hidden, tokens).astype(BF16)


def kept_kernel(*refs):
    hidden_refs, token_refs = refs[:X], refs[X : 2 * X]
    got_ref, own_ref, *out_refs = refs[2 * X :]
    here, _, core = places()
    tokens = jnp.concatenate([ref[...] for ref in token_refs], axis=0)
    for k in range(Y):
        y = lax.rem(here + k, Y)
        first = pl.multiple_of(y * SHARE + core * HEAD, HEAD)
        hidden = jnp.concatenate([ref[:, pl.ds(first, HEAD)] for ref in hidden_refs], axis=0)
        rows = pl.ds(pl.multiple_of(y * HEAD, HEAD), HEAD)
        total = dot_tn(hidden, tokens) + got_ref[rows, :].astype(F32)
        if k:
            out_refs[k - 1][...] = total.astype(BF16)
        else:
            own_ref[...] = total


def project_grad(hidden_parts, key_grad):
    tokens = [key_grad] + [shift_xy(key_grad, k, 0) for k in range(1, X)]
    cost = pl.CostEstimate(
        flops=2 * X * SEG_LEN * Y * HEAD * KV_COLS,
        bytes_accessed=4 * SEG_LEN * Q_COLS,
        transcendentals=0,
    )
    given = pl.pallas_call(
        given_kernel,
        out_shape=jax.ShapeDtypeStruct((Y * HEAD, KV_COLS), BF16),
        in_specs=[VMEM_SPEC] * (2 * X),
        out_specs=VMEM_SPEC,
        name="given",
        cost_estimate=cost,
    )(*hidden_parts, *tokens)
    own, *low = pl.pallas_call(
        kept_kernel,
        out_shape=[jax.ShapeDtypeStruct((HEAD, KV_COLS), F32)]
        + [jax.ShapeDtypeStruct((HEAD, KV_COLS), BF16)] * (Y - 1),
        in_specs=[VMEM_SPEC] * (2 * X + 1),
        out_specs=[VMEM_SPEC] * Y,
        name="kept",
        cost_estimate=cost,
    )(*hidden_parts, *tokens, swap_cores(given))
    total = own
    for k in range(1, Y):
        total = total + shift_xy(low[k - 1], 0, k).astype(F32)
    z = lax.axis_index("seq")
    for bit in (1, 2, 4):
        halves = total.reshape(-1, 2, 16, KV_COLS)
        side = lax.rem(lax.div(z, bit), 2)
        got = swap_seq(taken(halves, 1 - side, 1).astype(BF16), bit)
        total = taken(halves, side, 1) + got.astype(F32)
    return total.reshape(16, KV_COLS)


def attention_grads(hidden, queries, keys, values, out_grad, parents, counts):
    q = queries.reshape(SEG_LEN, Q_COLS)
    g = out_grad.reshape(SEG_LEN, Q_COLS)
    own = ring_packet(
        keys.reshape(SEG_LEN, KV_COLS), values.reshape(SEG_LEN, KV_COLS), parents, counts
    )
    up, down = own, own
    below, above = {}, {}
    hidden_parts = None
    for step in range(1, 5):
        down = shift_seq(down, -1)
        above[step] = down
        if step < 4:
            up = shift_seq(up, 1)
            below[step] = up
        if step == 1:
            hidden_parts = hidden_shifts(hidden)
    state, stats = add_stats(q, g, [own], [0], (parents, counts), None)
    for step in range(1, 4):
        state, stats = add_stats(q, g, [below[step]], [step], state, stats)
    stats, *hidden_parts = lax.optimization_barrier((stats, *hidden_parts))
    state, stats = add_stats(
        q, g, [above[s] for s in (4, 3, 2, 1)], [4, 5, 6, 7], state, stats, last=True
    )

    acc, [far] = add_grads(state, q, g, stats, [above[4]], [4], None, BF16)
    down = shift_seq(far, -1)
    up = None
    for step in range(3, 0, -1):
        acc, [low, high] = add_grads(
            state, q, g, stats, [below[step], above[step]], [step, 8 - step], acc, F32
        )
        down = shift_seq((low + down.astype(F32)).astype(BF16), -1)
        up = shift_seq((high if up is None else high + up.astype(F32)).astype(BF16), 1)
    dq, [mine] = add_grads(state, q, g, stats, [own], [0], acc, F32, last=True)
    key_grad, value_grad = finish(mine, down, up)
    return dq, key_grad, value_grad, hidden_parts


def local(hidden_in, queries, keys, values, out_grad, parents, counts):
    dq, key_grad, value_grad, hidden_parts = attention_grads(
        hidden_in.reshape(SEG_LEN, -1), queries, keys, values, out_grad, parents, counts
    )
    weight_grad = project_grad(hidden_parts, key_grad)
    return (
        dq.reshape(1, 1, SEG_LEN, Q_COLS),
        key_grad.reshape(1, 1, SEG_LEN, KV_COLS),
        value_grad.reshape(1, 1, SEG_LEN, KV_COLS),
        weight_grad,
    )


def solution(mesh):
    wide = P("dp", "seq", None, None)
    return jax.shard_map(
        local,
        mesh=mesh,
        in_specs=(wide, wide, wide, wide, wide, P("dp", "seq"), P("dp", "seq")),
        out_specs=(wide, wide, wide, P(("dp", "seq"), None)),
        check_vma=False,
    )
```

```python
import functools
import math

import jax
import jax.numpy as jnp
from jax import lax
from jax.experimental import pallas as pl
from jax.experimental.pallas import tpu as pltpu
from jax.sharding import PartitionSpec as P

SEGMENTS = 8
SEG_LEN = 128
KV_HEADS = 4
GROUP = 8
HEAD = 128
KV_COLS = KV_HEADS * HEAD
Q_COLS = KV_HEADS * GROUP * HEAD
GROUP_COLS = GROUP * HEAD
STATS_HEADS = 2
KERNEL_VMEM = 16 << 20
SCALE = 1.0 / math.sqrt(HEAD)
SCALE_LOG2 = SCALE * math.log2(math.e)
NEG_FILL = -1e30
DEAD_LSE = 1e30
LABEL_ROWS = 16
STATE = 16
BF16 = jnp.bfloat16
F32 = jnp.float32

X, Y, CORES = 4, 4, 2
SHARE = CORES * HEAD


def dot_nt(a, b):
    return lax.dot_general(a, b, (((1,), (1,)), ((), ())), preferred_element_type=F32)


def dot_nn(a, b):
    return lax.dot_general(a, b, (((1,), (0,)), ((), ())), preferred_element_type=F32)


def dot_tn(a, b):
    return lax.dot_general(a, b, (((0,), (0,)), ((), ())), preferred_element_type=F32)


def key_bias(live):
    position = lax.broadcasted_iota(jnp.int32, (SEG_LEN, 1), 0)
    return jnp.where(position < live, 0.0, NEG_FILL).astype(F32)


def own_bias(live, heads):
    key_at = lax.broadcasted_iota(jnp.int32, (SEG_LEN, SEG_LEN), 0)
    query_at = lax.broadcasted_iota(jnp.int32, (SEG_LEN, SEG_LEN), 1)
    tile = jnp.where((key_at <= query_at) & (key_at < live), 0.0, NEG_FILL).astype(F32)
    return jnp.concatenate([tile] * heads, axis=1)


def key_value(ref, group):
    first = 2 * group * HEAD
    return ref[:SEG_LEN, first : first + HEAD], ref[:SEG_LEN, first + HEAD : first + 2 * HEAD]


def group_cols(group):
    return slice(group * GROUP_COLS, (group + 1) * GROUP_COLS)


def prep_kernel(q_ref, g_ref, *out_refs):
    for ref, (rows_ref, turned_ref) in ((q_ref, out_refs[:2]), (g_ref, out_refs[2:])):
        for head in range(KV_HEADS * GROUP):
            part = slice(head * HEAD, (head + 1) * HEAD)
            block = ref[:, part]
            rows_ref[part, :] = block
            turned_ref[:, part] = block.T


def stats_kernel(distances, first, last, *refs):
    if first:
        parent_ref, count_ref, q_ref, g_ref, packet_ref, out_ref, state_ref = refs
    else:
        old_ref, q_ref, g_ref = refs[:3]
        packet_refs = refs[3:-3]
        in_ref, out_ref, state_ref = refs[-3:]
    me = lax.axis_index("seq")

    def add_segment(packet_ref, bias, start):
        width = STATS_HEADS * HEAD
        for group in range(KV_HEADS):
            k, v = key_value(packet_ref, group)
            for chunk in range(GROUP_COLS // width):
                at = group * GROUP_COLS + chunk * width
                cols = slice(at, at + width)
                scores = dot_nn(k, q_ref[:, cols]) * SCALE_LOG2 + bias
                grad_probs = dot_nn(v, g_ref[:, cols])
                top = jnp.max(scores, axis=0, keepdims=True)
                if not start:
                    old_top = out_ref[0:1, cols]
                    top = jnp.maximum(top, old_top)
                weights = jnp.exp2(scores - top)
                total = jnp.sum(weights, axis=0, keepdims=True)
                mixed = jnp.sum(weights * grad_probs, axis=0, keepdims=True)
                if not start:
                    shrink = jnp.exp2(old_top - top)
                    total = total + out_ref[1:2, cols] * shrink
                    mixed = mixed + out_ref[2:3, cols] * shrink
                out_ref[0:1, cols] = top
                out_ref[1:2, cols] = total
                out_ref[2:3, cols] = mixed

    if first:
        live = count_ref[0, 0]
        state_ref[0] = parent_ref[0, 0]
        for i in range(1, SEGMENTS):
            state_ref[i] = 0
        state_ref[SEGMENTS] = live
        add_segment(packet_ref, own_bias(live, STATS_HEADS), True)
    else:
        for i in range(SEGMENTS + 1):
            state_ref[i] = old_ref[i]
        out_ref[...] = in_ref[...]
        for packet_ref, distance in zip(packet_refs, distances):

            @pl.when(state_ref[0] == me - distance)
            def _():
                labels = packet_ref[SEG_LEN:, :HEAD].astype(F32)
                parent = jnp.max(labels[: LABEL_ROWS // 2, :]).astype(jnp.int32)
                live = jnp.max(labels[LABEL_ROWS // 2 :, :]).astype(jnp.int32)
                state_ref[0] = parent
                state_ref[distance] = live
                add_segment(packet_ref, key_bias(live), False)

    if last:
        live = state_ref[SEGMENTS]
        position = lax.broadcasted_iota(jnp.int32, (1, Q_COLS), 1) & (SEG_LEN - 1)
        total = out_ref[1:2, :]
        row_delta = out_ref[2:3, :] / total
        lse = out_ref[0:1, :] + jnp.log2(total)
        out_ref[0:1, :] = jnp.where(position < live, lse, DEAD_LSE)
        out_ref[1:2, :] = row_delta


def grads_kernel(distances, first, last, *refs):
    state_ref, q_ref, qt_ref, g_ref, gt_ref, stats_ref = refs[:6]
    count = len(distances)
    packet_refs = refs[6 : 6 + count]
    rest = refs[6 + count :]
    if first:
        acc_ref, *out_refs = rest
    else:
        in_ref, acc_ref, *out_refs = rest

    def add_segment(packet_ref, out_ref, bias, source_ref):
        for group in range(KV_HEADS):
            k, v = key_value(packet_ref, group)
            cols = group_cols(group)
            scores = dot_nn(k, qt_ref[:, cols]) * SCALE_LOG2 + bias
            probs = jnp.exp2(scores - stats_ref[0:1, cols])
            grad_probs = dot_nn(v, gt_ref[:, cols])
            grad_scores = (probs * (grad_probs - stats_ref[1:2, cols])).astype(BF16)
            dv = dot_nn(probs.astype(BF16), g_ref[cols, :])
            dk = dot_nn(grad_scores, q_ref[cols, :]) * SCALE
            dq = dot_nn(k.T, grad_scores)
            if source_ref is not None:
                dq = dq + source_ref[:, cols]
            if last:
                for head in range(GROUP):
                    part = slice(head * HEAD, (head + 1) * HEAD)
                    at = (group * GROUP + head) * HEAD
                    acc_ref[:, at : at + HEAD] = (dq[:, part] * SCALE).T.astype(BF16)
            else:
                acc_ref[:, cols] = dq
            first_col = 2 * group * HEAD
            out_ref[:, first_col : first_col + HEAD] = dk.astype(out_ref.dtype)
            out_ref[:, first_col + HEAD : first_col + 2 * HEAD] = dv.astype(out_ref.dtype)

    if last:
        add_segment(
            packet_refs[0], out_refs[0], own_bias(state_ref[SEGMENTS], GROUP), in_ref
        )
        return
    source_ref = None if first else in_ref
    for packet_ref, out_ref, distance in zip(packet_refs, out_refs, distances):
        live = state_ref[distance]

        @pl.when(live > 0)
        def _():
            add_segment(packet_ref, out_ref, key_bias(live), source_ref)

        @pl.when(live == 0)
        def _():
            out_ref[...] = jnp.zeros_like(out_ref)
            if source_ref is None:
                acc_ref[...] = jnp.zeros_like(acc_ref)
            elif source_ref is not acc_ref:
                acc_ref[...] = source_ref[...]

        source_ref = acc_ref


SMEM_SPEC = pl.BlockSpec(memory_space=pltpu.SMEM)
VMEM_SPEC = pl.BlockSpec(memory_space=pltpu.VMEM)
STATS_SHAPE = jax.ShapeDtypeStruct((8, Q_COLS), F32)
STATE_SHAPE = jax.ShapeDtypeStruct((STATE,), jnp.int32)
BLOCK_FLOPS = 2 * SEG_LEN * SEG_LEN * HEAD * KV_HEADS * GROUP


def on_core(kernel, name, out_shape, operands, scalars=0, out_specs=None, flops=0, aliases=None):
    many = isinstance(out_shape, list)
    if out_specs is None:
        out_specs = [VMEM_SPEC] * len(out_shape) if many else VMEM_SPEC
    moved = sum(o.size * o.dtype.itemsize for o in operands)
    return pl.pallas_call(
        kernel,
        out_shape=out_shape,
        in_specs=[SMEM_SPEC] * scalars + [VMEM_SPEC] * (len(operands) - scalars),
        out_specs=out_specs,
        name=name,
        input_output_aliases=aliases or {},
        cost_estimate=pl.CostEstimate(flops=flops, bytes_accessed=moved, transcendentals=0),
        compiler_params=pltpu.CompilerParams(vmem_limit_bytes=KERNEL_VMEM),
    )(*operands)


def prepared(array_q, array_g):
    shapes = [(KV_HEADS * GROUP * SEG_LEN, HEAD), (HEAD, KV_HEADS * GROUP * SEG_LEN)] * 2
    return on_core(
        prep_kernel,
        "prep",
        [jax.ShapeDtypeStruct(shape, BF16) for shape in shapes],
        [array_q, array_g],
    )


def add_stats(heads, packets, distances, state, stats, last=False):
    _, qt, _, gt = heads
    first = stats is None
    scalars = list(state) if first else [state]
    operands = [*scalars, qt, gt, *packets]
    if not first:
        operands.append(stats)
    stats, state = on_core(
        functools.partial(stats_kernel, tuple(distances), first, last),
        "stats",
        [STATS_SHAPE, STATE_SHAPE],
        operands,
        scalars=len(scalars),
        out_specs=[VMEM_SPEC, SMEM_SPEC],
        flops=4 * BLOCK_FLOPS * len(packets),
    )
    return state, stats


def add_grads(heads, state, stats, packets, distances, acc, out_dtype, last=False):
    first = acc is None
    operands = [state, *heads, stats, *packets]
    aliases = {}
    if not first:
        if not last:
            aliases = {len(operands): 0}
        operands.append(acc)
    if last:
        out_shapes = [jax.ShapeDtypeStruct((SEG_LEN, Q_COLS), BF16)]
    else:
        out_shapes = [jax.ShapeDtypeStruct((HEAD, Q_COLS), F32)]
    out_shapes += [jax.ShapeDtypeStruct((SEG_LEN, 2 * KV_COLS), out_dtype)] * len(packets)
    acc, *parts = on_core(
        functools.partial(grads_kernel, tuple(distances), first, last),
        "grads",
        out_shapes,
        operands,
        scalars=1,
        flops=10 * BLOCK_FLOPS * len(packets),
        aliases=aliases,
    )
    return acc, parts


def shift_seq(array, k):
    return lax.ppermute(array, "seq", [(i, (i + k) % SEGMENTS) for i in range(SEGMENTS)])


def swap_cores(array):
    return lax.ppermute(array, "dp", [(i, i ^ 1) for i in range(X * Y * CORES)])


def dp_index(y, x, core):
    return (y % Y * X + x % X) * CORES + core


def shift_xy(array, along_x, along_y):
    pairs = [
        (dp_index(y, x, c), dp_index(y + along_y, x + along_x, c))
        for y in range(Y)
        for x in range(X)
        for c in range(CORES)
    ]
    return lax.ppermute(array, "dp", pairs)


def swap_seq(array, bit):
    return lax.ppermute(array, "seq", [(i, i ^ bit) for i in range(SEGMENTS)])


def pack_kernel(parent_ref, count_ref, k_ref, v_ref, out_ref):
    for head in range(KV_HEADS):
        cols = slice(head * HEAD, (head + 1) * HEAD)
        first = 2 * head * HEAD
        out_ref[:SEG_LEN, first : first + HEAD] = k_ref[:, cols]
        out_ref[:SEG_LEN, first + HEAD : first + 2 * HEAD] = v_ref[:, cols]
    row = lax.broadcasted_iota(jnp.int32, (LABEL_ROWS, 2 * KV_COLS), 0)
    labels = jnp.where(row < LABEL_ROWS // 2, parent_ref[0, 0], count_ref[0, 0])
    out_ref[SEG_LEN:, :] = labels.astype(F32).astype(BF16)


def ring_packet(keys, values, parents, counts):
    return on_core(
        pack_kernel,
        "pack",
        jax.ShapeDtypeStruct((SEG_LEN + LABEL_ROWS, 2 * KV_COLS), BF16),
        [parents, counts, keys, values],
        scalars=2,
    )


def finish_kernel(mine_ref, down_ref, up_ref, key_ref, value_ref, near_ref):
    for head in range(KV_HEADS):
        cols = slice(head * HEAD, (head + 1) * HEAD)
        for side, ref in enumerate((key_ref, value_ref)):
            first = (2 * head + side) * HEAD
            part = slice(first, first + HEAD)
            total = mine_ref[:, part] + (
                down_ref[:, part].astype(F32) + up_ref[:, part].astype(F32)
            )
            ref[:, cols] = total.astype(BF16)
            if side == 0:
                near_ref[:, cols] = total.astype(BF16)


def finish(mine, down, up):
    return on_core(
        finish_kernel,
        "finish",
        [jax.ShapeDtypeStruct((SEG_LEN, KV_COLS), BF16)] * 3,
        [mine, down, up],
    )


def taken(array, index, axis):
    return lax.dynamic_index_in_dim(array, index, axis, keepdims=False)


def places():
    dp = lax.axis_index("dp")
    core = lax.rem(dp, CORES)
    x = lax.rem(lax.div(dp, CORES), X)
    y = lax.div(dp, CORES * X)
    return y, x, core


def deal_kernel(hidden_ref, *out_refs):
    x = places()[1]
    for k, out_ref in enumerate(out_refs):
        to = lax.rem(x + k, X)
        for y in range(Y):
            first = pl.multiple_of((y * X + to) * SHARE, SHARE)
            out_ref[:, y * SHARE : (y + 1) * SHARE] = hidden_ref[:, pl.ds(first, SHARE)]


def hidden_shares(hidden):
    return on_core(
        deal_kernel, "deal", [jax.ShapeDtypeStruct((SEG_LEN, Y * SHARE), BF16)] * X, [hidden]
    )


def turn_kernel(*refs):
    part_refs, out_refs = refs[:X], refs[X:]
    here, _, core = places()
    for side, out_ref in enumerate(out_refs):
        for k in range(Y):
            of = lax.rem(here + k, Y) * CORES + lax.rem(core + side, CORES)
            first = pl.multiple_of(of * HEAD, HEAD)
            for i, ref in enumerate(part_refs):
                out_ref[k * HEAD : (k + 1) * HEAD, i * SEG_LEN : (i + 1) * SEG_LEN] = ref[
                    :, pl.ds(first, HEAD)
                ].T


def turned(parts):
    return on_core(
        turn_kernel,
        "turn",
        [jax.ShapeDtypeStruct((Y * HEAD, X * SEG_LEN), BF16)] * CORES,
        list(parts),
    )


def given_kernel(hidden_ref, *refs):
    token_refs, (out_ref,) = refs[:X], refs[X:]
    tokens = jnp.concatenate([ref[...] for ref in token_refs], axis=0)
    out_ref[...] = dot_nn(hidden_ref[...], tokens).astype(BF16)


def kept_kernel(hidden_ref, *refs):
    token_refs, got_ref, own_ref, out_refs = refs[:X], refs[X], refs[X + 1], refs[X + 2 :]
    tokens = jnp.concatenate([ref[...] for ref in token_refs], axis=0)
    total = dot_nn(hidden_ref[...], tokens) + got_ref[...].astype(F32)
    own_ref[...] = total[:HEAD]
    for k, ref in enumerate(out_refs):
        ref[...] = total[(k + 1) * HEAD : (k + 2) * HEAD].astype(BF16)


def project_grad(hidden_own, hidden_other, key_grad):
    tokens = [key_grad] + [shift_xy(key_grad, k, 0) for k in range(1, X)]
    flops = 2 * X * SEG_LEN * Y * HEAD * KV_COLS
    given = on_core(
        given_kernel,
        "given",
        jax.ShapeDtypeStruct((Y * HEAD, KV_COLS), BF16),
        [hidden_other, *tokens],
        flops=flops,
    )
    own, *low = on_core(
        kept_kernel,
        "kept",
        [jax.ShapeDtypeStruct((HEAD, KV_COLS), F32)]
        + [jax.ShapeDtypeStruct((HEAD, KV_COLS), BF16)] * (Y - 1),
        [hidden_own, *tokens, swap_cores(given)],
        flops=flops,
    )
    total = own
    for k in range(1, Y):
        total = total + shift_xy(low[k - 1], 0, k).astype(F32)
    z = lax.axis_index("seq")
    for bit in (1, 2, 4):
        halves = total.reshape(-1, 2, 16, KV_COLS)
        side = lax.rem(lax.div(z, bit), 2)
        got = swap_seq(taken(halves, 1 - side, 1).astype(BF16), bit)
        total = taken(halves, side, 1) + got.astype(F32)
    return total.reshape(16, KV_COLS)


def all_grads(hidden, queries, keys, values, out_grad, parents, counts):
    barrier = lax.optimization_barrier
    own = ring_packet(
        keys.reshape(SEG_LEN, KV_COLS), values.reshape(SEG_LEN, KV_COLS), parents, counts
    )
    up, down = own, own
    below, above = {}, {}
    state, stats = (parents, counts), None
    hidden_parts = None
    for step in range(1, 5):
        if step == 2:
            heads = prepared(queries.reshape(SEG_LEN, Q_COLS), out_grad.reshape(SEG_LEN, Q_COLS))
            up, down, *heads = barrier((up, down, *heads))
        if step == 3:
            shares = hidden_shares(hidden)
            state, stats = add_stats(heads, [own], [0], state, None)
            up, down, state, stats, *shares = barrier((up, down, state, stats, *shares))
            hidden_parts = [
                shift_xy(share, k, 0) if k else share for k, share in enumerate(shares)
            ]
        if step == 4:
            for done in (1, 2):
                state, stats = add_stats(heads, [below[done]], [done], state, stats)
            down, state, stats = barrier((down, state, stats))
        down = shift_seq(down, -1)
        above[step] = down
        if step < 4:
            up = shift_seq(up, 1)
            below[step] = up
    state, stats = add_stats(heads, [below[3]], [3], state, stats)
    stats, *hidden_parts = barrier((stats, *hidden_parts))
    state, stats = add_stats(
        heads, [above[s] for s in (4, 3, 2, 1)], [4, 5, 6, 7], state, stats, last=True
    )

    acc, [far] = add_grads(heads, state, stats, [above[4]], [4], None, BF16)
    down = shift_seq(far, -1)
    up = None
    for step in range(3, 0, -1):
        acc, [low, high] = add_grads(
            heads, state, stats, [below[step], above[step]], [step, 8 - step], acc, F32
        )
        down = shift_seq((low + down.astype(F32)).astype(BF16), -1)
        up = shift_seq((high if up is None else high + up.astype(F32)).astype(BF16), 1)
        if step == 1:
            acc, *hidden_parts = barrier((acc, *turned(hidden_parts)))
    dq, [mine] = add_grads(heads, state, stats, [own], [0], acc, F32, last=True)
    key_grad, value_grad, near = finish(mine, down, up)
    return dq, key_grad, value_grad, project_grad(*hidden_parts, near)


def local(hidden_in, queries, keys, values, out_grad, parents, counts):
    dq, key_grad, value_grad, weight_grad = all_grads(
        hidden_in.reshape(SEG_LEN, -1), queries, keys, values, out_grad, parents, counts
    )
    return (
        dq.reshape(1, 1, SEG_LEN, Q_COLS),
        key_grad.reshape(1, 1, SEG_LEN, KV_COLS),
        value_grad.reshape(1, 1, SEG_LEN, KV_COLS),
        weight_grad,
    )


def solution(mesh):
    wide = P("dp", "seq", None, None)
    return jax.shard_map(
        local,
        mesh=mesh,
        in_specs=(wide, wide, wide, wide, wide, P("dp", "seq"), P("dp", "seq")),
        out_specs=(wide, wide, wide, P(("dp", "seq"), None)),
        check_vma=False,
    )
```

```python
import functools
import math

import jax
import jax.numpy as jnp
from jax import lax
from jax.experimental import pallas as pl
from jax.experimental.pallas import tpu as pltpu
from jax.sharding import PartitionSpec as P

SEGMENTS = 8
SEG_LEN = 128
KV_HEADS = 4
GROUP = 8
HEAD = 128
KV_COLS = KV_HEADS * HEAD
Q_COLS = KV_HEADS * GROUP * HEAD
GROUP_COLS = GROUP * HEAD
STATS_HEADS = 2
KERNEL_VMEM = 16 << 20
SCALE = 1.0 / math.sqrt(HEAD)
SCALE_LOG2 = SCALE * math.log2(math.e)
NEG_FILL = -1e30
DEAD_LSE = 1e30
LABEL_ROWS = 16
PACKET_ROWS = 2 * KV_HEADS * SEG_LEN
STATE = 16
BF16 = jnp.bfloat16
F32 = jnp.float32

X, Y, CORES = 4, 4, 2
SHARE = CORES * HEAD


def dot_nt(a, b):
    return lax.dot_general(a, b, (((1,), (1,)), ((), ())), preferred_element_type=F32)


def dot_nn(a, b):
    return lax.dot_general(a, b, (((1,), (0,)), ((), ())), preferred_element_type=F32)


def dot_tn(a, b):
    return lax.dot_general(a, b, (((0,), (0,)), ((), ())), preferred_element_type=F32)


def key_bias(live):
    position = lax.broadcasted_iota(jnp.int32, (SEG_LEN, 1), 0)
    return jnp.where(position < live, 0.0, NEG_FILL).astype(F32)


def own_bias(live, heads):
    key_at = lax.broadcasted_iota(jnp.int32, (SEG_LEN, SEG_LEN), 0)
    query_at = lax.broadcasted_iota(jnp.int32, (SEG_LEN, SEG_LEN), 1)
    tile = jnp.where((key_at <= query_at) & (key_at < live), 0.0, NEG_FILL).astype(F32)
    return jnp.concatenate([tile] * heads, axis=1)


def block_rows(group, side):
    first = (2 * group + side) * SEG_LEN
    return slice(first, first + SEG_LEN)


def key_value(ref, group):
    return ref[block_rows(group, 0), :], ref[block_rows(group, 1), :]


def group_cols(group):
    return slice(group * GROUP_COLS, (group + 1) * GROUP_COLS)


def prep_kernel(q_ref, g_ref, *out_refs):
    for ref, (rows_ref, turned_ref) in ((q_ref, out_refs[:2]), (g_ref, out_refs[2:])):
        for head in range(KV_HEADS * GROUP):
            part = slice(head * HEAD, (head + 1) * HEAD)
            block = ref[:, part]
            rows_ref[part, :] = block
            turned_ref[:, part] = block.T


def stats_kernel(distances, first, last, *refs):
    if first:
        parent_ref, count_ref, q_ref, g_ref, packet_ref, out_ref, state_ref = refs
    else:
        old_ref, q_ref, g_ref = refs[:3]
        packet_refs = refs[3:-3]
        in_ref, out_ref, state_ref = refs[-3:]
    me = lax.axis_index("seq")

    def add_segment(packet_ref, bias, start):
        width = STATS_HEADS * HEAD
        for group in range(KV_HEADS):
            k, v = key_value(packet_ref, group)
            for chunk in range(GROUP_COLS // width):
                at = group * GROUP_COLS + chunk * width
                cols = slice(at, at + width)
                scores = dot_nn(k, q_ref[:, cols]) * SCALE_LOG2 + bias
                grad_probs = dot_nn(v, g_ref[:, cols])
                top = jnp.max(scores, axis=0, keepdims=True)
                if not start:
                    old_top = out_ref[0:1, cols]
                    top = jnp.maximum(top, old_top)
                weights = jnp.exp2(scores - top)
                total = jnp.sum(weights, axis=0, keepdims=True)
                mixed = jnp.sum(weights * grad_probs, axis=0, keepdims=True)
                if not start:
                    shrink = jnp.exp2(old_top - top)
                    total = total + out_ref[1:2, cols] * shrink
                    mixed = mixed + out_ref[2:3, cols] * shrink
                out_ref[0:1, cols] = top
                out_ref[1:2, cols] = total
                out_ref[2:3, cols] = mixed

    if first:
        live = count_ref[0, 0]
        state_ref[0] = parent_ref[0, 0]
        for i in range(1, SEGMENTS):
            state_ref[i] = 0
        state_ref[SEGMENTS] = live
        add_segment(packet_ref, own_bias(live, STATS_HEADS), True)
    else:
        for i in range(SEGMENTS + 1):
            state_ref[i] = old_ref[i]
        out_ref[...] = in_ref[...]
        for packet_ref, distance in zip(packet_refs, distances):

            @pl.when(state_ref[0] == me - distance)
            def _():
                labels = packet_ref[PACKET_ROWS:, :].astype(F32)
                parent = jnp.max(labels[: LABEL_ROWS // 2, :]).astype(jnp.int32)
                live = jnp.max(labels[LABEL_ROWS // 2 :, :]).astype(jnp.int32)
                state_ref[0] = parent
                state_ref[distance] = live
                add_segment(packet_ref, key_bias(live), False)

    if last:
        live = state_ref[SEGMENTS]
        position = lax.broadcasted_iota(jnp.int32, (1, Q_COLS), 1) & (SEG_LEN - 1)
        total = out_ref[1:2, :]
        row_delta = out_ref[2:3, :] / total
        lse = out_ref[0:1, :] + jnp.log2(total)
        out_ref[0:1, :] = jnp.where(position < live, lse, DEAD_LSE)
        out_ref[1:2, :] = row_delta


def grads_kernel(distances, first, last, *refs):
    state_ref, q_ref, qt_ref, g_ref, gt_ref, stats_ref = refs[:6]
    count = len(distances)
    packet_refs = refs[6 : 6 + count]
    rest = refs[6 + count :]
    if first:
        acc_ref, *out_refs = rest
    else:
        in_ref, acc_ref, *out_refs = rest

    def add_segment(packet_ref, out_ref, bias, source_ref):
        for group in range(KV_HEADS):
            k, v = key_value(packet_ref, group)
            cols = group_cols(group)
            scores = dot_nn(k, qt_ref[:, cols]) * SCALE_LOG2 + bias
            probs = jnp.exp2(scores - stats_ref[0:1, cols])
            grad_probs = dot_nn(v, gt_ref[:, cols])
            grad_scores = (probs * (grad_probs - stats_ref[1:2, cols])).astype(BF16)
            dv = dot_nn(probs.astype(BF16), g_ref[cols, :])
            dk = dot_nn(grad_scores, q_ref[cols, :]) * SCALE
            dq = dot_nn(k.T, grad_scores)
            if source_ref is not None:
                dq = dq + source_ref[:, cols]
            if last:
                for head in range(GROUP):
                    part = slice(head * HEAD, (head + 1) * HEAD)
                    at = (group * GROUP + head) * HEAD
                    acc_ref[:, at : at + HEAD] = (dq[:, part] * SCALE).T.astype(BF16)
            else:
                acc_ref[:, cols] = dq
            out_ref[block_rows(group, 0), :] = dk.astype(out_ref.dtype)
            out_ref[block_rows(group, 1), :] = dv.astype(out_ref.dtype)

    if last:
        add_segment(
            packet_refs[0], out_refs[0], own_bias(state_ref[SEGMENTS], GROUP), in_ref
        )
        return
    source_ref = None if first else in_ref
    for packet_ref, out_ref, distance in zip(packet_refs, out_refs, distances):
        live = state_ref[distance]

        @pl.when(live > 0)
        def _():
            add_segment(packet_ref, out_ref, key_bias(live), source_ref)

        @pl.when(live == 0)
        def _():
            out_ref[...] = jnp.zeros_like(out_ref)
            if source_ref is None:
                acc_ref[...] = jnp.zeros_like(acc_ref)
            elif source_ref is not acc_ref:
                acc_ref[...] = source_ref[...]

        source_ref = acc_ref


SMEM_SPEC = pl.BlockSpec(memory_space=pltpu.SMEM)
VMEM_SPEC = pl.BlockSpec(memory_space=pltpu.VMEM)
STATS_SHAPE = jax.ShapeDtypeStruct((8, Q_COLS), F32)
STATE_SHAPE = jax.ShapeDtypeStruct((STATE,), jnp.int32)
BLOCK_FLOPS = 2 * SEG_LEN * SEG_LEN * HEAD * KV_HEADS * GROUP


def on_core(kernel, name, out_shape, operands, scalars=0, out_specs=None, flops=0, aliases=None):
    many = isinstance(out_shape, list)
    if out_specs is None:
        out_specs = [VMEM_SPEC] * len(out_shape) if many else VMEM_SPEC
    moved = sum(o.size * o.dtype.itemsize for o in operands)
    return pl.pallas_call(
        kernel,
        out_shape=out_shape,
        in_specs=[SMEM_SPEC] * scalars + [VMEM_SPEC] * (len(operands) - scalars),
        out_specs=out_specs,
        name=name,
        input_output_aliases=aliases or {},
        cost_estimate=pl.CostEstimate(flops=flops, bytes_accessed=moved, transcendentals=0),
        compiler_params=pltpu.CompilerParams(vmem_limit_bytes=KERNEL_VMEM),
    )(*operands)


def prepared(array_q, array_g):
    shapes = [(KV_HEADS * GROUP * SEG_LEN, HEAD), (HEAD, KV_HEADS * GROUP * SEG_LEN)] * 2
    return on_core(
        prep_kernel,
        "prep",
        [jax.ShapeDtypeStruct(shape, BF16) for shape in shapes],
        [array_q, array_g],
    )


def add_stats(heads, packets, distances, state, stats, last=False):
    _, qt, _, gt = heads
    first = stats is None
    scalars = list(state) if first else [state]
    operands = [*scalars, qt, gt, *packets]
    if not first:
        operands.append(stats)
    stats, state = on_core(
        functools.partial(stats_kernel, tuple(distances), first, last),
        "stats",
        [STATS_SHAPE, STATE_SHAPE],
        operands,
        scalars=len(scalars),
        out_specs=[VMEM_SPEC, SMEM_SPEC],
        flops=4 * BLOCK_FLOPS * len(packets),
    )
    return state, stats


def add_grads(heads, state, stats, packets, distances, acc, out_dtype, last=False):
    first = acc is None
    operands = [state, *heads, stats, *packets]
    aliases = {}
    if not first:
        if not last:
            aliases = {len(operands): 0}
        operands.append(acc)
    if last:
        out_shapes = [jax.ShapeDtypeStruct((SEG_LEN, Q_COLS), BF16)]
    else:
        out_shapes = [jax.ShapeDtypeStruct((HEAD, Q_COLS), F32)]
    out_shapes += [jax.ShapeDtypeStruct((PACKET_ROWS, HEAD), out_dtype)] * len(packets)
    acc, *parts = on_core(
        functools.partial(grads_kernel, tuple(distances), first, last),
        "grads",
        out_shapes,
        operands,
        scalars=1,
        flops=10 * BLOCK_FLOPS * len(packets),
        aliases=aliases,
    )
    return acc, parts


def shift_seq(array, k):
    return lax.ppermute(array, "seq", [(i, (i + k) % SEGMENTS) for i in range(SEGMENTS)])


def swap_cores(array):
    return lax.ppermute(array, "dp", [(i, i ^ 1) for i in range(X * Y * CORES)])


def dp_index(y, x, core):
    return (y % Y * X + x % X) * CORES + core


def shift_xy(array, along_x, along_y):
    pairs = [
        (dp_index(y, x, c), dp_index(y + along_y, x + along_x, c))
        for y in range(Y)
        for x in range(X)
        for c in range(CORES)
    ]
    return lax.ppermute(array, "dp", pairs)


def pack_kernel(parent_ref, count_ref, k_ref, v_ref, out_ref, sems):
    copies = []
    for head in range(KV_HEADS):
        for side, ref in enumerate((k_ref, v_ref)):
            copies.append(
                pltpu.make_async_copy(
                    ref.at[:, pl.ds(head * HEAD, HEAD)],
                    out_ref.at[pl.ds((2 * head + side) * SEG_LEN, SEG_LEN), :],
                    sems.at[2 * head + side],
                )
            )
    for copy in copies:
        copy.start()
    row = lax.broadcasted_iota(jnp.int32, (LABEL_ROWS, HEAD), 0)
    labels = jnp.where(row < LABEL_ROWS // 2, parent_ref[0, 0], count_ref[0, 0])
    out_ref[PACKET_ROWS:, :] = labels.astype(F32).astype(BF16)
    for copy in copies:
        copy.wait()


def ring_packet(keys, values, parents, counts):
    return pl.pallas_call(
        pack_kernel,
        out_shape=jax.ShapeDtypeStruct((PACKET_ROWS + LABEL_ROWS, HEAD), BF16),
        in_specs=[SMEM_SPEC, SMEM_SPEC] + [pl.BlockSpec(memory_space=pltpu.HBM)] * 2,
        out_specs=VMEM_SPEC,
        scratch_shapes=[pltpu.SemaphoreType.DMA((2 * KV_HEADS,))],
        name="pack",
        compiler_params=pltpu.CompilerParams(vmem_limit_bytes=KERNEL_VMEM),
    )(parents, counts, keys, values)


def finish_kernel(mine_ref, down_ref, up_ref, key_ref, value_ref, near_ref):
    for head in range(KV_HEADS):
        cols = slice(head * HEAD, (head + 1) * HEAD)
        for side, ref in enumerate((key_ref, value_ref)):
            rows = block_rows(head, side)
            total = mine_ref[rows, :] + (
                down_ref[rows, :].astype(F32) + up_ref[rows, :].astype(F32)
            )
            ref[:, cols] = total.astype(BF16)
            if side == 0:
                near_ref[:, cols] = total.astype(BF16)


def finish(mine, down, up):
    return on_core(
        finish_kernel,
        "finish",
        [jax.ShapeDtypeStruct((SEG_LEN, KV_COLS), BF16)] * 3,
        [mine, down, up],
    )


def taken(array, index, axis):
    return lax.dynamic_index_in_dim(array, index, axis, keepdims=False)


def places():
    dp = lax.axis_index("dp")
    core = lax.rem(dp, CORES)
    x = lax.rem(lax.div(dp, CORES), X)
    y = lax.div(dp, CORES * X)
    return y, x, core


def deal_kernel(hidden_ref, *out_refs):
    x = places()[1]
    for k, out_ref in enumerate(out_refs):
        to = lax.rem(x + k, X)
        for y in range(Y):
            first = pl.multiple_of((y * X + to) * SHARE, SHARE)
            out_ref[:, y * SHARE : (y + 1) * SHARE] = hidden_ref[:, pl.ds(first, SHARE)]


def hidden_shares(hidden):
    return on_core(
        deal_kernel, "deal", [jax.ShapeDtypeStruct((SEG_LEN, Y * SHARE), BF16)] * X, [hidden]
    )


def turn_kernel(*refs):
    part_refs, out_refs = refs[:X], refs[X:]
    here, _, core = places()
    for side, out_ref in enumerate(out_refs):
        for k in range(Y):
            of = lax.rem(here + k, Y) * CORES + lax.rem(core + side, CORES)
            first = pl.multiple_of(of * HEAD, HEAD)
            for i, ref in enumerate(part_refs):
                out_ref[k * HEAD : (k + 1) * HEAD, i * SEG_LEN : (i + 1) * SEG_LEN] = ref[
                    :, pl.ds(first, HEAD)
                ].T


def turned(parts):
    return on_core(
        turn_kernel,
        "turn",
        [jax.ShapeDtypeStruct((Y * HEAD, X * SEG_LEN), BF16)] * CORES,
        list(parts),
    )


def given_kernel(hidden_ref, *refs):
    token_refs, (out_ref,) = refs[:X], refs[X:]
    tokens = jnp.concatenate([ref[...] for ref in token_refs], axis=0)
    out_ref[...] = dot_nn(hidden_ref[...], tokens).astype(BF16)


def kept_kernel(hidden_ref, *refs):
    token_refs, got_ref, own_ref, out_refs = refs[:X], refs[X], refs[X + 1], refs[X + 2 :]
    tokens = jnp.concatenate([ref[...] for ref in token_refs], axis=0)
    total = dot_nn(hidden_ref[...], tokens) + got_ref[...].astype(F32)
    own_ref[...] = total[:HEAD]
    for k, ref in enumerate(out_refs):
        ref[...] = total[(k + 1) * HEAD : (k + 2) * HEAD].astype(BF16)


def project_grad(hidden_own, hidden_other, key_grad):
    tokens = [key_grad] + [shift_xy(key_grad, k, 0) for k in range(1, X)]
    flops = 2 * X * SEG_LEN * Y * HEAD * KV_COLS
    given = on_core(
        given_kernel,
        "given",
        jax.ShapeDtypeStruct((Y * HEAD, KV_COLS), BF16),
        [hidden_other, *tokens],
        flops=flops,
    )
    own, *low = on_core(
        kept_kernel,
        "kept",
        [jax.ShapeDtypeStruct((HEAD, KV_COLS), F32)]
        + [jax.ShapeDtypeStruct((HEAD, KV_COLS), BF16)] * (Y - 1),
        [hidden_own, *tokens, swap_cores(given)],
        flops=flops,
    )
    total = own
    for k in range(1, Y):
        total = total + shift_xy(low[k - 1], 0, k).astype(F32)
    rows = lax.all_to_all(total.astype(BF16), "seq", 0, 0, tiled=True)
    return jnp.sum(rows.reshape(SEGMENTS, -1, KV_COLS).astype(F32), axis=0)


def all_grads(hidden, queries, keys, values, out_grad, parents, counts):
    barrier = lax.optimization_barrier
    own = ring_packet(
        keys.reshape(SEG_LEN, KV_COLS), values.reshape(SEG_LEN, KV_COLS), parents, counts
    )
    up, down = own, own
    below, above = {}, {}
    state, stats = (parents, counts), None
    hidden_parts = None
    for step in range(1, 5):
        if step == 2:
            heads = prepared(queries.reshape(SEG_LEN, Q_COLS), out_grad.reshape(SEG_LEN, Q_COLS))
            shares = hidden_shares(hidden)
            up, down, *rest = barrier((up, down, *heads, *shares))
            heads, shares = rest[:4], rest[4:]
            hidden_parts = [
                shift_xy(share, k, 0) if k else share for k, share in enumerate(shares)
            ]
        if step == 3:
            state, stats = add_stats(heads, [own], [0], state, None)
            up, down, state, stats, hidden_parts[1], hidden_parts[3] = barrier(
                (up, down, state, stats, hidden_parts[1], hidden_parts[3])
            )
        if step == 4:
            for done in (1, 2):
                state, stats = add_stats(heads, [below[done]], [done], state, stats)
            down, state, stats, hidden_parts[2] = barrier(
                (down, state, stats, hidden_parts[2])
            )
        down = shift_seq(down, -1)
        above[step] = down
        if step < 4:
            up = shift_seq(up, 1)
            below[step] = up
    state, stats = add_stats(heads, [below[3]], [3], state, stats)
    state, stats = add_stats(
        heads, [above[s] for s in (4, 3, 2, 1)], [4, 5, 6, 7], state, stats, last=True
    )

    acc, [far] = add_grads(heads, state, stats, [above[4]], [4], None, BF16)
    down = shift_seq(far, -1)
    up = None
    for step in range(3, 0, -1):
        acc, [low, high] = add_grads(
            heads, state, stats, [below[step], above[step]], [step, 8 - step], acc, F32
        )
        down = shift_seq((low + down.astype(F32)).astype(BF16), -1)
        up = shift_seq((high if up is None else high + up.astype(F32)).astype(BF16), 1)
        if step == 1:
            acc, *hidden_parts = barrier((acc, *turned(hidden_parts)))
    dq, [mine] = add_grads(heads, state, stats, [own], [0], acc, F32, last=True)
    key_grad, value_grad, near = finish(mine, down, up)
    return dq, key_grad, value_grad, project_grad(*hidden_parts, near)


def local(hidden_in, queries, keys, values, out_grad, parents, counts):
    dq, key_grad, value_grad, weight_grad = all_grads(
        hidden_in.reshape(SEG_LEN, -1), queries, keys, values, out_grad, parents, counts
    )
    return (
        dq.reshape(1, 1, SEG_LEN, Q_COLS),
        key_grad.reshape(1, 1, SEG_LEN, KV_COLS),
        value_grad.reshape(1, 1, SEG_LEN, KV_COLS),
        weight_grad,
    )


def solution(mesh):
    wide = P("dp", "seq", None, None)
    return jax.shard_map(
        local,
        mesh=mesh,
        in_specs=(wide, wide, wide, wide, wide, P("dp", "seq"), P("dp", "seq")),
        out_specs=(wide, wide, wide, P(("dp", "seq"), None)),
        check_vma=False,
    )
```

```python
import functools
import math

import jax
import jax.numpy as jnp
from jax import lax
from jax.experimental import pallas as pl
from jax.experimental.pallas import tpu as pltpu
from jax.sharding import PartitionSpec as P

SEGMENTS = 8
SEG_LEN = 128
KV_HEADS = 4
GROUP = 8
HEAD = 128
KV_COLS = KV_HEADS * HEAD
Q_COLS = KV_HEADS * GROUP * HEAD
GROUP_COLS = GROUP * HEAD
STATS_HEADS = 2
KERNEL_VMEM = 16 << 20
SCALE = 1.0 / math.sqrt(HEAD)
SCALE_LOG2 = SCALE * math.log2(math.e)
NEG_FILL = -1e30
DEAD_LSE = 1e30
LABEL_ROWS = 16
PACKET_ROWS = 2 * KV_HEADS * SEG_LEN
STATE = 16
BF16 = jnp.bfloat16
F32 = jnp.float32

X, Y, CORES = 4, 4, 2
SHARE = CORES * HEAD


def dot_nt(a, b):
    return lax.dot_general(a, b, (((1,), (1,)), ((), ())), preferred_element_type=F32)


def dot_nn(a, b):
    return lax.dot_general(a, b, (((1,), (0,)), ((), ())), preferred_element_type=F32)


def dot_tn(a, b):
    return lax.dot_general(a, b, (((0,), (0,)), ((), ())), preferred_element_type=F32)


def key_bias(live):
    position = lax.broadcasted_iota(jnp.int32, (SEG_LEN, 1), 0)
    return jnp.where(position < live, 0.0, NEG_FILL).astype(F32)


def own_bias(live, heads):
    key_at = lax.broadcasted_iota(jnp.int32, (SEG_LEN, SEG_LEN), 0)
    query_at = lax.broadcasted_iota(jnp.int32, (SEG_LEN, SEG_LEN), 1)
    tile = jnp.where((key_at <= query_at) & (key_at < live), 0.0, NEG_FILL).astype(F32)
    return jnp.concatenate([tile] * heads, axis=1)


def block_rows(group, side):
    first = (2 * group + side) * SEG_LEN
    return slice(first, first + SEG_LEN)


def key_value(ref, group):
    return ref[block_rows(group, 0), :], ref[block_rows(group, 1), :]


def group_cols(group):
    return slice(group * GROUP_COLS, (group + 1) * GROUP_COLS)


def prep_kernel(q_ref, g_ref, *out_refs):
    for ref, (rows_ref, turned_ref) in ((q_ref, out_refs[:2]), (g_ref, out_refs[2:])):
        for head in range(KV_HEADS * GROUP):
            part = slice(head * HEAD, (head + 1) * HEAD)
            block = ref[:, part]
            rows_ref[part, :] = block
            turned_ref[:, part] = block.T


def scalar_of(rows):
    return jnp.max(rows.astype(F32)).astype(jnp.int32)


def state_value(ref, index):
    return scalar_of(ref[pl.ds(index, 1), :])


def set_state(ref, index, value):
    ref[pl.ds(index, 1), :] = jnp.full((1, HEAD), value, jnp.int32).astype(F32)


def stats_kernel(steps, first, last, *refs):
    if first:
        parent_ref, count_ref, q_ref, g_ref, packet_ref, out_ref, state_ref = refs
    else:
        q_ref, g_ref = refs[:2]
        packet_refs = refs[2:-4]
        in_ref, old_ref, out_ref, state_ref = refs[-4:]
    me = lax.axis_index("seq")

    def add_segment(packet_ref, bias, start):
        width = STATS_HEADS * HEAD
        for group in range(KV_HEADS):
            k, v = key_value(packet_ref, group)
            for chunk in range(GROUP_COLS // width):
                at = group * GROUP_COLS + chunk * width
                cols = slice(at, at + width)
                scores = dot_nn(k, q_ref[:, cols]) * SCALE_LOG2 + bias
                grad_probs = dot_nn(v, g_ref[:, cols])
                top = jnp.max(scores, axis=0, keepdims=True)
                if not start:
                    old_top = out_ref[0:1, cols]
                    top = jnp.maximum(top, old_top)
                weights = jnp.exp2(scores - top)
                total = jnp.sum(weights, axis=0, keepdims=True)
                mixed = jnp.sum(weights * grad_probs, axis=0, keepdims=True)
                if not start:
                    shrink = jnp.exp2(old_top - top)
                    total = total + out_ref[1:2, cols] * shrink
                    mixed = mixed + out_ref[2:3, cols] * shrink
                out_ref[0:1, cols] = top
                out_ref[1:2, cols] = total
                out_ref[2:3, cols] = mixed

    if first:
        live = count_ref[0, 0]
        state_ref[...] = jnp.zeros_like(state_ref)
        set_state(state_ref, 0, parent_ref[0, 0])
        set_state(state_ref, SEGMENTS, live)
        add_segment(packet_ref, own_bias(live, STATS_HEADS), True)
    else:
        state_ref[...] = old_ref[...]
        out_ref[...] = in_ref[...]
        if last:
            (packet_ref,), ((distance, _),) = packet_refs, steps
            live_there = state_value(old_ref, distance)

            @pl.when(live_there > 0)
            def _():
                add_segment(packet_ref, key_bias(live_there), False)

        else:
            current = state_value(old_ref, 0)
            for packet_ref, (distance, looked_up) in zip(packet_refs, steps):
                top_row = packet_ref.shape[0] - LABEL_ROWS
                hit = current == me - distance
                parent = scalar_of(packet_ref[top_row:, :][: LABEL_ROWS // 2])
                current = jnp.where(hit, parent, current)

                @pl.when(hit)
                def _():
                    live = scalar_of(packet_ref[top_row:, :][LABEL_ROWS // 2 :])
                    set_state(state_ref, distance, live)
                    if not looked_up:
                        add_segment(packet_ref, key_bias(live), False)

            set_state(state_ref, 0, current)

    if last:
        live = state_value(old_ref, SEGMENTS)
        position = lax.broadcasted_iota(jnp.int32, (1, Q_COLS), 1) & (SEG_LEN - 1)
        total = out_ref[1:2, :]
        row_delta = out_ref[2:3, :] / total
        lse = out_ref[0:1, :] + jnp.log2(total)
        out_ref[0:1, :] = jnp.where(position < live, lse, DEAD_LSE)
        out_ref[1:2, :] = row_delta


def grads_kernel(distances, first, last, *refs):
    state_ref, q_ref, qt_ref, g_ref, gt_ref, stats_ref = refs[:6]
    count = len(distances)
    packet_refs = refs[6 : 6 + count]
    rest = refs[6 + count :]
    if first:
        acc_ref, *out_refs = rest
    else:
        in_ref, acc_ref, *out_refs = rest

    def add_segment(packet_ref, dk_ref, dv_ref, bias, source_ref):
        for group in range(KV_HEADS):
            k, v = key_value(packet_ref, group)
            cols = group_cols(group)
            rows = slice(group * SEG_LEN, (group + 1) * SEG_LEN)
            scores = dot_nn(k, qt_ref[:, cols]) * SCALE_LOG2 + bias
            probs = jnp.exp2(scores - stats_ref[0:1, cols])
            grad_probs = dot_nn(v, gt_ref[:, cols])
            grad_scores = (probs * (grad_probs - stats_ref[1:2, cols])).astype(BF16)
            dv = dot_nn(probs.astype(BF16), g_ref[cols, :])
            dk = dot_nn(grad_scores, q_ref[cols, :]) * SCALE
            dq = dot_nn(k.T, grad_scores)
            if source_ref is not None:
                dq = dq + source_ref[:, cols]
            if last:
                for head in range(GROUP):
                    part = slice(head * HEAD, (head + 1) * HEAD)
                    at = (group * GROUP + head) * HEAD
                    acc_ref[:, at : at + HEAD] = (dq[:, part] * SCALE).T.astype(BF16)
            else:
                acc_ref[:, cols] = dq
            dk_ref[rows, :] = dk.astype(dk_ref.dtype)
            dv_ref[rows, :] = dv.astype(dv_ref.dtype)

    if last:
        bias = own_bias(state_value(state_ref, SEGMENTS), GROUP)
        add_segment(packet_refs[0], *out_refs, bias, in_ref)
        return
    source_ref = None if first else in_ref
    for i, (packet_ref, distance) in enumerate(zip(packet_refs, distances)):
        dk_ref, dv_ref = out_refs[2 * i : 2 * i + 2]
        live = state_value(state_ref, distance)

        @pl.when(live > 0)
        def _():
            add_segment(packet_ref, dk_ref, dv_ref, key_bias(live), source_ref)

        @pl.when(live == 0)
        def _():
            dk_ref[...] = jnp.zeros_like(dk_ref)
            dv_ref[...] = jnp.zeros_like(dv_ref)
            if source_ref is None:
                acc_ref[...] = jnp.zeros_like(acc_ref)
            elif source_ref is not acc_ref:
                acc_ref[...] = source_ref[...]

        source_ref = acc_ref


SMEM_SPEC = pl.BlockSpec(memory_space=pltpu.SMEM)
VMEM_SPEC = pl.BlockSpec(memory_space=pltpu.VMEM)
STATS_SHAPE = jax.ShapeDtypeStruct((8, Q_COLS), F32)
STATE_SHAPE = jax.ShapeDtypeStruct((STATE, HEAD), F32)
BLOCK_FLOPS = 2 * SEG_LEN * SEG_LEN * HEAD * KV_HEADS * GROUP


def on_core(kernel, name, out_shape, operands, scalars=0, out_specs=None, flops=0, aliases=None):
    many = isinstance(out_shape, list)
    if out_specs is None:
        out_specs = [VMEM_SPEC] * len(out_shape) if many else VMEM_SPEC
    moved = sum(o.size * o.dtype.itemsize for o in operands)
    return pl.pallas_call(
        kernel,
        out_shape=out_shape,
        in_specs=[SMEM_SPEC] * scalars + [VMEM_SPEC] * (len(operands) - scalars),
        out_specs=out_specs,
        name=name,
        input_output_aliases=aliases or {},
        cost_estimate=pl.CostEstimate(flops=flops, bytes_accessed=moved, transcendentals=0),
        compiler_params=pltpu.CompilerParams(vmem_limit_bytes=KERNEL_VMEM),
    )(*operands)


def prepared(array_q, array_g):
    shapes = [(KV_HEADS * GROUP * SEG_LEN, HEAD), (HEAD, KV_HEADS * GROUP * SEG_LEN)] * 2
    return on_core(
        prep_kernel,
        "prep",
        [jax.ShapeDtypeStruct(shape, BF16) for shape in shapes],
        [array_q, array_g],
    )


def add_stats(heads, packets, steps, state, stats, last=False):
    _, qt, _, gt = heads
    first = stats is None
    if first:
        operands = [*state, qt, gt, *packets]
    else:
        operands = [qt, gt, *packets, stats, state]
    stats, state = on_core(
        functools.partial(stats_kernel, tuple(steps), first, last),
        "stats",
        [STATS_SHAPE, STATE_SHAPE],
        operands,
        scalars=len(state) if first else 0,
        flops=4 * BLOCK_FLOPS * len(packets),
    )
    return state, stats


def add_grads(heads, state, stats, packets, distances, acc, out_dtype, last=False):
    first = acc is None
    operands = [state, *heads, stats, *packets]
    aliases = {}
    if not first:
        if not last:
            aliases = {len(operands): 0}
        operands.append(acc)
    if last:
        out_shapes = [jax.ShapeDtypeStruct((SEG_LEN, Q_COLS), BF16)]
    else:
        out_shapes = [jax.ShapeDtypeStruct((HEAD, Q_COLS), F32)]
    out_shapes += [jax.ShapeDtypeStruct((KV_COLS, HEAD), out_dtype)] * (2 * len(packets))
    return on_core(
        functools.partial(grads_kernel, tuple(distances), first, last),
        "grads",
        out_shapes,
        operands,
        flops=10 * BLOCK_FLOPS * len(packets),
        aliases=aliases,
    )


def shift_seq(array, k):
    return lax.ppermute(array, "seq", [(i, (i + k) % SEGMENTS) for i in range(SEGMENTS)])


def swap_cores(array):
    return lax.ppermute(array, "dp", [(i, i ^ 1) for i in range(X * Y * CORES)])


def dp_index(y, x, core):
    return (y % Y * X + x % X) * CORES + core


def shift_xy(array, along_x, along_y):
    pairs = [
        (dp_index(y, x, c), dp_index(y + along_y, x + along_x, c))
        for y in range(Y)
        for x in range(X)
        for c in range(CORES)
    ]
    return lax.ppermute(array, "dp", pairs)


def pack_kernel(parent_ref, count_ref, k_ref, v_ref, out_ref, sems):
    copies = []
    for head in range(KV_HEADS):
        for side, ref in enumerate((k_ref, v_ref)):
            copies.append(
                pltpu.make_async_copy(
                    ref.at[:, pl.ds(head * HEAD, HEAD)],
                    out_ref.at[pl.ds((2 * head + side) * SEG_LEN, SEG_LEN), :],
                    sems.at[2 * head + side],
                )
            )
    for copy in copies:
        copy.start()
    row = lax.broadcasted_iota(jnp.int32, (LABEL_ROWS, HEAD), 0)
    labels = jnp.where(row < LABEL_ROWS // 2, parent_ref[0, 0], count_ref[0, 0])
    out_ref[PACKET_ROWS:, :] = labels.astype(F32).astype(BF16)
    for copy in copies:
        copy.wait()


def ring_packet(keys, values, parents, counts):
    return pl.pallas_call(
        pack_kernel,
        out_shape=jax.ShapeDtypeStruct((PACKET_ROWS + LABEL_ROWS, HEAD), BF16),
        in_specs=[SMEM_SPEC, SMEM_SPEC] + [pl.BlockSpec(memory_space=pltpu.HBM)] * 2,
        out_specs=VMEM_SPEC,
        scratch_shapes=[pltpu.SemaphoreType.DMA((2 * KV_HEADS,))],
        name="pack",
        compiler_params=pltpu.CompilerParams(vmem_limit_bytes=KERNEL_VMEM),
    )(parents, counts, keys, values)


def finish_kernel(mine_ref, down_ref, up_ref, *out_refs):
    for head in range(KV_HEADS):
        rows = slice(head * SEG_LEN, (head + 1) * SEG_LEN)
        total = mine_ref[rows, :] + (
            down_ref[rows, :].astype(F32) + up_ref[rows, :].astype(F32)
        )
        for ref in out_refs:
            ref[:, head * HEAD : (head + 1) * HEAD] = total.astype(BF16)


def finish(mine, down, up, copies):
    return on_core(
        finish_kernel,
        "finish",
        [jax.ShapeDtypeStruct((SEG_LEN, KV_COLS), BF16)] * copies,
        [mine, down, up],
    )


def taken(array, index, axis):
    return lax.dynamic_index_in_dim(array, index, axis, keepdims=False)


def places():
    dp = lax.axis_index("dp")
    core = lax.rem(dp, CORES)
    x = lax.rem(lax.div(dp, CORES), X)
    y = lax.div(dp, CORES * X)
    return y, x, core


def deal_kernel(hidden_ref, *out_refs):
    x = places()[1]
    for k, out_ref in enumerate(out_refs):
        to = lax.rem(x + k, X)
        for y in range(Y):
            first = pl.multiple_of((y * X + to) * SHARE, SHARE)
            out_ref[:, y * SHARE : (y + 1) * SHARE] = hidden_ref[:, pl.ds(first, SHARE)]


def hidden_shares(hidden):
    return on_core(
        deal_kernel, "deal", [jax.ShapeDtypeStruct((SEG_LEN, Y * SHARE), BF16)] * X, [hidden]
    )


def turn_kernel(*refs):
    part_refs, out_refs = refs[:X], refs[X:]
    here, _, core = places()
    for side, out_ref in enumerate(out_refs):
        for k in range(Y):
            of = lax.rem(here + k, Y) * CORES + lax.rem(core + side, CORES)
            first = pl.multiple_of(of * HEAD, HEAD)
            for i, ref in enumerate(part_refs):
                out_ref[k * HEAD : (k + 1) * HEAD, i * SEG_LEN : (i + 1) * SEG_LEN] = ref[
                    :, pl.ds(first, HEAD)
                ].T


def turned(parts):
    return on_core(
        turn_kernel,
        "turn",
        [jax.ShapeDtypeStruct((Y * HEAD, X * SEG_LEN), BF16)] * CORES,
        list(parts),
    )


def given_kernel(hidden_ref, *refs):
    token_refs, (out_ref,) = refs[:X], refs[X:]
    tokens = jnp.concatenate([ref[...] for ref in token_refs], axis=0)
    out_ref[...] = dot_nn(hidden_ref[...], tokens).astype(BF16)


def kept_kernel(hidden_ref, *refs):
    token_refs, got_ref, own_ref, out_refs = refs[:X], refs[X], refs[X + 1], refs[X + 2 :]
    tokens = jnp.concatenate([ref[...] for ref in token_refs], axis=0)
    total = dot_nn(hidden_ref[...], tokens) + got_ref[...].astype(F32)
    own_ref[...] = total[:HEAD]
    for k, ref in enumerate(out_refs):
        ref[...] = total[(k + 1) * HEAD : (k + 2) * HEAD].astype(BF16)


def all_grads(hidden, queries, keys, values, out_grad, parents, counts):
    barrier = lax.optimization_barrier
    own = ring_packet(
        keys.reshape(SEG_LEN, KV_COLS), values.reshape(SEG_LEN, KV_COLS), parents, counts
    )
    up, down = own, own
    below, above = {}, {}
    state, stats = (parents, counts), None
    for step in range(1, 5):
        if step == 2:
            heads = prepared(queries.reshape(SEG_LEN, Q_COLS), out_grad.reshape(SEG_LEN, Q_COLS))
            shares = hidden_shares(hidden)
            up, down, *rest = barrier((up, down, *heads, *shares))
            heads, shares = rest[:4], rest[4:]
            hidden_parts = [
                shift_xy(share, k, 0) if k else share for k, share in enumerate(shares)
            ]
            label = shift_seq(own[PACKET_ROWS:], 4)
        if step == 3:
            state, stats = add_stats(heads, [own], [], state, None)
            up, down, state, stats, hidden_parts[1], hidden_parts[3], label = barrier(
                (up, down, state, stats, hidden_parts[1], hidden_parts[3], label)
            )
        if step == 4:
            state, stats = add_stats(
                heads, [below[1], below[2]], [(1, False), (2, False)], state, stats
            )
            down, state, stats, hidden_parts[2] = barrier(
                (down, state, stats, hidden_parts[2])
            )
        down = shift_seq(down, -1)
        above[step] = down
        if step < 4:
            up = shift_seq(up, 1)
            below[step] = up
    state, stats = add_stats(
        heads,
        [below[3], label, above[3], above[2], above[1]],
        [(3, False), (4, True), (5, False), (6, False), (7, False)],
        state,
        stats,
    )
    state, stats = add_stats(heads, [above[4]], [(4, False)], state, stats, last=True)

    dvs = {}
    acc, dk, dvs[4] = add_grads(heads, state, stats, [above[4]], [4], None, BF16)
    down, up = shift_seq(dk, -1), None
    for step in range(3, 0, -1):
        acc, low, dvs[step], high, dvs[8 - step] = add_grads(
            heads, state, stats, [below[step], above[step]], [step, 8 - step], acc, F32
        )
        acc, down = barrier((acc, down))
        down = shift_seq((low + down.astype(F32)).astype(BF16), -1)
        up = shift_seq((high if up is None else high + up.astype(F32)).astype(BF16), 1)
        if step == 1:
            acc, *hidden_parts = barrier((acc, *turned(hidden_parts)))
    value_up = shift_seq(dvs[4], 1)
    dq, mine, dvs[0] = add_grads(heads, state, stats, [own], [0], acc, F32, last=True)
    key_grad, near = finish(mine, down, up, 2)
    near, value_up, dvs[3] = barrier((near, value_up, dvs[3]))

    def value_step(step, value_up, value_down):
        value_up = (dvs[8 - step] + value_up.astype(F32)).astype(BF16)
        if value_down is None:
            value_down = dvs[step].astype(BF16)
        else:
            value_down = (dvs[step] + value_down.astype(F32)).astype(BF16)
        return shift_seq(value_up, 1), shift_seq(value_down, -1)

    hidden_own, hidden_other = hidden_parts
    flops = 2 * X * SEG_LEN * Y * HEAD * KV_COLS
    tokens = [near] + [shift_xy(near, k, 0) for k in range(1, X)]
    value_up, value_down = value_step(3, value_up, None)
    *tokens, value_up, value_down = barrier((*tokens, value_up, value_down))
    given = on_core(
        given_kernel,
        "given",
        jax.ShapeDtypeStruct((Y * HEAD, KV_COLS), BF16),
        [hidden_other, *tokens],
        flops=flops,
    )
    value_up, value_down = value_step(2, value_up, value_down)
    kept, *low = on_core(
        kept_kernel,
        "kept",
        [jax.ShapeDtypeStruct((HEAD, KV_COLS), F32)]
        + [jax.ShapeDtypeStruct((HEAD, KV_COLS), BF16)] * (Y - 1),
        [hidden_own, *tokens, swap_cores(given)],
        flops=flops,
    )
    others = [shift_xy(low[k - 1], 0, k) for k in range(1, Y)]
    *others, value_up, value_down = barrier((*others, value_up, value_down))
    value_up, value_down = value_step(1, value_up, value_down)
    total = kept
    for other in others:
        total = total + other.astype(F32)
    rows = lax.all_to_all(total.astype(BF16), "seq", 0, 0, tiled=True)
    rows, value_up, value_down = barrier((rows, value_up, value_down))
    weight_grad = jnp.sum(rows.reshape(SEGMENTS, -1, KV_COLS).astype(F32), axis=0)
    value_grad = finish(dvs[0], value_down, value_up, 1)[0]
    return dq, key_grad, value_grad, weight_grad


def local(hidden_in, queries, keys, values, out_grad, parents, counts):
    dq, key_grad, value_grad, weight_grad = all_grads(
        hidden_in.reshape(SEG_LEN, -1), queries, keys, values, out_grad, parents, counts
    )
    return (
        dq.reshape(1, 1, SEG_LEN, Q_COLS),
        key_grad.reshape(1, 1, SEG_LEN, KV_COLS),
        value_grad.reshape(1, 1, SEG_LEN, KV_COLS),
        weight_grad,
    )


def solution(mesh):
    wide = P("dp", "seq", None, None)
    return jax.shard_map(
        local,
        mesh=mesh,
        in_specs=(wide, wide, wide, wide, wide, P("dp", "seq"), P("dp", "seq")),
        out_specs=(wide, wide, wide, P(("dp", "seq"), None)),
        check_vma=False,
    )
```

```python
import functools
import math

import jax
import jax.numpy as jnp
from jax import lax
from jax.experimental import pallas as pl
from jax.experimental.pallas import tpu as pltpu
from jax.sharding import PartitionSpec as P

SEGMENTS = 8
SEG_LEN = 128
KV_HEADS = 4
GROUP = 8
HEAD = 128
KV_COLS = KV_HEADS * HEAD
Q_COLS = KV_HEADS * GROUP * HEAD
GROUP_COLS = GROUP * HEAD
STATS_HEADS = 2
KERNEL_VMEM = 16 << 20
SCALE = 1.0 / math.sqrt(HEAD)
SCALE_LOG2 = SCALE * math.log2(math.e)
NEG_FILL = -1e30
DEAD_LSE = 1e30
LABEL_ROWS = 16
PACKET_ROWS = 2 * KV_HEADS * SEG_LEN
STATE = 16
BF16 = jnp.bfloat16
F32 = jnp.float32

X, Y, CORES = 4, 4, 2
SHARE = CORES * HEAD


def dot_nt(a, b):
    return lax.dot_general(a, b, (((1,), (1,)), ((), ())), preferred_element_type=F32)


def dot_nn(a, b):
    return lax.dot_general(a, b, (((1,), (0,)), ((), ())), preferred_element_type=F32)


def dot_tn(a, b):
    return lax.dot_general(a, b, (((0,), (0,)), ((), ())), preferred_element_type=F32)


def key_bias(live):
    position = lax.broadcasted_iota(jnp.int32, (SEG_LEN, 1), 0)
    return jnp.where(position < live, 0.0, NEG_FILL).astype(F32)


def own_bias(live, heads):
    key_at = lax.broadcasted_iota(jnp.int32, (SEG_LEN, SEG_LEN), 0)
    query_at = lax.broadcasted_iota(jnp.int32, (SEG_LEN, SEG_LEN), 1)
    tile = jnp.where((key_at <= query_at) & (key_at < live), 0.0, NEG_FILL).astype(F32)
    return jnp.concatenate([tile] * heads, axis=1)


def block_rows(group):
    return slice(group * SEG_LEN, (group + 1) * SEG_LEN)


def key_value(refs, group):
    k_ref, v_ref = refs[0], refs[-1]
    first = KV_COLS if len(refs) == 1 else 0
    rows = block_rows(group)
    return k_ref[rows, :], v_ref[first + rows.start : first + rows.stop, :]


def group_cols(group):
    return slice(group * GROUP_COLS, (group + 1) * GROUP_COLS)


def prep_kernel(q_ref, g_ref, *out_refs):
    for ref, (rows_ref, turned_ref) in ((q_ref, out_refs[:2]), (g_ref, out_refs[2:])):
        for head in range(KV_HEADS * GROUP):
            part = slice(head * HEAD, (head + 1) * HEAD)
            block = ref[:, part]
            rows_ref[part, :] = block
            turned_ref[:, part] = block.T


def scalar_of(rows):
    return jnp.max(rows.astype(F32)).astype(jnp.int32)


def state_value(ref, index):
    return scalar_of(ref[pl.ds(index, 1), :])


def set_state(ref, index, value):
    ref[pl.ds(index, 1), :] = jnp.full((1, HEAD), value, jnp.int32).astype(F32)


def stats_kernel(steps, first, last, *refs):
    if first:
        parent_ref, count_ref, q_ref, g_ref, packet_ref, out_ref, state_ref = refs
    else:
        q_ref, g_ref = refs[:2]
        packet_refs = refs[2:-4]
        in_ref, old_ref, out_ref, state_ref = refs[-4:]
    me = lax.axis_index("seq")

    def add_segment(packet, bias, start):
        width = STATS_HEADS * HEAD
        for group in range(KV_HEADS):
            k, v = key_value(packet, group)
            for chunk in range(GROUP_COLS // width):
                at = group * GROUP_COLS + chunk * width
                cols = slice(at, at + width)
                scores = dot_nn(k, q_ref[:, cols]) * SCALE_LOG2 + bias
                grad_probs = dot_nn(v, g_ref[:, cols])
                top = jnp.max(scores, axis=0, keepdims=True)
                if not start:
                    old_top = out_ref[0:1, cols]
                    top = jnp.maximum(top, old_top)
                weights = jnp.exp2(scores - top)
                total = jnp.sum(weights, axis=0, keepdims=True)
                mixed = jnp.sum(weights * grad_probs, axis=0, keepdims=True)
                if not start:
                    shrink = jnp.exp2(old_top - top)
                    total = total + out_ref[1:2, cols] * shrink
                    mixed = mixed + out_ref[2:3, cols] * shrink
                out_ref[0:1, cols] = top
                out_ref[1:2, cols] = total
                out_ref[2:3, cols] = mixed

    if first:
        live = count_ref[0, 0]
        state_ref[...] = jnp.zeros_like(state_ref)
        set_state(state_ref, 0, parent_ref[0, 0])
        set_state(state_ref, SEGMENTS, live)
        add_segment([packet_ref], own_bias(live, STATS_HEADS), True)
    else:
        state_ref[...] = old_ref[...]
        out_ref[...] = in_ref[...]
        if last:
            ((distance, _),) = steps
            live_there = state_value(old_ref, distance)

            @pl.when(live_there > 0)
            def _():
                add_segment(packet_refs, key_bias(live_there), False)

        else:
            current = state_value(old_ref, 0)
            for packet_ref, (distance, looked_up) in zip(packet_refs, steps):
                top_row = packet_ref.shape[0] - LABEL_ROWS
                hit = current == me - distance
                parent = scalar_of(packet_ref[top_row:, :][: LABEL_ROWS // 2])
                current = jnp.where(hit, parent, current)

                @pl.when(hit)
                def _():
                    live = scalar_of(packet_ref[top_row:, :][LABEL_ROWS // 2 :])
                    set_state(state_ref, distance, live)
                    if not looked_up:
                        add_segment([packet_ref], key_bias(live), False)

            set_state(state_ref, 0, current)

    if last:
        live = state_value(old_ref, SEGMENTS)
        position = lax.broadcasted_iota(jnp.int32, (1, Q_COLS), 1) & (SEG_LEN - 1)
        total = out_ref[1:2, :]
        row_delta = out_ref[2:3, :] / total
        lse = out_ref[0:1, :] + jnp.log2(total)
        out_ref[0:1, :] = jnp.where(position < live, lse, DEAD_LSE)
        out_ref[1:2, :] = row_delta


def grads_kernel(distances, first, last, *refs):
    state_ref, q_ref, qt_ref, g_ref, gt_ref, stats_ref = refs[:6]
    if first:
        packets, rest = [refs[6:8]], refs[8:]
    else:
        count = len(distances)
        packets, rest = [[ref] for ref in refs[6 : 6 + count]], refs[6 + count :]
    if first:
        acc_ref, *out_refs = rest
    else:
        in_ref, acc_ref, *out_refs = rest

    def add_segment(packet, dk_ref, dv_ref, bias, source_ref):
        for group in range(KV_HEADS):
            k, v = key_value(packet, group)
            cols = group_cols(group)
            rows = block_rows(group)
            scores = dot_nn(k, qt_ref[:, cols]) * SCALE_LOG2 + bias
            probs = jnp.exp2(scores - stats_ref[0:1, cols])
            grad_probs = dot_nn(v, gt_ref[:, cols])
            grad_scores = (probs * (grad_probs - stats_ref[1:2, cols])).astype(BF16)
            dv = dot_nn(probs.astype(BF16), g_ref[cols, :])
            dk = dot_nn(grad_scores, q_ref[cols, :]) * SCALE
            dq = dot_nn(k.T, grad_scores)
            if source_ref is not None:
                dq = dq + source_ref[:, cols]
            if last:
                for head in range(GROUP):
                    part = slice(head * HEAD, (head + 1) * HEAD)
                    at = (group * GROUP + head) * HEAD
                    acc_ref[:, at : at + HEAD] = (dq[:, part] * SCALE).T.astype(BF16)
            else:
                acc_ref[:, cols] = dq
            dk_ref[rows, :] = dk.astype(dk_ref.dtype)
            dv_ref[rows, :] = dv.astype(dv_ref.dtype)

    if last:
        bias = own_bias(state_value(state_ref, SEGMENTS), GROUP)
        add_segment(packets[0], *out_refs, bias, in_ref)
        return
    source_ref = None if first else in_ref
    for i, (packet, distance) in enumerate(zip(packets, distances)):
        dk_ref, dv_ref = out_refs[2 * i : 2 * i + 2]
        live = state_value(state_ref, distance)

        @pl.when(live > 0)
        def _():
            add_segment(packet, dk_ref, dv_ref, key_bias(live), source_ref)

        @pl.when(live == 0)
        def _():
            dk_ref[...] = jnp.zeros_like(dk_ref)
            dv_ref[...] = jnp.zeros_like(dv_ref)
            if source_ref is None:
                acc_ref[...] = jnp.zeros_like(acc_ref)
            elif source_ref is not acc_ref:
                acc_ref[...] = source_ref[...]

        source_ref = acc_ref


SMEM_SPEC = pl.BlockSpec(memory_space=pltpu.SMEM)
VMEM_SPEC = pl.BlockSpec(memory_space=pltpu.VMEM)
STATS_SHAPE = jax.ShapeDtypeStruct((8, Q_COLS), F32)
STATE_SHAPE = jax.ShapeDtypeStruct((STATE, HEAD), F32)
BLOCK_FLOPS = 2 * SEG_LEN * SEG_LEN * HEAD * KV_HEADS * GROUP


def on_core(kernel, name, out_shape, operands, scalars=0, out_specs=None, flops=0, aliases=None):
    many = isinstance(out_shape, list)
    if out_specs is None:
        out_specs = [VMEM_SPEC] * len(out_shape) if many else VMEM_SPEC
    moved = sum(o.size * o.dtype.itemsize for o in operands)
    return pl.pallas_call(
        kernel,
        out_shape=out_shape,
        in_specs=[SMEM_SPEC] * scalars + [VMEM_SPEC] * (len(operands) - scalars),
        out_specs=out_specs,
        name=name,
        input_output_aliases=aliases or {},
        cost_estimate=pl.CostEstimate(flops=flops, bytes_accessed=moved, transcendentals=0),
        compiler_params=pltpu.CompilerParams(vmem_limit_bytes=KERNEL_VMEM),
    )(*operands)


def prepared(array_q, array_g):
    shapes = [(KV_HEADS * GROUP * SEG_LEN, HEAD), (HEAD, KV_HEADS * GROUP * SEG_LEN)] * 2
    return on_core(
        prep_kernel,
        "prep",
        [jax.ShapeDtypeStruct(shape, BF16) for shape in shapes],
        [array_q, array_g],
    )


def add_stats(heads, packets, steps, state, stats, last=False):
    _, qt, _, gt = heads
    first = stats is None
    if first:
        operands = [*state, qt, gt, *packets]
    else:
        operands = [qt, gt, *packets, stats, state]
    stats, state = on_core(
        functools.partial(stats_kernel, tuple(steps), first, last),
        "stats",
        [STATS_SHAPE, STATE_SHAPE],
        operands,
        scalars=len(state) if first else 0,
        flops=4 * BLOCK_FLOPS * len(packets),
    )
    return state, stats


def add_grads(heads, state, stats, packets, distances, acc, dtypes, last=False):
    first = acc is None
    operands = [state, *heads, stats, *packets]
    aliases = {}
    if not first:
        if not last:
            aliases = {len(operands): 0}
        operands.append(acc)
    if last:
        out_shapes = [jax.ShapeDtypeStruct((SEG_LEN, Q_COLS), BF16)]
    else:
        out_shapes = [jax.ShapeDtypeStruct((HEAD, Q_COLS), F32)]
    out_shapes += [jax.ShapeDtypeStruct((KV_COLS, HEAD), dtype) for dtype in dtypes]
    return on_core(
        functools.partial(grads_kernel, tuple(distances), first, last),
        "grads",
        out_shapes,
        operands,
        flops=10 * BLOCK_FLOPS * len(packets),
        aliases=aliases,
    )


def shift_seq(array, k):
    return lax.ppermute(array, "seq", [(i, (i + k) % SEGMENTS) for i in range(SEGMENTS)])


def swap_cores(array):
    return lax.ppermute(array, "dp", [(i, i ^ 1) for i in range(X * Y * CORES)])


def dp_index(y, x, core):
    return (y % Y * X + x % X) * CORES + core


def shift_xy(array, along_x, along_y):
    pairs = [
        (dp_index(y, x, c), dp_index(y + along_y, x + along_x, c))
        for y in range(Y)
        for x in range(X)
        for c in range(CORES)
    ]
    return lax.ppermute(array, "dp", pairs)


def pack_kernel(parent_ref, count_ref, k_ref, v_ref, out_ref, sems):
    copies = []
    for head in range(KV_HEADS):
        for side, ref in enumerate((k_ref, v_ref)):
            copies.append(
                pltpu.make_async_copy(
                    ref.at[:, pl.ds(head * HEAD, HEAD)],
                    out_ref.at[pl.ds((side * KV_HEADS + head) * SEG_LEN, SEG_LEN), :],
                    sems.at[2 * head + side],
                )
            )
    for copy in copies:
        copy.start()
    row = lax.broadcasted_iota(jnp.int32, (LABEL_ROWS, HEAD), 0)
    labels = jnp.where(row < LABEL_ROWS // 2, parent_ref[0, 0], count_ref[0, 0])
    out_ref[PACKET_ROWS:, :] = labels.astype(F32).astype(BF16)
    for copy in copies:
        copy.wait()


def ring_packet(keys, values, parents, counts):
    return pl.pallas_call(
        pack_kernel,
        out_shape=jax.ShapeDtypeStruct((PACKET_ROWS + LABEL_ROWS, HEAD), BF16),
        in_specs=[SMEM_SPEC, SMEM_SPEC] + [pl.BlockSpec(memory_space=pltpu.HBM)] * 2,
        out_specs=VMEM_SPEC,
        scratch_shapes=[pltpu.SemaphoreType.DMA((2 * KV_HEADS,))],
        name="pack",
        compiler_params=pltpu.CompilerParams(vmem_limit_bytes=KERNEL_VMEM),
    )(parents, counts, keys, values)


def finish_kernel(mine_ref, down_ref, up_ref, *out_refs):
    for head in range(KV_HEADS):
        rows = block_rows(head)
        total = mine_ref[rows, :] + (
            down_ref[rows, :].astype(F32) + up_ref[rows, :].astype(F32)
        )
        for ref in out_refs:
            ref[:, head * HEAD : (head + 1) * HEAD] = total.astype(BF16)


def finish(mine, down, up, copies):
    return on_core(
        finish_kernel,
        "finish",
        [jax.ShapeDtypeStruct((SEG_LEN, KV_COLS), BF16)] * copies,
        [mine, down, up],
    )


def taken(array, index, axis):
    return lax.dynamic_index_in_dim(array, index, axis, keepdims=False)


def places():
    dp = lax.axis_index("dp")
    core = lax.rem(dp, CORES)
    x = lax.rem(lax.div(dp, CORES), X)
    y = lax.div(dp, CORES * X)
    return y, x, core


def deal_kernel(hidden_ref, *out_refs):
    x = places()[1]
    for k, out_ref in enumerate(out_refs):
        to = lax.rem(x + k, X)
        for y in range(Y):
            first = pl.multiple_of((y * X + to) * SHARE, SHARE)
            out_ref[:, y * SHARE : (y + 1) * SHARE] = hidden_ref[:, pl.ds(first, SHARE)]


def hidden_shares(hidden):
    return on_core(
        deal_kernel, "deal", [jax.ShapeDtypeStruct((SEG_LEN, Y * SHARE), BF16)] * X, [hidden]
    )


def turn_kernel(*refs):
    part_refs, out_refs = refs[:X], refs[X:]
    here, _, core = places()
    for side, out_ref in enumerate(out_refs):
        for k in range(Y):
            of = lax.rem(here + k, Y) * CORES + lax.rem(core + side, CORES)
            first = pl.multiple_of(of * HEAD, HEAD)
            for i, ref in enumerate(part_refs):
                out_ref[k * HEAD : (k + 1) * HEAD, i * SEG_LEN : (i + 1) * SEG_LEN] = ref[
                    :, pl.ds(first, HEAD)
                ].T


def turned(parts):
    return on_core(
        turn_kernel,
        "turn",
        [jax.ShapeDtypeStruct((Y * HEAD, X * SEG_LEN), BF16)] * CORES,
        list(parts),
    )


def given_kernel(hidden_ref, *refs):
    token_refs, (out_ref,) = refs[:X], refs[X:]
    tokens = jnp.concatenate([ref[...] for ref in token_refs], axis=0)
    out_ref[...] = dot_nn(hidden_ref[...], tokens).astype(BF16)


def kept_kernel(hidden_ref, *refs):
    token_refs, got_ref, own_ref, out_refs = refs[:X], refs[X], refs[X + 1], refs[X + 2 :]
    tokens = jnp.concatenate([ref[...] for ref in token_refs], axis=0)
    total = dot_nn(hidden_ref[...], tokens) + got_ref[...].astype(F32)
    own_ref[...] = total[:HEAD]
    for k, ref in enumerate(out_refs):
        ref[...] = total[(k + 1) * HEAD : (k + 2) * HEAD].astype(BF16)


def all_grads(hidden, queries, keys, values, out_grad, parents, counts):
    barrier = lax.optimization_barrier
    own = ring_packet(
        keys.reshape(SEG_LEN, KV_COLS), values.reshape(SEG_LEN, KV_COLS), parents, counts
    )
    up, down = own, own
    below, above = {}, {}
    state, stats = (parents, counts), None
    for step in range(1, 5):
        if step == 2:
            heads = prepared(queries.reshape(SEG_LEN, Q_COLS), out_grad.reshape(SEG_LEN, Q_COLS))
            shares = hidden_shares(hidden)
            up, down, *rest = barrier((up, down, *heads, *shares))
            heads, shares = rest[:4], rest[4:]
            hidden_parts = [
                shift_xy(share, k, 0) if k else share for k, share in enumerate(shares)
            ]
            label = shift_seq(own[PACKET_ROWS:], 4)
        if step == 3:
            state, stats = add_stats(heads, [own], [], state, None)
            up, down, state, stats, hidden_parts[1], hidden_parts[3] = barrier(
                (up, down, state, stats, hidden_parts[1], hidden_parts[3])
            )
        if step == 4:
            state, stats = add_stats(
                heads, [below[1], below[2]], [(1, False), (2, False)], state, stats
            )
            up, down, state, stats = barrier((up, down, state, stats))
            farthest = [shift_seq(up[:KV_COLS], 1), shift_seq(down[KV_COLS:PACKET_ROWS], -1)]
            break
        down, up = shift_seq(down, -1), shift_seq(up, 1)
        above[step], below[step] = down, up
    state, stats = add_stats(
        heads,
        [below[3], label, above[3], above[2], above[1]],
        [(3, False), (4, True), (5, False), (6, False), (7, False)],
        state,
        stats,
    )
    stats, hidden_parts[2] = barrier((stats, hidden_parts[2]))
    state, stats = add_stats(heads, farthest, [(4, False)], state, stats, last=True)

    dvs = {}
    acc, dk, dvs[4] = add_grads(heads, state, stats, farthest, [4], None, [BF16] * 2)
    down, up = shift_seq(dk, -1), None
    for step in range(3, 0, -1):
        starts = step == 3
        acc, low, dvs[step], high, dvs[8 - step] = add_grads(
            heads,
            state,
            stats,
            [below[step], above[step]],
            [step, 8 - step],
            acc,
            [F32, BF16 if starts else F32, BF16 if starts else F32, F32],
        )
        acc, down = barrier((acc, down))
        down = shift_seq((low + down.astype(F32)).astype(BF16), -1)
        up = shift_seq(high if starts else (high + up.astype(F32)).astype(BF16), 1)
        if step == 1:
            acc, *hidden_parts = barrier((acc, *turned(hidden_parts)))
    value_up = shift_seq(dvs[4], 1)
    dq, mine, dvs[0] = add_grads(heads, state, stats, [own], [0], acc, [F32] * 2, last=True)
    key_grad, near = finish(mine, down, up, 2)
    near, dvs[3], dvs[5] = barrier((near, dvs[3], dvs[5]))

    def value_step(step, value_up, value_down):
        value_up = (dvs[8 - step] + value_up.astype(F32)).astype(BF16)
        if value_down is None:
            value_down = dvs[step]
        else:
            value_down = (dvs[step] + value_down.astype(F32)).astype(BF16)
        return shift_seq(value_up, 1), shift_seq(value_down, -1)

    hidden_own, hidden_other = hidden_parts
    flops = 2 * X * SEG_LEN * Y * HEAD * KV_COLS
    tokens = [near] + [shift_xy(near, k, 0) for k in range(1, X)]
    value_up, value_down = value_step(3, value_up, None)
    given = on_core(
        given_kernel,
        "given",
        jax.ShapeDtypeStruct((Y * HEAD, KV_COLS), BF16),
        [hidden_other, *tokens],
        flops=flops,
    )
    given, value_up, value_down = barrier((given, value_up, value_down))
    value_up, value_down = value_step(2, value_up, value_down)
    kept, *low = on_core(
        kept_kernel,
        "kept",
        [jax.ShapeDtypeStruct((HEAD, KV_COLS), F32)]
        + [jax.ShapeDtypeStruct((HEAD, KV_COLS), BF16)] * (Y - 1),
        [hidden_own, *tokens, swap_cores(given)],
        flops=flops,
    )
    *low, dvs[1], dvs[7] = barrier((*low, dvs[1], dvs[7]))
    others = [shift_xy(low[k - 1], 0, k) for k in range(1, Y)]
    value_up, value_down = value_step(1, value_up, value_down)
    total = kept
    for other in others:
        total = total + other.astype(F32)
    total, value_up, value_down = barrier((total.astype(BF16), value_up, value_down))
    rows = lax.all_to_all(total, "seq", 0, 0, tiled=True)
    value_grad = finish(dvs[0], value_down, value_up, 1)[0]
    weight_grad = jnp.sum(rows.reshape(SEGMENTS, -1, KV_COLS).astype(F32), axis=0)
    return dq, key_grad, value_grad, weight_grad


def local(hidden_in, queries, keys, values, out_grad, parents, counts):
    dq, key_grad, value_grad, weight_grad = all_grads(
        hidden_in.reshape(SEG_LEN, -1), queries, keys, values, out_grad, parents, counts
    )
    return (
        dq.reshape(1, 1, SEG_LEN, Q_COLS),
        key_grad.reshape(1, 1, SEG_LEN, KV_COLS),
        value_grad.reshape(1, 1, SEG_LEN, KV_COLS),
        weight_grad,
    )


def solution(mesh):
    wide = P("dp", "seq", None, None)
    return jax.shard_map(
        local,
        mesh=mesh,
        in_specs=(wide, wide, wide, wide, wide, P("dp", "seq"), P("dp", "seq")),
        out_specs=(wide, wide, wide, P(("dp", "seq"), None)),
        check_vma=False,
    )
```

```python
import functools
import math

import jax
import jax.numpy as jnp
from jax import lax
from jax.experimental import pallas as pl
from jax.experimental.pallas import tpu as pltpu
from jax.sharding import PartitionSpec as P

SEGMENTS = 8
SEG_LEN = 128
KV_HEADS = 4
GROUP = 8
HEAD = 128
KV_COLS = KV_HEADS * HEAD
Q_COLS = KV_HEADS * GROUP * HEAD
GROUP_COLS = GROUP * HEAD
STATS_HEADS = 2
KERNEL_VMEM = 16 << 20
SCALE = 1.0 / math.sqrt(HEAD)
SCALE_LOG2 = SCALE * math.log2(math.e)
NEG_FILL = -1e30
DEAD_LSE = 1e30
LABEL_ROWS = 16
PACKET_ROWS = 2 * KV_HEADS * SEG_LEN
STATE = 16
BF16 = jnp.bfloat16
F32 = jnp.float32

X, Y, CORES = 4, 4, 2
SHARE = CORES * HEAD


def dot_nt(a, b):
    return lax.dot_general(a, b, (((1,), (1,)), ((), ())), preferred_element_type=F32)


def dot_nn(a, b):
    return lax.dot_general(a, b, (((1,), (0,)), ((), ())), preferred_element_type=F32)


def dot_tn(a, b):
    return lax.dot_general(a, b, (((0,), (0,)), ((), ())), preferred_element_type=F32)


def key_bias(live):
    position = lax.broadcasted_iota(jnp.int32, (SEG_LEN, 1), 0)
    return jnp.where(position < live, 0.0, NEG_FILL).astype(F32)


def own_bias(live, heads):
    key_at = lax.broadcasted_iota(jnp.int32, (SEG_LEN, SEG_LEN), 0)
    query_at = lax.broadcasted_iota(jnp.int32, (SEG_LEN, SEG_LEN), 1)
    tile = jnp.where((key_at <= query_at) & (key_at < live), 0.0, NEG_FILL).astype(F32)
    return jnp.concatenate([tile] * heads, axis=1)


def block_rows(group):
    return slice(group * SEG_LEN, (group + 1) * SEG_LEN)


def key_value(refs, group):
    k_ref, v_ref = refs[0], refs[-1]
    first = KV_COLS if len(refs) == 1 else 0
    rows = block_rows(group)
    return k_ref[rows, :], v_ref[first + rows.start : first + rows.stop, :]


def group_cols(group):
    return slice(group * GROUP_COLS, (group + 1) * GROUP_COLS)


def prep_kernel(q_ref, g_ref, *out_refs):
    for ref, (rows_ref, turned_ref) in ((q_ref, out_refs[:2]), (g_ref, out_refs[2:])):
        for head in range(KV_HEADS * GROUP):
            part = slice(head * HEAD, (head + 1) * HEAD)
            block = ref[:, part]
            rows_ref[part, :] = block
            turned_ref[:, part] = block.T


def scalar_of(rows):
    return jnp.max(rows.astype(F32)).astype(jnp.int32)


def state_value(ref, index):
    return scalar_of(ref[pl.ds(index, 1), :])


def set_state(ref, index, value):
    ref[pl.ds(index, 1), :] = jnp.full((1, HEAD), value, jnp.int32).astype(F32)


def stats_kernel(steps, first, last, *refs):
    if first:
        parent_ref, count_ref, q_ref, g_ref, packet_ref, out_ref, state_ref = refs
    else:
        q_ref, g_ref = refs[:2]
        packet_refs = refs[2:-4]
        in_ref, old_ref, out_ref, state_ref = refs[-4:]
    me = lax.axis_index("seq")

    def add_segment(packet, bias, start):
        width = STATS_HEADS * HEAD
        for group in range(KV_HEADS):
            k, v = key_value(packet, group)
            for chunk in range(GROUP_COLS // width):
                at = group * GROUP_COLS + chunk * width
                cols = slice(at, at + width)
                scores = dot_nn(k, q_ref[:, cols]) * SCALE_LOG2 + bias
                grad_probs = dot_nn(v, g_ref[:, cols])
                top = jnp.max(scores, axis=0, keepdims=True)
                if not start:
                    old_top = out_ref[0:1, cols]
                    top = jnp.maximum(top, old_top)
                weights = jnp.exp2(scores - top)
                total = jnp.sum(weights, axis=0, keepdims=True)
                mixed = jnp.sum(weights * grad_probs, axis=0, keepdims=True)
                if not start:
                    shrink = jnp.exp2(old_top - top)
                    total = total + out_ref[1:2, cols] * shrink
                    mixed = mixed + out_ref[2:3, cols] * shrink
                out_ref[0:1, cols] = top
                out_ref[1:2, cols] = total
                out_ref[2:3, cols] = mixed

    if first:
        live = count_ref[0, 0]
        state_ref[...] = jnp.zeros_like(state_ref)
        set_state(state_ref, 0, parent_ref[0, 0])
        set_state(state_ref, SEGMENTS, live)
        add_segment([packet_ref], own_bias(live, STATS_HEADS), True)
    else:
        state_ref[...] = old_ref[...]
        out_ref[...] = in_ref[...]
        if last:
            ((distance, _),) = steps
            live_there = state_value(old_ref, distance)

            @pl.when(live_there > 0)
            def _():
                add_segment(packet_refs, key_bias(live_there), False)

        else:
            current = state_value(old_ref, 0)
            for packet_ref, (distance, looked_up) in zip(packet_refs, steps):
                top_row = packet_ref.shape[0] - LABEL_ROWS
                hit = current == me - distance
                parent = scalar_of(packet_ref[top_row:, :][: LABEL_ROWS // 2])
                current = jnp.where(hit, parent, current)

                @pl.when(hit)
                def _():
                    live = scalar_of(packet_ref[top_row:, :][LABEL_ROWS // 2 :])
                    set_state(state_ref, distance, live)
                    if not looked_up:
                        add_segment([packet_ref], key_bias(live), False)

            set_state(state_ref, 0, current)

    if last:
        live = state_value(old_ref, SEGMENTS)
        position = lax.broadcasted_iota(jnp.int32, (1, Q_COLS), 1) & (SEG_LEN - 1)
        total = out_ref[1:2, :]
        row_delta = out_ref[2:3, :] / total
        lse = out_ref[0:1, :] + jnp.log2(total)
        out_ref[0:1, :] = jnp.where(position < live, lse, DEAD_LSE)
        out_ref[1:2, :] = row_delta


def grads_kernel(distances, own, halved, *refs):
    state_ref, q_ref, qt_ref, g_ref, gt_ref, stats_ref = refs[:6]
    count = 2 if halved else len(distances)
    arrays, out_refs = refs[6 : 6 + count], refs[6 + count :]
    packets = [arrays] if halved else [[ref] for ref in arrays]

    def one_segment(packet, dk_ref, dv_ref, ds_ref, bias):
        for group in range(KV_HEADS):
            k, v = key_value(packet, group)
            cols = group_cols(group)
            rows = block_rows(group)
            scores = dot_nn(k, qt_ref[:, cols]) * SCALE_LOG2 + bias
            probs = jnp.exp2(scores - stats_ref[0:1, cols])
            grad_probs = dot_nn(v, gt_ref[:, cols])
            grad_scores = (probs * (grad_probs - stats_ref[1:2, cols])).astype(BF16)
            dv = dot_nn(probs.astype(BF16), g_ref[cols, :])
            dk = dot_nn(grad_scores, q_ref[cols, :]) * SCALE
            ds_ref[:, cols] = grad_scores
            dk_ref[rows, :] = dk.astype(dk_ref.dtype)
            dv_ref[rows, :] = dv.astype(dv_ref.dtype)

    if own:
        bias = own_bias(state_value(state_ref, SEGMENTS), GROUP)
        one_segment(packets[0], *out_refs, bias)
        return
    for i, (packet, distance) in enumerate(zip(packets, distances)):
        outs = out_refs[3 * i : 3 * i + 3]
        live = state_value(state_ref, distance)

        @pl.when(live > 0)
        def _():
            one_segment(packet, *outs, key_bias(live))

        @pl.when(live == 0)
        def _():
            for ref in outs:
                ref[...] = jnp.zeros_like(ref)


def query_kernel(*refs):
    key_refs, ds_refs, (out_ref,) = refs[:SEGMENTS], refs[SEGMENTS:-1], refs[-1:]
    for group in range(KV_HEADS):
        cols = group_cols(group)
        total = jnp.zeros((HEAD, GROUP_COLS), F32)
        for key_ref, ds_ref in zip(key_refs, ds_refs):
            total = total + dot_nn(key_ref[block_rows(group), :].T, ds_ref[:, cols])
        for head in range(GROUP):
            part = slice(head * HEAD, (head + 1) * HEAD)
            at = (group * GROUP + head) * HEAD
            out_ref[:, at : at + HEAD] = (total[:, part] * SCALE).T.astype(BF16)


SMEM_SPEC = pl.BlockSpec(memory_space=pltpu.SMEM)
VMEM_SPEC = pl.BlockSpec(memory_space=pltpu.VMEM)
STATS_SHAPE = jax.ShapeDtypeStruct((8, Q_COLS), F32)
STATE_SHAPE = jax.ShapeDtypeStruct((STATE, HEAD), F32)
BLOCK_FLOPS = 2 * SEG_LEN * SEG_LEN * HEAD * KV_HEADS * GROUP


def on_core(kernel, name, out_shape, operands, scalars=0, out_specs=None, flops=0, aliases=None):
    many = isinstance(out_shape, list)
    if out_specs is None:
        out_specs = [VMEM_SPEC] * len(out_shape) if many else VMEM_SPEC
    moved = sum(o.size * o.dtype.itemsize for o in operands)
    return pl.pallas_call(
        kernel,
        out_shape=out_shape,
        in_specs=[SMEM_SPEC] * scalars + [VMEM_SPEC] * (len(operands) - scalars),
        out_specs=out_specs,
        name=name,
        input_output_aliases=aliases or {},
        cost_estimate=pl.CostEstimate(flops=flops, bytes_accessed=moved, transcendentals=0),
        compiler_params=pltpu.CompilerParams(vmem_limit_bytes=KERNEL_VMEM),
    )(*operands)


def prepared(array_q, array_g):
    shapes = [(KV_HEADS * GROUP * SEG_LEN, HEAD), (HEAD, KV_HEADS * GROUP * SEG_LEN)] * 2
    return on_core(
        prep_kernel,
        "prep",
        [jax.ShapeDtypeStruct(shape, BF16) for shape in shapes],
        [array_q, array_g],
    )


def add_stats(heads, packets, steps, state, stats, last=False):
    _, qt, _, gt = heads
    first = stats is None
    if first:
        operands = [*state, qt, gt, *packets]
    else:
        operands = [qt, gt, *packets, stats, state]
    stats, state = on_core(
        functools.partial(stats_kernel, tuple(steps), first, last),
        "stats",
        [STATS_SHAPE, STATE_SHAPE],
        operands,
        scalars=len(state) if first else 0,
        flops=4 * BLOCK_FLOPS * len(packets),
    )
    return state, stats


def segment_grads(heads, state, stats, packets, distances, dtypes, own=False, halved=False):
    count = len(distances)
    shapes = [(KV_COLS, HEAD), (KV_COLS, HEAD), (SEG_LEN, Q_COLS)] * count
    return on_core(
        functools.partial(grads_kernel, tuple(distances), own, halved),
        "grads",
        [jax.ShapeDtypeStruct(shape, dtype) for shape, dtype in zip(shapes, dtypes)],
        [state, *heads, stats, *packets],
        flops=8 * BLOCK_FLOPS * count,
    )


def query_grads(packets, grad_scores):
    return on_core(
        query_kernel,
        "query",
        jax.ShapeDtypeStruct((SEG_LEN, Q_COLS), BF16),
        [*packets, *grad_scores],
        flops=2 * SEGMENTS * BLOCK_FLOPS,
    )


def shift_seq(array, k):
    return lax.ppermute(array, "seq", [(i, (i + k) % SEGMENTS) for i in range(SEGMENTS)])


def swap_cores(array):
    return lax.ppermute(array, "dp", [(i, i ^ 1) for i in range(X * Y * CORES)])


def dp_index(y, x, core):
    return (y % Y * X + x % X) * CORES + core


def shift_xy(array, along_x, along_y):
    pairs = [
        (dp_index(y, x, c), dp_index(y + along_y, x + along_x, c))
        for y in range(Y)
        for x in range(X)
        for c in range(CORES)
    ]
    return lax.ppermute(array, "dp", pairs)


def pack_kernel(parent_ref, count_ref, k_ref, v_ref, out_ref, sems):
    copies = []
    for head in range(KV_HEADS):
        for side, ref in enumerate((k_ref, v_ref)):
            copies.append(
                pltpu.make_async_copy(
                    ref.at[:, pl.ds(head * HEAD, HEAD)],
                    out_ref.at[pl.ds((side * KV_HEADS + head) * SEG_LEN, SEG_LEN), :],
                    sems.at[2 * head + side],
                )
            )
    for copy in copies:
        copy.start()
    row = lax.broadcasted_iota(jnp.int32, (LABEL_ROWS, HEAD), 0)
    labels = jnp.where(row < LABEL_ROWS // 2, parent_ref[0, 0], count_ref[0, 0])
    out_ref[PACKET_ROWS:, :] = labels.astype(F32).astype(BF16)
    for copy in copies:
        copy.wait()


def ring_packet(keys, values, parents, counts):
    return pl.pallas_call(
        pack_kernel,
        out_shape=jax.ShapeDtypeStruct((PACKET_ROWS + LABEL_ROWS, HEAD), BF16),
        in_specs=[SMEM_SPEC, SMEM_SPEC] + [pl.BlockSpec(memory_space=pltpu.HBM)] * 2,
        out_specs=VMEM_SPEC,
        scratch_shapes=[pltpu.SemaphoreType.DMA((2 * KV_HEADS,))],
        name="pack",
        compiler_params=pltpu.CompilerParams(vmem_limit_bytes=KERNEL_VMEM),
    )(
        parents,
        counts,
        pltpu.with_memory_space_constraint(keys, pltpu.HBM),
        pltpu.with_memory_space_constraint(values, pltpu.HBM),
    )


def finish_kernel(mine_ref, down_ref, up_ref, *out_refs):
    for head in range(KV_HEADS):
        rows = block_rows(head)
        total = mine_ref[rows, :] + (
            down_ref[rows, :].astype(F32) + up_ref[rows, :].astype(F32)
        )
        for ref in out_refs:
            ref[:, head * HEAD : (head + 1) * HEAD] = total.astype(BF16)


def finish(mine, down, up, copies):
    return on_core(
        finish_kernel,
        "finish",
        [jax.ShapeDtypeStruct((SEG_LEN, KV_COLS), BF16)] * copies,
        [mine, down, up],
    )


def taken(array, index, axis):
    return lax.dynamic_index_in_dim(array, index, axis, keepdims=False)


def places():
    dp = lax.axis_index("dp")
    core = lax.rem(dp, CORES)
    x = lax.rem(lax.div(dp, CORES), X)
    y = lax.div(dp, CORES * X)
    return y, x, core


def deal_kernel(hidden_ref, *out_refs):
    x = places()[1]
    for k, out_ref in enumerate(out_refs):
        to = lax.rem(x + k, X)
        for y in range(Y):
            first = pl.multiple_of((y * X + to) * SHARE, SHARE)
            out_ref[:, y * SHARE : (y + 1) * SHARE] = hidden_ref[:, pl.ds(first, SHARE)]


def hidden_shares(hidden):
    return on_core(
        deal_kernel, "deal", [jax.ShapeDtypeStruct((SEG_LEN, Y * SHARE), BF16)] * X, [hidden]
    )


def turn_kernel(*refs):
    part_refs, out_refs = refs[:X], refs[X:]
    here, _, core = places()
    for side, out_ref in enumerate(out_refs):
        for k in range(Y):
            of = lax.rem(here + k, Y) * CORES + lax.rem(core + side, CORES)
            first = pl.multiple_of(of * HEAD, HEAD)
            for i, ref in enumerate(part_refs):
                out_ref[k * HEAD : (k + 1) * HEAD, i * SEG_LEN : (i + 1) * SEG_LEN] = ref[
                    :, pl.ds(first, HEAD)
                ].T


def turned(parts):
    return on_core(
        turn_kernel,
        "turn",
        [jax.ShapeDtypeStruct((Y * HEAD, X * SEG_LEN), BF16)] * CORES,
        list(parts),
    )


def given_kernel(hidden_ref, *refs):
    token_refs, (out_ref,) = refs[:X], refs[X:]
    tokens = jnp.concatenate([ref[...] for ref in token_refs], axis=0)
    out_ref[...] = dot_nn(hidden_ref[...], tokens).astype(BF16)


def kept_kernel(hidden_ref, *refs):
    token_refs, got_ref, own_ref, out_refs = refs[:X], refs[X], refs[X + 1], refs[X + 2 :]
    tokens = jnp.concatenate([ref[...] for ref in token_refs], axis=0)
    total = dot_nn(hidden_ref[...], tokens) + got_ref[...].astype(F32)
    own_ref[...] = total[:HEAD]
    for k, ref in enumerate(out_refs):
        ref[...] = total[(k + 1) * HEAD : (k + 2) * HEAD].astype(BF16)


def all_grads(hidden, queries, keys, values, out_grad, parents, counts):
    barrier = lax.optimization_barrier
    own = ring_packet(
        keys.reshape(SEG_LEN, KV_COLS), values.reshape(SEG_LEN, KV_COLS), parents, counts
    )
    up, down = own, own
    below, above = {}, {}
    state, stats = (parents, counts), None
    for step in range(1, 5):
        if step == 2:
            heads = prepared(queries.reshape(SEG_LEN, Q_COLS), out_grad.reshape(SEG_LEN, Q_COLS))
            shares = hidden_shares(hidden)
            label = shift_seq(own[PACKET_ROWS:], 4)
            up, down, label, *rest = barrier((up, down, label, *heads, *shares))
            heads, shares = rest[:4], rest[4:]
            hidden_parts = [
                shift_xy(share, k, 0) if k else share for k, share in enumerate(shares)
            ]
        if step == 3:
            state, stats = add_stats(heads, [own], [], state, None)
            up, down, state, stats = barrier((up, down, state, stats))
            stats, hidden_parts[1] = barrier((stats, hidden_parts[1]))
        if step == 4:
            state, stats = add_stats(
                heads, [below[1], below[2]], [(1, False), (2, False)], state, stats
            )
            up, down, state, stats = barrier((up, down, state, stats))
            farthest = [shift_seq(up[:KV_COLS], 1), shift_seq(down[KV_COLS:PACKET_ROWS], -1)]
            break
        down, up = shift_seq(down, -1), shift_seq(up, 1)
        above[step], below[step] = down, up
    state, stats = add_stats(
        heads,
        [below[3], label, above[3], above[2], above[1]],
        [(3, False), (4, True), (5, False), (6, False), (7, False)],
        state,
        stats,
    )
    stats, hidden_parts[2], hidden_parts[3] = barrier(
        (stats, hidden_parts[2], hidden_parts[3])
    )
    state, stats = add_stats(heads, farthest, [(4, False)], state, stats, last=True)

    dvs, dss = {}, {}
    dk, dvs[4], dss[4] = segment_grads(
        heads, state, stats, farthest, [4], [BF16] * 3, halved=True
    )
    down, up = shift_seq(dk, -1), None
    for step in range(3, 0, -1):
        starts = BF16 if step == 3 else F32
        low, dvs[step], dss[step], high, dvs[8 - step], dss[8 - step] = segment_grads(
            heads,
            state,
            stats,
            [below[step], above[step]],
            [step, 8 - step],
            [F32, starts, BF16, starts, F32, BF16],
        )
        stats, down = barrier((stats, down))
        down = shift_seq((low + down.astype(F32)).astype(BF16), -1)
        up = shift_seq(high if step == 3 else (high + up.astype(F32)).astype(BF16), 1)
    stats, *hidden_parts = barrier((stats, *turned(hidden_parts)))
    value_up = shift_seq(dvs[4], 1)
    mine, dvs[0], dss[0] = segment_grads(
        heads, state, stats, [own], [0], [F32, F32, BF16], own=True
    )
    key_grad, near = finish(mine, down, up, 2)
    near, dvs[3], dvs[5] = barrier((near, dvs[3], dvs[5]))

    def value_step(step, value_up, value_down):
        value_up = (dvs[8 - step] + value_up.astype(F32)).astype(BF16)
        if value_down is None:
            value_down = dvs[step]
        else:
            value_down = (dvs[step] + value_down.astype(F32)).astype(BF16)
        return shift_seq(value_up, 1), shift_seq(value_down, -1)

    hidden_own, hidden_other = hidden_parts
    flops = 2 * X * SEG_LEN * Y * HEAD * KV_COLS
    tokens = [near] + [shift_xy(near, k, 0) for k in range(1, X)]
    value_up, value_down = value_step(3, value_up, None)
    given = on_core(
        given_kernel,
        "given",
        jax.ShapeDtypeStruct((Y * HEAD, KV_COLS), BF16),
        [hidden_other, *tokens],
        flops=flops,
    )
    given, value_up, value_down = barrier((given, value_up, value_down))
    value_up, value_down = value_step(2, value_up, value_down)
    kept, *low = on_core(
        kept_kernel,
        "kept",
        [jax.ShapeDtypeStruct((HEAD, KV_COLS), F32)]
        + [jax.ShapeDtypeStruct((HEAD, KV_COLS), BF16)] * (Y - 1),
        [hidden_own, *tokens, swap_cores(given)],
        flops=flops,
    )
    *low, dvs[1], dvs[7] = barrier((*low, dvs[1], dvs[7]))
    others = [shift_xy(low[k - 1], 0, k) for k in range(1, Y)]
    value_up, value_down = value_step(1, value_up, value_down)
    total = kept
    for other in others:
        total = total + other.astype(F32)
    total, value_up, value_down, dss[0] = barrier(
        (total.astype(BF16), value_up, value_down, dss[0])
    )
    rows = lax.all_to_all(total, "seq", 0, 0, tiled=True)
    value_grad = finish(dvs[0], value_down, value_up, 1)[0]
    packets = [own, below[1], below[2], below[3], farthest[0], above[3], above[2], above[1]]
    dq = query_grads(packets, [dss[distance] for distance in range(SEGMENTS)])
    weight_grad = jnp.sum(rows.reshape(SEGMENTS, -1, KV_COLS).astype(F32), axis=0)
    return dq, key_grad, value_grad, weight_grad


def local(hidden_in, queries, keys, values, out_grad, parents, counts):
    dq, key_grad, value_grad, weight_grad = all_grads(
        hidden_in.reshape(SEG_LEN, -1), queries, keys, values, out_grad, parents, counts
    )
    return (
        dq.reshape(1, 1, SEG_LEN, Q_COLS),
        key_grad.reshape(1, 1, SEG_LEN, KV_COLS),
        value_grad.reshape(1, 1, SEG_LEN, KV_COLS),
        weight_grad,
    )


def solution(mesh):
    wide = P("dp", "seq", None, None)
    return jax.shard_map(
        local,
        mesh=mesh,
        in_specs=(wide, wide, wide, wide, wide, P("dp", "seq"), P("dp", "seq")),
        out_specs=(wide, wide, wide, P(("dp", "seq"), None)),
        check_vma=False,
    )
```

```python
import functools
import math

import jax
import jax.numpy as jnp
from jax import lax
from jax.experimental import pallas as pl
from jax.experimental.pallas import tpu as pltpu
from jax.sharding import PartitionSpec as P

SEGMENTS = 8
SEG_LEN = 128
KV_HEADS = 4
GROUP = 8
HEAD = 128
KV_COLS = KV_HEADS * HEAD
Q_COLS = KV_HEADS * GROUP * HEAD
GROUP_COLS = GROUP * HEAD
STATS_HEADS = 2
KERNEL_VMEM = 8 << 20
QUERY_VMEM = 16 << 20
SCALE = 1.0 / math.sqrt(HEAD)
SCALE_LOG2 = SCALE * math.log2(math.e)
NEG_FILL = -1e30
DEAD_LSE = 1e30
LABEL_ROWS = 16
PACKET_ROWS = 2 * KV_HEADS * SEG_LEN
STATE = 16
BF16 = jnp.bfloat16
F32 = jnp.float32

X, Y, CORES = 4, 4, 2
SHARE = CORES * HEAD


def dot_nt(a, b):
    return lax.dot_general(a, b, (((1,), (1,)), ((), ())), preferred_element_type=F32)


def dot_nn(a, b):
    return lax.dot_general(a, b, (((1,), (0,)), ((), ())), preferred_element_type=F32)


def dot_tn(a, b):
    return lax.dot_general(a, b, (((0,), (0,)), ((), ())), preferred_element_type=F32)


def key_bias(live):
    position = lax.broadcasted_iota(jnp.int32, (SEG_LEN, 1), 0)
    return jnp.where(position < live, 0.0, NEG_FILL).astype(F32)


def own_bias(live, heads):
    key_at = lax.broadcasted_iota(jnp.int32, (SEG_LEN, SEG_LEN), 0)
    query_at = lax.broadcasted_iota(jnp.int32, (SEG_LEN, SEG_LEN), 1)
    tile = jnp.where((key_at <= query_at) & (key_at < live), 0.0, NEG_FILL).astype(F32)
    return jnp.concatenate([tile] * heads, axis=1)


def block_rows(group):
    return slice(group * SEG_LEN, (group + 1) * SEG_LEN)


def key_value(refs, group):
    k_ref, v_ref = refs[0], refs[-1]
    first = KV_COLS if len(refs) == 1 else 0
    rows = block_rows(group)
    return k_ref[rows, :], v_ref[first + rows.start : first + rows.stop, :]


def group_cols(group):
    return slice(group * GROUP_COLS, (group + 1) * GROUP_COLS)


def scalar_of(rows):
    return jnp.max(rows.astype(F32)).astype(jnp.int32)


def state_value(ref, index):
    return scalar_of(ref[pl.ds(index, 1), :])


def set_state(ref, index, value):
    ref[pl.ds(index, 1), :] = jnp.full((1, HEAD), value, jnp.int32).astype(F32)


def stats_kernel(steps, first, last, *refs):
    if first:
        parent_ref, count_ref, q_ref, g_ref, packet_ref, out_ref, state_ref = refs
    else:
        q_ref, g_ref = refs[:2]
        packet_refs = refs[2:-4]
        in_ref, old_ref, out_ref, state_ref = refs[-4:]
    me = lax.axis_index("seq")

    def add_segment(packet, bias, start):
        width = STATS_HEADS * HEAD
        for group in range(KV_HEADS):
            k, v = key_value(packet, group)
            for chunk in range(GROUP_COLS // width):
                at = group * GROUP_COLS + chunk * width
                cols = slice(at, at + width)
                scores = dot_nn(k, q_ref[:, cols]) * SCALE_LOG2 + bias
                grad_probs = dot_nn(v, g_ref[:, cols])
                top = jnp.max(scores, axis=0, keepdims=True)
                if not start:
                    old_top = out_ref[0:1, cols]
                    top = jnp.maximum(top, old_top)
                weights = jnp.exp2(scores - top)
                total = jnp.sum(weights, axis=0, keepdims=True)
                mixed = jnp.sum(weights * grad_probs, axis=0, keepdims=True)
                if not start:
                    shrink = jnp.exp2(old_top - top)
                    total = total + out_ref[1:2, cols] * shrink
                    mixed = mixed + out_ref[2:3, cols] * shrink
                out_ref[0:1, cols] = top
                out_ref[1:2, cols] = total
                out_ref[2:3, cols] = mixed

    if first:
        live = count_ref[0, 0]
        state_ref[...] = jnp.zeros_like(state_ref)
        set_state(state_ref, 0, parent_ref[0, 0])
        set_state(state_ref, SEGMENTS, live)
        add_segment([packet_ref], own_bias(live, STATS_HEADS), True)
    else:
        state_ref[...] = old_ref[...]
        out_ref[...] = in_ref[...]
        if last:
            ((distance, _),) = steps
            live_there = state_value(old_ref, distance)

            @pl.when(live_there > 0)
            def _():
                add_segment(packet_refs, key_bias(live_there), False)

        else:
            current = state_value(old_ref, 0)
            for packet_ref, (distance, looked_up) in zip(packet_refs, steps):
                top_row = packet_ref.shape[0] - LABEL_ROWS
                hit = current == me - distance
                parent = scalar_of(packet_ref[top_row:, :][: LABEL_ROWS // 2])
                current = jnp.where(hit, parent, current)

                @pl.when(hit)
                def _():
                    live = scalar_of(packet_ref[top_row:, :][LABEL_ROWS // 2 :])
                    set_state(state_ref, distance, live)
                    if not looked_up:
                        add_segment([packet_ref], key_bias(live), False)

            set_state(state_ref, 0, current)

    if last:
        live = state_value(old_ref, SEGMENTS)
        position = lax.broadcasted_iota(jnp.int32, (1, Q_COLS), 1) & (SEG_LEN - 1)
        total = out_ref[1:2, :]
        row_delta = out_ref[2:3, :] / total
        lse = out_ref[0:1, :] + jnp.log2(total)
        out_ref[0:1, :] = jnp.where(position < live, lse, DEAD_LSE)
        out_ref[1:2, :] = row_delta


def grads_kernel(distances, own, halved, *refs):
    state_ref, q_ref, qt_ref, g_ref, gt_ref, stats_ref = refs[:6]
    count = 2 if halved else len(distances)
    arrays, out_refs = refs[6 : 6 + count], refs[6 + count :]
    packets = [arrays] if halved else [[ref] for ref in arrays]

    def one_segment(packet, dk_ref, dv_ref, ds_ref, bias):
        for group in range(KV_HEADS):
            k, v = key_value(packet, group)
            cols = group_cols(group)
            rows = block_rows(group)
            scores = dot_nn(k, qt_ref[:, cols]) * SCALE_LOG2 + bias
            probs = jnp.exp2(scores - stats_ref[0:1, cols])
            grad_probs = dot_nn(v, gt_ref[:, cols])
            grad_scores = (probs * (grad_probs - stats_ref[1:2, cols])).astype(BF16)
            dv = dot_nn(probs.astype(BF16), g_ref[cols, :])
            dk = dot_nn(grad_scores, q_ref[cols, :]) * SCALE
            ds_ref[:, cols] = grad_scores
            dk_ref[rows, :] = dk.astype(dk_ref.dtype)
            dv_ref[rows, :] = dv.astype(dv_ref.dtype)

    if own:
        bias = own_bias(state_value(state_ref, SEGMENTS), GROUP)
        one_segment(packets[0], *out_refs, bias)
        return
    for i, (packet, distance) in enumerate(zip(packets, distances)):
        outs = out_refs[3 * i : 3 * i + 3]
        live = state_value(state_ref, distance)

        @pl.when(live > 0)
        def _():
            one_segment(packet, *outs, key_bias(live))

        @pl.when(live == 0)
        def _():
            for ref in outs:
                ref[...] = jnp.zeros_like(ref)


def query_kernel(*refs):
    key_refs, ds_refs, (out_ref,) = refs[:SEGMENTS], refs[SEGMENTS:-1], refs[-1:]
    total = jnp.zeros((HEAD, GROUP_COLS), F32)
    for key_ref, ds_ref in zip(key_refs, ds_refs):
        total = total + dot_nn(key_ref[...].T, ds_ref[...])
    for head in range(GROUP):
        part = slice(head * HEAD, (head + 1) * HEAD)
        out_ref[:, part] = (total[:, part] * SCALE).T.astype(BF16)


SMEM_SPEC = pl.BlockSpec(memory_space=pltpu.SMEM)
VMEM_SPEC = pl.BlockSpec(memory_space=pltpu.VMEM)
STATS_SHAPE = jax.ShapeDtypeStruct((8, Q_COLS), F32)
STATE_SHAPE = jax.ShapeDtypeStruct((STATE, HEAD), F32)
BLOCK_FLOPS = 2 * SEG_LEN * SEG_LEN * HEAD * KV_HEADS * GROUP


def on_core(kernel, name, out_shape, operands, scalars=0, out_specs=None, flops=0, aliases=None):
    many = isinstance(out_shape, list)
    if out_specs is None:
        out_specs = [VMEM_SPEC] * len(out_shape) if many else VMEM_SPEC
    moved = sum(o.size * o.dtype.itemsize for o in operands)
    return pl.pallas_call(
        kernel,
        out_shape=out_shape,
        in_specs=[SMEM_SPEC] * scalars + [VMEM_SPEC] * (len(operands) - scalars),
        out_specs=out_specs,
        name=name,
        input_output_aliases=aliases or {},
        cost_estimate=pl.CostEstimate(flops=flops, bytes_accessed=moved, transcendentals=0),
        compiler_params=pltpu.CompilerParams(vmem_limit_bytes=KERNEL_VMEM),
    )(*operands)


def add_stats(heads, packets, steps, state, stats, last=False):
    _, qt, _, gt = heads
    first = stats is None
    if first:
        operands = [*state, qt, gt, *packets]
    else:
        operands = [qt, gt, *packets, stats, state]
    stats, state = on_core(
        functools.partial(stats_kernel, tuple(steps), first, last),
        "stats",
        [STATS_SHAPE, STATE_SHAPE],
        operands,
        scalars=len(state) if first else 0,
        flops=4 * BLOCK_FLOPS * len(packets),
    )
    return state, stats


def segment_grads(heads, state, stats, packets, distances, dtypes, own=False, halved=False):
    count = len(distances)
    shapes = [(KV_COLS, HEAD), (KV_COLS, HEAD), (SEG_LEN, Q_COLS)] * count
    return on_core(
        functools.partial(grads_kernel, tuple(distances), own, halved),
        "grads",
        [jax.ShapeDtypeStruct(shape, dtype) for shape, dtype in zip(shapes, dtypes)],
        [state, *heads, stats, *packets],
        flops=8 * BLOCK_FLOPS * count,
    )


def query_grads(packets, grad_scores):
    columns = pl.BlockSpec((SEG_LEN, GROUP_COLS), lambda group: (0, group))
    return pl.pallas_call(
        query_kernel,
        grid=(KV_HEADS,),
        out_shape=jax.ShapeDtypeStruct((SEG_LEN, Q_COLS), BF16),
        in_specs=[pl.BlockSpec((SEG_LEN, HEAD), lambda group: (group, 0))] * SEGMENTS
        + [columns] * SEGMENTS,
        out_specs=columns,
        name="query",
        cost_estimate=pl.CostEstimate(
            flops=2 * SEGMENTS * BLOCK_FLOPS,
            bytes_accessed=2 * (SEGMENTS + 1) * SEG_LEN * Q_COLS,
            transcendentals=0,
        ),
        compiler_params=pltpu.CompilerParams(vmem_limit_bytes=QUERY_VMEM),
    )(*packets, *grad_scores)


def shift_seq(array, k):
    return lax.ppermute(array, "seq", [(i, (i + k) % SEGMENTS) for i in range(SEGMENTS)])


def swap_cores(array):
    return lax.ppermute(array, "dp", [(i, i ^ 1) for i in range(X * Y * CORES)])


def dp_index(y, x, core):
    return (y % Y * X + x % X) * CORES + core


def shift_xy(array, along_x, along_y):
    pairs = [
        (dp_index(y, x, c), dp_index(y + along_y, x + along_x, c))
        for y in range(Y)
        for x in range(X)
        for c in range(CORES)
    ]
    return lax.ppermute(array, "dp", pairs)


def pack_kernel(parent_ref, count_ref, k_ref, v_ref, out_ref, sems):
    copies = []
    for head in range(KV_HEADS):
        for side, ref in enumerate((k_ref, v_ref)):
            copies.append(
                pltpu.make_async_copy(
                    ref.at[:, pl.ds(head * HEAD, HEAD)],
                    out_ref.at[pl.ds((side * KV_HEADS + head) * SEG_LEN, SEG_LEN), :],
                    sems.at[2 * head + side],
                )
            )
    for copy in copies:
        copy.start()
    row = lax.broadcasted_iota(jnp.int32, (LABEL_ROWS, HEAD), 0)
    labels = jnp.where(row < LABEL_ROWS // 2, parent_ref[0, 0], count_ref[0, 0])
    out_ref[PACKET_ROWS:, :] = labels.astype(F32).astype(BF16)
    for copy in copies:
        copy.wait()


def ring_packet(keys, values, parents, counts):
    return pl.pallas_call(
        pack_kernel,
        out_shape=jax.ShapeDtypeStruct((PACKET_ROWS + LABEL_ROWS, HEAD), BF16),
        in_specs=[SMEM_SPEC, SMEM_SPEC] + [pl.BlockSpec(memory_space=pltpu.HBM)] * 2,
        out_specs=VMEM_SPEC,
        scratch_shapes=[pltpu.SemaphoreType.DMA((2 * KV_HEADS,))],
        name="pack",
        compiler_params=pltpu.CompilerParams(vmem_limit_bytes=KERNEL_VMEM),
    )(
        parents,
        counts,
        pltpu.with_memory_space_constraint(keys, pltpu.HBM),
        pltpu.with_memory_space_constraint(values, pltpu.HBM),
    )


def finish_kernel(mine_ref, down_ref, up_ref, *out_refs):
    for head in range(KV_HEADS):
        rows = block_rows(head)
        total = mine_ref[rows, :] + (
            down_ref[rows, :].astype(F32) + up_ref[rows, :].astype(F32)
        )
        for ref in out_refs:
            ref[:, head * HEAD : (head + 1) * HEAD] = total.astype(BF16)


def finish(mine, down, up, copies):
    return on_core(
        finish_kernel,
        "finish",
        [jax.ShapeDtypeStruct((SEG_LEN, KV_COLS), BF16)] * copies,
        [mine, down, up],
    )


def taken(array, index, axis):
    return lax.dynamic_index_in_dim(array, index, axis, keepdims=False)


def places():
    dp = lax.axis_index("dp")
    core = lax.rem(dp, CORES)
    x = lax.rem(lax.div(dp, CORES), X)
    y = lax.div(dp, CORES * X)
    return y, x, core


def load_kernel(q_ref, g_ref, hidden_ref, *refs):
    head_refs, share_refs, (buffer, head_sems, share_sems) = refs[:4], refs[4:-3], refs[-3:]
    copies = [
        pltpu.make_async_copy(ref, buffer.at[i], head_sems.at[i])
        for i, ref in enumerate((q_ref, g_ref))
    ]
    x = places()[1]
    for k, ref in enumerate(share_refs):
        to = lax.rem(x + k, X)
        for y in range(Y):
            first = pl.multiple_of((y * X + to) * SHARE, SHARE)
            copies.append(
                pltpu.make_async_copy(
                    hidden_ref.at[:, pl.ds(first, SHARE)],
                    ref.at[:, pl.ds(y * SHARE, SHARE)],
                    share_sems.at[k * Y + y],
                )
            )
    for copy in copies:
        copy.start()
    for i in range(2):
        copies[i].wait()
        rows_ref, turned_ref = head_refs[2 * i : 2 * i + 2]
        for head in range(KV_HEADS * GROUP):
            part = slice(head * HEAD, (head + 1) * HEAD)
            block = buffer[i, :, part]
            rows_ref[part, :] = block
            turned_ref[:, part] = block.T
    for copy in copies[2:]:
        copy.wait()


def loaded(array_q, array_g, hidden):
    shapes = [(KV_HEADS * GROUP * SEG_LEN, HEAD), (HEAD, KV_HEADS * GROUP * SEG_LEN)] * 2
    shapes += [(SEG_LEN, Y * SHARE)] * X
    outs = pl.pallas_call(
        load_kernel,
        out_shape=[jax.ShapeDtypeStruct(shape, BF16) for shape in shapes],
        in_specs=[pl.BlockSpec(memory_space=pltpu.HBM)] * 3,
        out_specs=[VMEM_SPEC] * len(shapes),
        scratch_shapes=[
            pltpu.VMEM((2, SEG_LEN, Q_COLS), BF16),
            pltpu.SemaphoreType.DMA((2,)),
            pltpu.SemaphoreType.DMA((X * Y,)),
        ],
        name="load",
        compiler_params=pltpu.CompilerParams(vmem_limit_bytes=KERNEL_VMEM),
    )(*[pltpu.with_memory_space_constraint(a, pltpu.HBM) for a in (array_q, array_g, hidden)])
    return outs[:4], outs[4:]


def turn_kernel(*refs):
    part_refs, out_refs = refs[:X], refs[X:]
    here, _, core = places()
    for side, out_ref in enumerate(out_refs):
        for k in range(Y):
            of = lax.rem(here + k, Y) * CORES + lax.rem(core + side, CORES)
            first = pl.multiple_of(of * HEAD, HEAD)
            for i, ref in enumerate(part_refs):
                out_ref[k * HEAD : (k + 1) * HEAD, i * SEG_LEN : (i + 1) * SEG_LEN] = ref[
                    :, pl.ds(first, HEAD)
                ].T


def turned(parts):
    return on_core(
        turn_kernel,
        "turn",
        [jax.ShapeDtypeStruct((Y * HEAD, X * SEG_LEN), BF16)] * CORES,
        list(parts),
    )


def given_kernel(hidden_ref, *refs):
    token_refs, (out_ref,) = refs[:X], refs[X:]
    tokens = jnp.concatenate([ref[...] for ref in token_refs], axis=0)
    out_ref[...] = dot_nn(hidden_ref[...], tokens).astype(BF16)


def kept_kernel(hidden_ref, *refs):
    token_refs, got_ref, own_ref, out_refs = refs[:X], refs[X], refs[X + 1], refs[X + 2 :]
    tokens = jnp.concatenate([ref[...] for ref in token_refs], axis=0)
    total = dot_nn(hidden_ref[...], tokens) + got_ref[...].astype(F32)
    own_ref[...] = total[:HEAD]
    for k, ref in enumerate(out_refs):
        ref[...] = total[(k + 1) * HEAD : (k + 2) * HEAD].astype(BF16)


def all_grads(hidden, queries, keys, values, out_grad, parents, counts):
    barrier = lax.optimization_barrier
    own = ring_packet(
        keys.reshape(SEG_LEN, KV_COLS), values.reshape(SEG_LEN, KV_COLS), parents, counts
    )
    up, down = own, own
    below, above = {}, {}
    state, stats = (parents, counts), None
    for step in range(1, 5):
        if step == 2:
            heads, shares = loaded(
                queries.reshape(SEG_LEN, Q_COLS), out_grad.reshape(SEG_LEN, Q_COLS), hidden
            )
            label = shift_seq(own[PACKET_ROWS:], 4)
            up, down, label, *rest = barrier((up, down, label, *heads, *shares))
            heads, shares = rest[:4], rest[4:]
            hidden_parts = [
                shift_xy(share, k, 0) if k else share for k, share in enumerate(shares)
            ]
        if step == 3:
            state, stats = add_stats(heads, [own], [], state, None)
            up, down, state, stats = barrier((up, down, state, stats))
            stats, hidden_parts[1] = barrier((stats, hidden_parts[1]))
        if step == 4:
            state, stats = add_stats(
                heads, [below[1], below[2]], [(1, False), (2, False)], state, stats
            )
            up, down, state, stats = barrier((up, down, state, stats))
            farthest = [shift_seq(up[:KV_COLS], 1), shift_seq(down[KV_COLS:PACKET_ROWS], -1)]
            break
        down, up = shift_seq(down, -1), shift_seq(up, 1)
        above[step], below[step] = down, up
    state, stats = add_stats(
        heads,
        [below[3], label, above[3], above[2], above[1]],
        [(3, False), (4, True), (5, False), (6, False), (7, False)],
        state,
        stats,
    )
    stats, hidden_parts[2], hidden_parts[3] = barrier(
        (stats, hidden_parts[2], hidden_parts[3])
    )
    state, stats = add_stats(heads, farthest, [(4, False)], state, stats, last=True)

    dvs, dss = {}, {}
    dk, dvs[4], dss[4] = segment_grads(
        heads, state, stats, farthest, [4], [BF16] * 3, halved=True
    )
    down, up = shift_seq(dk, -1), None
    for step in range(3, 0, -1):
        starts = BF16 if step == 3 else F32
        low, dvs[step], dss[step], high, dvs[8 - step], dss[8 - step] = segment_grads(
            heads,
            state,
            stats,
            [below[step], above[step]],
            [step, 8 - step],
            [F32, starts, BF16, starts, F32, BF16],
        )
        stats, down = barrier((stats, down))
        down = shift_seq((low + down.astype(F32)).astype(BF16), -1)
        up = shift_seq(high if step == 3 else (high + up.astype(F32)).astype(BF16), 1)
    stats, *hidden_parts = barrier((stats, *turned(hidden_parts)))
    value_up = shift_seq(dvs[4], 1)
    mine, dvs[0], dss[0] = segment_grads(
        heads, state, stats, [own], [0], [F32, F32, BF16], own=True
    )
    key_grad, near = finish(mine, down, up, 2)
    near, dvs[3], dvs[5] = barrier((near, dvs[3], dvs[5]))

    def value_step(step, value_up, value_down):
        value_up = (dvs[8 - step] + value_up.astype(F32)).astype(BF16)
        if value_down is None:
            value_down = dvs[step]
        else:
            value_down = (dvs[step] + value_down.astype(F32)).astype(BF16)
        return shift_seq(value_up, 1), shift_seq(value_down, -1)

    hidden_own, hidden_other = hidden_parts
    flops = 2 * X * SEG_LEN * Y * HEAD * KV_COLS
    tokens = [near] + [shift_xy(near, k, 0) for k in range(1, X)]
    value_up, value_down = value_step(3, value_up, None)
    given = on_core(
        given_kernel,
        "given",
        jax.ShapeDtypeStruct((Y * HEAD, KV_COLS), BF16),
        [hidden_other, *tokens],
        flops=flops,
    )
    given, value_up, value_down = barrier((given, value_up, value_down))
    value_up, value_down = value_step(2, value_up, value_down)
    kept, *low = on_core(
        kept_kernel,
        "kept",
        [jax.ShapeDtypeStruct((HEAD, KV_COLS), F32)]
        + [jax.ShapeDtypeStruct((HEAD, KV_COLS), BF16)] * (Y - 1),
        [hidden_own, *tokens, swap_cores(given)],
        flops=flops,
    )
    *low, dvs[1], dvs[7] = barrier((*low, dvs[1], dvs[7]))
    others = [shift_xy(low[k - 1], 0, k) for k in range(1, Y)]
    value_up, value_down = value_step(1, value_up, value_down)
    total = kept
    for other in others:
        total = total + other.astype(F32)
    total, value_up, value_down, dss[0] = barrier(
        (total.astype(BF16), value_up, value_down, dss[0])
    )
    rows = lax.all_to_all(total, "seq", 0, 0, tiled=True)
    value_grad = finish(dvs[0], value_down, value_up, 1)[0]
    packets = [own, below[1], below[2], below[3], farthest[0], above[3], above[2], above[1]]
    dq = query_grads(packets, [dss[distance] for distance in range(SEGMENTS)])
    weight_grad = jnp.sum(rows.reshape(SEGMENTS, -1, KV_COLS).astype(F32), axis=0)
    return dq, key_grad, value_grad, weight_grad


def local(hidden_in, queries, keys, values, out_grad, parents, counts):
    dq, key_grad, value_grad, weight_grad = all_grads(
        hidden_in.reshape(SEG_LEN, -1), queries, keys, values, out_grad, parents, counts
    )
    return (
        dq.reshape(1, 1, SEG_LEN, Q_COLS),
        key_grad.reshape(1, 1, SEG_LEN, KV_COLS),
        value_grad.reshape(1, 1, SEG_LEN, KV_COLS),
        weight_grad,
    )


def solution(mesh):
    wide = P("dp", "seq", None, None)
    return jax.shard_map(
        local,
        mesh=mesh,
        in_specs=(wide, wide, wide, wide, wide, P("dp", "seq"), P("dp", "seq")),
        out_specs=(wide, wide, wide, P(("dp", "seq"), None)),
        check_vma=False,
    )
```

```python
import functools
import itertools
import math

import jax
import jax.numpy as jnp
from jax import lax
from jax.experimental import pallas as pl
from jax.experimental.pallas import tpu as pltpu
from jax.sharding import PartitionSpec as P

SEGMENTS = 8
SEG_LEN = 128
KV_HEADS = 4
GROUP = 8
HEAD = 128
KV_COLS = KV_HEADS * HEAD
Q_COLS = KV_HEADS * GROUP * HEAD
GROUP_COLS = GROUP * HEAD
STATS_HEADS = 2
KERNEL_VMEM = 16 << 20
SCALE = 1.0 / math.sqrt(HEAD)
SCALE_LOG2 = SCALE * math.log2(math.e)
NEG_FILL = -1e30
DEAD_LSE = 1e30
LABEL_ROWS = 16
PACKET_ROWS = 2 * KV_HEADS * SEG_LEN
STATE = 16
BF16 = jnp.bfloat16
F32 = jnp.float32

X, Y, CORES = 4, 4, 2
SHARE = CORES * HEAD


def dot_nt(a, b):
    return lax.dot_general(a, b, (((1,), (1,)), ((), ())), preferred_element_type=F32)


def dot_nn(a, b):
    return lax.dot_general(a, b, (((1,), (0,)), ((), ())), preferred_element_type=F32)


def dot_tn(a, b):
    return lax.dot_general(a, b, (((0,), (0,)), ((), ())), preferred_element_type=F32)


def key_bias(live):
    position = lax.broadcasted_iota(jnp.int32, (SEG_LEN, 1), 0)
    return jnp.where(position < live, 0.0, NEG_FILL).astype(F32)


def own_bias(live, heads):
    key_at = lax.broadcasted_iota(jnp.int32, (SEG_LEN, SEG_LEN), 0)
    query_at = lax.broadcasted_iota(jnp.int32, (SEG_LEN, SEG_LEN), 1)
    tile = jnp.where((key_at <= query_at) & (key_at < live), 0.0, NEG_FILL).astype(F32)
    return jnp.concatenate([tile] * heads, axis=1)


def block_rows(group):
    return slice(group * SEG_LEN, (group + 1) * SEG_LEN)


def key_value(refs, group):
    k_ref, v_ref = refs[0], refs[-1]
    first = KV_COLS if len(refs) == 1 else 0
    rows = block_rows(group)
    return k_ref[rows, :], v_ref[first + rows.start : first + rows.stop, :]


def group_cols(group):
    return slice(group * GROUP_COLS, (group + 1) * GROUP_COLS)


def scalar_of(rows):
    return jnp.max(rows.astype(F32)).astype(jnp.int32)


def state_value(ref, index):
    return scalar_of(ref[pl.ds(index, 1), :])


def set_state(ref, index, value):
    ref[pl.ds(index, 1), :] = jnp.full((1, HEAD), value, jnp.int32).astype(F32)


def stats_kernel(steps, first, last, *refs):
    if first:
        parent_ref, count_ref, q_ref, g_ref, packet_ref, out_ref, state_ref = refs
    else:
        q_ref, g_ref = refs[:2]
        packet_refs = refs[2:-4]
        in_ref, old_ref, out_ref, state_ref = refs[-4:]
    me = lax.axis_index("seq")

    def add_segment(packet, bias, start):
        width = STATS_HEADS * HEAD
        for group in range(KV_HEADS):
            k, v = key_value(packet, group)
            for chunk in range(GROUP_COLS // width):
                at = group * GROUP_COLS + chunk * width
                cols = slice(at, at + width)
                scores = dot_nn(k, q_ref[:, cols]) * SCALE_LOG2 + bias
                grad_probs = dot_nn(v, g_ref[:, cols])
                top = jnp.max(scores, axis=0, keepdims=True)
                if not start:
                    old_top = out_ref[0:1, cols]
                    top = jnp.maximum(top, old_top)
                weights = jnp.exp2(scores - top)
                total = jnp.sum(weights, axis=0, keepdims=True)
                mixed = jnp.sum(weights * grad_probs, axis=0, keepdims=True)
                if not start:
                    shrink = jnp.exp2(old_top - top)
                    total = total + out_ref[1:2, cols] * shrink
                    mixed = mixed + out_ref[2:3, cols] * shrink
                out_ref[0:1, cols] = top
                out_ref[1:2, cols] = total
                out_ref[2:3, cols] = mixed

    if first:
        live = count_ref[0, 0]
        state_ref[...] = jnp.zeros_like(state_ref)
        set_state(state_ref, 0, parent_ref[0, 0])
        set_state(state_ref, SEGMENTS, live)
        add_segment([packet_ref], own_bias(live, STATS_HEADS), True)
    else:
        state_ref[...] = old_ref[...]
        out_ref[...] = in_ref[...]
        if last:
            ((distance, _),) = steps
            live_there = state_value(old_ref, distance)

            @pl.when(live_there > 0)
            def _():
                add_segment(packet_refs, key_bias(live_there), False)

        else:
            current = state_value(old_ref, 0)
            for packet_ref, (distance, looked_up) in zip(packet_refs, steps):
                top_row = packet_ref.shape[0] - LABEL_ROWS
                hit = current == me - distance
                parent = scalar_of(packet_ref[top_row:, :][: LABEL_ROWS // 2])
                current = jnp.where(hit, parent, current)

                @pl.when(hit)
                def _():
                    live = scalar_of(packet_ref[top_row:, :][LABEL_ROWS // 2 :])
                    set_state(state_ref, distance, live)
                    if not looked_up:
                        add_segment([packet_ref], key_bias(live), False)

            set_state(state_ref, 0, current)

    if last:
        live = state_value(old_ref, SEGMENTS)
        position = lax.broadcasted_iota(jnp.int32, (1, Q_COLS), 1) & (SEG_LEN - 1)
        total = out_ref[1:2, :]
        row_delta = out_ref[2:3, :] / total
        lse = out_ref[0:1, :] + jnp.log2(total)
        out_ref[0:1, :] = jnp.where(position < live, lse, DEAD_LSE)
        out_ref[1:2, :] = row_delta


def grads_kernel(distances, first, last, *refs):
    state_ref, q_ref, qt_ref, g_ref, gt_ref, stats_ref = refs[:6]
    count = 2 if first else len(distances)
    arrays, rest = refs[6 : 6 + count], refs[6 + count :]
    packets = [arrays] if first else [[ref] for ref in arrays]
    if first:
        in_ref, (acc_ref, *out_refs) = None, rest
    else:
        in_ref, acc_ref, *out_refs = rest

    def run(segments):
        for group in range(KV_HEADS):
            blocks = [key_value(packet, group) for packet, _, _ in segments]
            k = jnp.concatenate([block[0] for block in blocks], axis=0)
            v = jnp.concatenate([block[1] for block in blocks], axis=0)
            bias = jnp.concatenate([bias for _, bias, _ in segments], axis=0)
            cols = group_cols(group)
            scores = dot_nn(k, qt_ref[:, cols]) * SCALE_LOG2 + bias
            probs = jnp.exp2(scores - stats_ref[0:1, cols])
            grad_probs = dot_nn(v, gt_ref[:, cols])
            grad_scores = (probs * (grad_probs - stats_ref[1:2, cols])).astype(BF16)
            dv = dot_nn(probs.astype(BF16), g_ref[cols, :])
            dk = dot_nn(grad_scores, q_ref[cols, :]) * SCALE
            dq = dot_nn(k.T, grad_scores)
            if in_ref is not None:
                dq = dq + in_ref[:, cols]
            if last:
                for head in range(GROUP):
                    part = slice(head * HEAD, (head + 1) * HEAD)
                    at = (group * GROUP + head) * HEAD
                    acc_ref[:, at : at + HEAD] = (dq[:, part] * SCALE).T.astype(BF16)
            else:
                acc_ref[:, cols] = dq
            for i, (_, _, (dk_ref, dv_ref)) in enumerate(segments):
                part = slice(i * SEG_LEN, (i + 1) * SEG_LEN)
                dk_ref[block_rows(group), :] = dk[part].astype(dk_ref.dtype)
                dv_ref[block_rows(group), :] = dv[part].astype(dv_ref.dtype)

    if last:
        bias = own_bias(state_value(state_ref, SEGMENTS), GROUP)
        run([(packets[0], bias, out_refs)])
        return
    lives = [state_value(state_ref, distance) for distance in distances]
    outs = [out_refs[2 * i : 2 * i + 2] for i in range(len(distances))]
    for chosen in itertools.product((False, True), repeat=len(distances)):
        taken_here = functools.reduce(
            jnp.logical_and,
            [(live > 0) if choice else (live == 0) for live, choice in zip(lives, chosen)],
        )

        @pl.when(taken_here)
        def _():
            for choice, pair in zip(chosen, outs):
                if not choice:
                    for ref in pair:
                        ref[...] = jnp.zeros_like(ref)
            if any(chosen):
                run(
                    [
                        (packet, key_bias(live), pair)
                        for packet, live, pair, choice in zip(packets, lives, outs, chosen)
                        if choice
                    ]
                )
            elif in_ref is None:
                acc_ref[...] = jnp.zeros_like(acc_ref)
            else:
                acc_ref[...] = in_ref[...]


SMEM_SPEC = pl.BlockSpec(memory_space=pltpu.SMEM)
VMEM_SPEC = pl.BlockSpec(memory_space=pltpu.VMEM)
STATS_SHAPE = jax.ShapeDtypeStruct((8, Q_COLS), F32)
STATE_SHAPE = jax.ShapeDtypeStruct((STATE, HEAD), F32)
BLOCK_FLOPS = 2 * SEG_LEN * SEG_LEN * HEAD * KV_HEADS * GROUP


def on_core(kernel, name, out_shape, operands, scalars=0, out_specs=None, flops=0, aliases=None):
    many = isinstance(out_shape, list)
    if out_specs is None:
        out_specs = [VMEM_SPEC] * len(out_shape) if many else VMEM_SPEC
    moved = sum(o.size * o.dtype.itemsize for o in operands)
    return pl.pallas_call(
        kernel,
        out_shape=out_shape,
        in_specs=[SMEM_SPEC] * scalars + [VMEM_SPEC] * (len(operands) - scalars),
        out_specs=out_specs,
        name=name,
        input_output_aliases=aliases or {},
        cost_estimate=pl.CostEstimate(flops=flops, bytes_accessed=moved, transcendentals=0),
        compiler_params=pltpu.CompilerParams(vmem_limit_bytes=KERNEL_VMEM),
    )(*operands)


def add_stats(heads, packets, steps, state, stats, last=False):
    _, qt, _, gt = heads
    first = stats is None
    if first:
        operands = [*state, qt, gt, *packets]
    else:
        operands = [qt, gt, *packets, stats, state]
    stats, state = on_core(
        functools.partial(stats_kernel, tuple(steps), first, last),
        "stats",
        [STATS_SHAPE, STATE_SHAPE],
        operands,
        scalars=len(state) if first else 0,
        flops=4 * BLOCK_FLOPS * len(packets),
    )
    return state, stats


def add_grads(heads, state, stats, packets, distances, acc, dtypes, last=False):
    first = acc is None
    operands = [state, *heads, stats, *packets]
    aliases = {}
    if not first:
        if not last:
            aliases = {len(operands): 0}
        operands.append(acc)
    if last:
        out_shapes = [jax.ShapeDtypeStruct((SEG_LEN, Q_COLS), BF16)]
    else:
        out_shapes = [jax.ShapeDtypeStruct((HEAD, Q_COLS), F32)]
    out_shapes += [jax.ShapeDtypeStruct((KV_COLS, HEAD), dtype) for dtype in dtypes]
    return on_core(
        functools.partial(grads_kernel, tuple(distances), first, last),
        "grads",
        out_shapes,
        operands,
        flops=10 * BLOCK_FLOPS * len(distances),
        aliases=aliases,
    )


def shift_seq(array, k):
    return lax.ppermute(array, "seq", [(i, (i + k) % SEGMENTS) for i in range(SEGMENTS)])


def swap_cores(array):
    return lax.ppermute(array, "dp", [(i, i ^ 1) for i in range(X * Y * CORES)])


def dp_index(y, x, core):
    return (y % Y * X + x % X) * CORES + core


def shift_xy(array, along_x, along_y):
    pairs = [
        (dp_index(y, x, c), dp_index(y + along_y, x + along_x, c))
        for y in range(Y)
        for x in range(X)
        for c in range(CORES)
    ]
    return lax.ppermute(array, "dp", pairs)


def pack_kernel(parent_ref, count_ref, k_ref, v_ref, out_ref, sems):
    copies = []
    for head in range(KV_HEADS):
        for side, ref in enumerate((k_ref, v_ref)):
            copies.append(
                pltpu.make_async_copy(
                    ref.at[:, pl.ds(head * HEAD, HEAD)],
                    out_ref.at[pl.ds((side * KV_HEADS + head) * SEG_LEN, SEG_LEN), :],
                    sems.at[2 * head + side],
                )
            )
    for copy in copies:
        copy.start()
    row = lax.broadcasted_iota(jnp.int32, (LABEL_ROWS, HEAD), 0)
    labels = jnp.where(row < LABEL_ROWS // 2, parent_ref[0, 0], count_ref[0, 0])
    out_ref[PACKET_ROWS:, :] = labels.astype(F32).astype(BF16)
    for copy in copies:
        copy.wait()


def ring_packet(keys, values, parents, counts):
    return pl.pallas_call(
        pack_kernel,
        out_shape=jax.ShapeDtypeStruct((PACKET_ROWS + LABEL_ROWS, HEAD), BF16),
        in_specs=[SMEM_SPEC, SMEM_SPEC] + [pl.BlockSpec(memory_space=pltpu.HBM)] * 2,
        out_specs=VMEM_SPEC,
        scratch_shapes=[pltpu.SemaphoreType.DMA((2 * KV_HEADS,))],
        name="pack",
        compiler_params=pltpu.CompilerParams(vmem_limit_bytes=KERNEL_VMEM),
    )(
        parents,
        counts,
        pltpu.with_memory_space_constraint(keys, pltpu.HBM),
        pltpu.with_memory_space_constraint(values, pltpu.HBM),
    )


def finish_kernel(mine_ref, down_ref, up_ref, *out_refs):
    for head in range(KV_HEADS):
        rows = block_rows(head)
        total = mine_ref[rows, :] + (
            down_ref[rows, :].astype(F32) + up_ref[rows, :].astype(F32)
        )
        for ref in out_refs:
            ref[:, head * HEAD : (head + 1) * HEAD] = total.astype(BF16)


def finish(mine, down, up, copies):
    return on_core(
        finish_kernel,
        "finish",
        [jax.ShapeDtypeStruct((SEG_LEN, KV_COLS), BF16)] * copies,
        [mine, down, up],
    )


def taken(array, index, axis):
    return lax.dynamic_index_in_dim(array, index, axis, keepdims=False)


def places():
    dp = lax.axis_index("dp")
    core = lax.rem(dp, CORES)
    x = lax.rem(lax.div(dp, CORES), X)
    y = lax.div(dp, CORES * X)
    return y, x, core


def load_kernel(q_ref, g_ref, hidden_ref, *refs):
    head_refs, share_refs, (buffer, head_sems, share_sems) = refs[:4], refs[4:-3], refs[-3:]
    copies = [
        pltpu.make_async_copy(ref, buffer.at[i], head_sems.at[i])
        for i, ref in enumerate((q_ref, g_ref))
    ]
    x = places()[1]
    for k, ref in enumerate(share_refs):
        to = lax.rem(x + k, X)
        for y in range(Y):
            first = pl.multiple_of((y * X + to) * SHARE, SHARE)
            copies.append(
                pltpu.make_async_copy(
                    hidden_ref.at[:, pl.ds(first, SHARE)],
                    ref.at[:, pl.ds(y * SHARE, SHARE)],
                    share_sems.at[k * Y + y],
                )
            )
    for copy in copies:
        copy.start()
    for i in range(2):
        copies[i].wait()
        rows_ref, turned_ref = head_refs[2 * i : 2 * i + 2]
        for head in range(KV_HEADS * GROUP):
            part = slice(head * HEAD, (head + 1) * HEAD)
            block = buffer[i, :, part]
            rows_ref[part, :] = block
            turned_ref[:, part] = block.T
    for copy in copies[2:]:
        copy.wait()


def loaded(array_q, array_g, hidden):
    shapes = [(KV_HEADS * GROUP * SEG_LEN, HEAD), (HEAD, KV_HEADS * GROUP * SEG_LEN)] * 2
    shapes += [(SEG_LEN, Y * SHARE)] * X
    outs = pl.pallas_call(
        load_kernel,
        out_shape=[jax.ShapeDtypeStruct(shape, BF16) for shape in shapes],
        in_specs=[pl.BlockSpec(memory_space=pltpu.HBM)] * 3,
        out_specs=[VMEM_SPEC] * len(shapes),
        scratch_shapes=[
            pltpu.VMEM((2, SEG_LEN, Q_COLS), BF16),
            pltpu.SemaphoreType.DMA((2,)),
            pltpu.SemaphoreType.DMA((X * Y,)),
        ],
        name="load",
        compiler_params=pltpu.CompilerParams(vmem_limit_bytes=KERNEL_VMEM),
    )(*[pltpu.with_memory_space_constraint(a, pltpu.HBM) for a in (array_q, array_g, hidden)])
    return outs[:4], outs[4:]


def turn_kernel(*refs):
    part_refs, out_refs = refs[:X], refs[X:]
    here, _, core = places()
    for side, out_ref in enumerate(out_refs):
        for k in range(Y):
            of = lax.rem(here + k, Y) * CORES + lax.rem(core + side, CORES)
            first = pl.multiple_of(of * HEAD, HEAD)
            for i, ref in enumerate(part_refs):
                out_ref[k * HEAD : (k + 1) * HEAD, i * SEG_LEN : (i + 1) * SEG_LEN] = ref[
                    :, pl.ds(first, HEAD)
                ].T


def turned(parts):
    return on_core(
        turn_kernel,
        "turn",
        [jax.ShapeDtypeStruct((Y * HEAD, X * SEG_LEN), BF16)] * CORES,
        list(parts),
    )


def given_kernel(hidden_ref, *refs):
    token_refs, (out_ref,) = refs[:X], refs[X:]
    tokens = jnp.concatenate([ref[...] for ref in token_refs], axis=0)
    out_ref[...] = dot_nn(hidden_ref[...], tokens).astype(BF16)


def kept_kernel(hidden_ref, *refs):
    token_refs, got_ref, own_ref, out_refs = refs[:X], refs[X], refs[X + 1], refs[X + 2 :]
    tokens = jnp.concatenate([ref[...] for ref in token_refs], axis=0)
    total = dot_nn(hidden_ref[...], tokens) + got_ref[...].astype(F32)
    own_ref[...] = total[:HEAD]
    for k, ref in enumerate(out_refs):
        ref[...] = total[(k + 1) * HEAD : (k + 2) * HEAD].astype(BF16)


def all_grads(hidden, queries, keys, values, out_grad, parents, counts):
    barrier = lax.optimization_barrier
    own = ring_packet(
        keys.reshape(SEG_LEN, KV_COLS), values.reshape(SEG_LEN, KV_COLS), parents, counts
    )
    up, down = own, own
    below, above = {}, {}
    state, stats = (parents, counts), None
    for step in range(1, 5):
        if step == 2:
            heads, shares = loaded(
                queries.reshape(SEG_LEN, Q_COLS), out_grad.reshape(SEG_LEN, Q_COLS), hidden
            )
            label = shift_seq(own[PACKET_ROWS:], 4)
            up, down, label, *rest = barrier((up, down, label, *heads, *shares))
            heads, shares = rest[:4], rest[4:]
            hidden_parts = [
                shift_xy(share, k, 0) if k else share for k, share in enumerate(shares)
            ]
        if step == 3:
            state, stats = add_stats(heads, [own], [], state, None)
            up, down, state, stats = barrier((up, down, state, stats))
            stats, hidden_parts[1] = barrier((stats, hidden_parts[1]))
        if step == 4:
            state, stats = add_stats(
                heads, [below[1], below[2]], [(1, False), (2, False)], state, stats
            )
            up, down, state, stats = barrier((up, down, state, stats))
            farthest = [shift_seq(up[:KV_COLS], 1), shift_seq(down[KV_COLS:PACKET_ROWS], -1)]
            break
        down, up = shift_seq(down, -1), shift_seq(up, 1)
        above[step], below[step] = down, up
    state, stats = add_stats(
        heads,
        [below[3], label, above[3], above[2], above[1]],
        [(3, False), (4, True), (5, False), (6, False), (7, False)],
        state,
        stats,
    )
    stats, hidden_parts[2], hidden_parts[3] = barrier(
        (stats, hidden_parts[2], hidden_parts[3])
    )
    state, stats = add_stats(heads, farthest, [(4, False)], state, stats, last=True)

    dvs = {}
    acc, dk, dvs[4] = add_grads(heads, state, stats, farthest, [4], None, [BF16] * 2)
    down, up = shift_seq(dk, -1), None
    for step in range(3, 0, -1):
        starts = BF16 if step == 3 else F32
        acc, low, dvs[step], high, dvs[8 - step] = add_grads(
            heads,
            state,
            stats,
            [below[step], above[step]],
            [step, 8 - step],
            acc,
            [F32, starts, starts, F32],
        )
        acc, down = barrier((acc, down))
        down = shift_seq((low + down.astype(F32)).astype(BF16), -1)
        up = shift_seq(high if step == 3 else (high + up.astype(F32)).astype(BF16), 1)
    acc, *hidden_parts = barrier((acc, *turned(hidden_parts)))
    value_up = shift_seq(dvs[4], 1)
    dq, mine, dvs[0] = add_grads(heads, state, stats, [own], [0], acc, [F32] * 2, last=True)
    key_grad, near = finish(mine, down, up, 2)
    near, dvs[3], dvs[5] = barrier((near, dvs[3], dvs[5]))

    def value_step(step, value_up, value_down):
        value_up = (dvs[8 - step] + value_up.astype(F32)).astype(BF16)
        if value_down is None:
            value_down = dvs[step]
        else:
            value_down = (dvs[step] + value_down.astype(F32)).astype(BF16)
        return shift_seq(value_up, 1), shift_seq(value_down, -1)

    hidden_own, hidden_other = hidden_parts
    flops = 2 * X * SEG_LEN * Y * HEAD * KV_COLS
    tokens = [near] + [shift_xy(near, k, 0) for k in range(1, X)]
    value_up, value_down = value_step(3, value_up, None)
    given = on_core(
        given_kernel,
        "given",
        jax.ShapeDtypeStruct((Y * HEAD, KV_COLS), BF16),
        [hidden_other, *tokens],
        flops=flops,
    )
    given, value_up, value_down = barrier((given, value_up, value_down))
    value_up, value_down = value_step(2, value_up, value_down)
    kept, *low = on_core(
        kept_kernel,
        "kept",
        [jax.ShapeDtypeStruct((HEAD, KV_COLS), F32)]
        + [jax.ShapeDtypeStruct((HEAD, KV_COLS), BF16)] * (Y - 1),
        [hidden_own, *tokens, swap_cores(given)],
        flops=flops,
    )
    *low, dvs[1], dvs[7] = barrier((*low, dvs[1], dvs[7]))
    others = [shift_xy(low[k - 1], 0, k) for k in range(1, Y)]
    value_up, value_down = value_step(1, value_up, value_down)
    total = kept
    for other in others:
        total = total + other.astype(F32)
    total, value_up, value_down = barrier((total.astype(BF16), value_up, value_down))
    rows = lax.all_to_all(total, "seq", 0, 0, tiled=True)
    value_grad = finish(dvs[0], value_down, value_up, 1)[0]
    weight_grad = jnp.sum(rows.reshape(SEGMENTS, -1, KV_COLS).astype(F32), axis=0)
    return dq, key_grad, value_grad, weight_grad


def local(hidden_in, queries, keys, values, out_grad, parents, counts):
    dq, key_grad, value_grad, weight_grad = all_grads(
        hidden_in.reshape(SEG_LEN, -1), queries, keys, values, out_grad, parents, counts
    )
    return (
        dq.reshape(1, 1, SEG_LEN, Q_COLS),
        key_grad.reshape(1, 1, SEG_LEN, KV_COLS),
        value_grad.reshape(1, 1, SEG_LEN, KV_COLS),
        weight_grad,
    )


def solution(mesh):
    wide = P("dp", "seq", None, None)
    return jax.shard_map(
        local,
        mesh=mesh,
        in_specs=(wide, wide, wide, wide, wide, P("dp", "seq"), P("dp", "seq")),
        out_specs=(wide, wide, wide, P(("dp", "seq"), None)),
        check_vma=False,
    )
```

```python
import functools
import itertools
import math

import jax
import jax.numpy as jnp
from jax import lax
from jax.experimental import pallas as pl
from jax.experimental.pallas import tpu as pltpu
from jax.sharding import PartitionSpec as P

SEGMENTS = 8
SEG_LEN = 128
KV_HEADS = 4
GROUP = 8
HEAD = 128
KV_COLS = KV_HEADS * HEAD
Q_COLS = KV_HEADS * GROUP * HEAD
GROUP_COLS = GROUP * HEAD
STATS_HEADS = 2
KERNEL_VMEM = 16 << 20
SCALE = 1.0 / math.sqrt(HEAD)
SCALE_LOG2 = SCALE * math.log2(math.e)
NEG_FILL = -1e30
DEAD_LSE = 1e30
LABEL_ROWS = 16
PACKET_ROWS = 2 * KV_HEADS * SEG_LEN
STATE = 16
BF16 = jnp.bfloat16
F32 = jnp.float32

X, Y, CORES = 4, 4, 2
SHARE = CORES * HEAD


def dot_nt(a, b):
    return lax.dot_general(a, b, (((1,), (1,)), ((), ())), preferred_element_type=F32)


def dot_nn(a, b):
    return lax.dot_general(a, b, (((1,), (0,)), ((), ())), preferred_element_type=F32)


def dot_tn(a, b):
    return lax.dot_general(a, b, (((0,), (0,)), ((), ())), preferred_element_type=F32)


def key_bias(live):
    position = lax.broadcasted_iota(jnp.int32, (SEG_LEN, 1), 0)
    return jnp.where(position < live, 0.0, NEG_FILL).astype(F32)


def own_bias(live, heads):
    key_at = lax.broadcasted_iota(jnp.int32, (SEG_LEN, SEG_LEN), 0)
    query_at = lax.broadcasted_iota(jnp.int32, (SEG_LEN, SEG_LEN), 1)
    tile = jnp.where((key_at <= query_at) & (key_at < live), 0.0, NEG_FILL).astype(F32)
    return jnp.concatenate([tile] * heads, axis=1)


def block_rows(group):
    return slice(group * SEG_LEN, (group + 1) * SEG_LEN)


def key_value(refs, group):
    k_ref, v_ref = refs[0], refs[-1]
    first = KV_COLS if len(refs) == 1 else 0
    rows = block_rows(group)
    return k_ref[rows, :], v_ref[first + rows.start : first + rows.stop, :]


def group_cols(group):
    return slice(group * GROUP_COLS, (group + 1) * GROUP_COLS)


def scalar_of(rows):
    return jnp.max(rows.astype(F32)).astype(jnp.int32)


def state_value(ref, index):
    return scalar_of(ref[pl.ds(index, 1), :])


def set_state(ref, index, value):
    ref[pl.ds(index, 1), :] = jnp.full((1, HEAD), value, jnp.int32).astype(F32)


def stats_kernel(steps, first, last, *refs):
    if first:
        parent_ref, count_ref, q_ref, g_ref, packet_ref, out_ref, state_ref = refs
    else:
        q_ref, g_ref = refs[:2]
        packet_refs = refs[2:-4]
        in_ref, old_ref, out_ref, state_ref = refs[-4:]
    me = lax.axis_index("seq")

    def add_segment(packet, bias, start):
        width = STATS_HEADS * HEAD
        for group in range(KV_HEADS):
            k, v = key_value(packet, group)
            for chunk in range(GROUP_COLS // width):
                at = group * GROUP_COLS + chunk * width
                cols = slice(at, at + width)
                scores = dot_nn(k, q_ref[:, cols]) * SCALE_LOG2 + bias
                grad_probs = dot_nn(v, g_ref[:, cols])
                top = jnp.max(scores, axis=0, keepdims=True)
                if not start:
                    old_top = out_ref[0:1, cols]
                    top = jnp.maximum(top, old_top)
                weights = jnp.exp2(scores - top)
                total = jnp.sum(weights, axis=0, keepdims=True)
                mixed = jnp.sum(weights * grad_probs, axis=0, keepdims=True)
                if not start:
                    shrink = jnp.exp2(old_top - top)
                    total = total + out_ref[1:2, cols] * shrink
                    mixed = mixed + out_ref[2:3, cols] * shrink
                out_ref[0:1, cols] = top
                out_ref[1:2, cols] = total
                out_ref[2:3, cols] = mixed

    if first:
        live = count_ref[0, 0]
        state_ref[...] = jnp.zeros_like(state_ref)
        set_state(state_ref, 0, parent_ref[0, 0])
        set_state(state_ref, SEGMENTS, live)
        add_segment([packet_ref], own_bias(live, STATS_HEADS), True)
    else:
        state_ref[...] = old_ref[...]
        out_ref[...] = in_ref[...]
        if last:
            ((distance, _),) = steps
            live_there = state_value(old_ref, distance)

            @pl.when(live_there > 0)
            def _():
                add_segment(packet_refs, key_bias(live_there), False)

        else:
            current = state_value(old_ref, 0)
            for packet_ref, (distance, looked_up) in zip(packet_refs, steps):
                top_row = packet_ref.shape[0] - LABEL_ROWS
                hit = current == me - distance
                parent = scalar_of(packet_ref[top_row:, :][: LABEL_ROWS // 2])
                current = jnp.where(hit, parent, current)

                @pl.when(hit)
                def _():
                    live = scalar_of(packet_ref[top_row:, :][LABEL_ROWS // 2 :])
                    set_state(state_ref, distance, live)
                    if not looked_up:
                        add_segment([packet_ref], key_bias(live), False)

            set_state(state_ref, 0, current)

    if last:
        live = state_value(old_ref, SEGMENTS)
        position = lax.broadcasted_iota(jnp.int32, (1, Q_COLS), 1) & (SEG_LEN - 1)
        total = out_ref[1:2, :]
        row_delta = out_ref[2:3, :] / total
        lse = out_ref[0:1, :] + jnp.log2(total)
        out_ref[0:1, :] = jnp.where(position < live, lse, DEAD_LSE)
        out_ref[1:2, :] = row_delta


def grads_kernel(distances, first, last, *refs):
    state_ref, q_ref, qt_ref, g_ref, gt_ref, stats_ref = refs[:6]
    count = 2 if first else len(distances)
    arrays, rest = refs[6 : 6 + count], refs[6 + count :]
    packets = [arrays] if first else [[ref] for ref in arrays]
    if first:
        in_ref, (acc_ref, *out_refs) = None, rest
    else:
        in_ref, acc_ref, *out_refs = rest

    def run(segments):
        for group in range(KV_HEADS):
            blocks = [key_value(packet, group) for packet, _, _ in segments]
            k = jnp.concatenate([block[0] for block in blocks], axis=0)
            v = jnp.concatenate([block[1] for block in blocks], axis=0)
            bias = jnp.concatenate([bias for _, bias, _ in segments], axis=0)
            cols = group_cols(group)
            scores = dot_nn(k, qt_ref[:, cols]) * SCALE_LOG2 + bias
            probs = jnp.exp2(scores - stats_ref[0:1, cols])
            grad_probs = dot_nn(v, gt_ref[:, cols])
            grad_scores = (probs * (grad_probs - stats_ref[1:2, cols])).astype(BF16)
            dv = dot_nn(probs.astype(BF16), g_ref[cols, :])
            dk = dot_nn(grad_scores, q_ref[cols, :]) * SCALE
            dq = dot_nn(k.T, grad_scores)
            if in_ref is not None:
                dq = dq + in_ref[:, cols]
            if last:
                for head in range(GROUP):
                    part = slice(head * HEAD, (head + 1) * HEAD)
                    at = (group * GROUP + head) * HEAD
                    acc_ref[:, at : at + HEAD] = (dq[:, part] * SCALE).T.astype(BF16)
            else:
                acc_ref[:, cols] = dq
            for i, (_, _, (dk_ref, dv_ref)) in enumerate(segments):
                part = slice(i * SEG_LEN, (i + 1) * SEG_LEN)
                dk_ref[block_rows(group), :] = dk[part].astype(dk_ref.dtype)
                dv_ref[block_rows(group), :] = dv[part].astype(dv_ref.dtype)

    if last:
        bias = own_bias(state_value(state_ref, SEGMENTS), GROUP)
        run([(packets[0], bias, out_refs)])
        return
    lives = [state_value(state_ref, distance) for distance in distances]
    outs = [out_refs[2 * i : 2 * i + 2] for i in range(len(distances))]
    for chosen in itertools.product((False, True), repeat=len(distances)):
        taken_here = functools.reduce(
            jnp.logical_and,
            [(live > 0) if choice else (live == 0) for live, choice in zip(lives, chosen)],
        )

        @pl.when(taken_here)
        def _():
            for choice, pair in zip(chosen, outs):
                if not choice:
                    for ref in pair:
                        ref[...] = jnp.zeros_like(ref)
            if any(chosen):
                run(
                    [
                        (packet, key_bias(live), pair)
                        for packet, live, pair, choice in zip(packets, lives, outs, chosen)
                        if choice
                    ]
                )
            elif in_ref is None:
                acc_ref[...] = jnp.zeros_like(acc_ref)
            else:
                acc_ref[...] = in_ref[...]


SMEM_SPEC = pl.BlockSpec(memory_space=pltpu.SMEM)
VMEM_SPEC = pl.BlockSpec(memory_space=pltpu.VMEM)
STATS_SHAPE = jax.ShapeDtypeStruct((8, Q_COLS), F32)
STATE_SHAPE = jax.ShapeDtypeStruct((STATE, HEAD), F32)
BLOCK_FLOPS = 2 * SEG_LEN * SEG_LEN * HEAD * KV_HEADS * GROUP


def on_core(kernel, name, out_shape, operands, scalars=0, out_specs=None, flops=0, aliases=None):
    many = isinstance(out_shape, list)
    if out_specs is None:
        out_specs = [VMEM_SPEC] * len(out_shape) if many else VMEM_SPEC
    moved = sum(o.size * o.dtype.itemsize for o in operands)
    return pl.pallas_call(
        kernel,
        out_shape=out_shape,
        in_specs=[SMEM_SPEC] * scalars + [VMEM_SPEC] * (len(operands) - scalars),
        out_specs=out_specs,
        name=name,
        input_output_aliases=aliases or {},
        cost_estimate=pl.CostEstimate(flops=flops, bytes_accessed=moved, transcendentals=0),
        compiler_params=pltpu.CompilerParams(vmem_limit_bytes=KERNEL_VMEM),
    )(*operands)


def add_stats(heads, packets, steps, state, stats, last=False):
    _, qt, _, gt = heads
    first = stats is None
    if first:
        operands = [*state, qt, gt, *packets]
    else:
        operands = [qt, gt, *packets, stats, state]
    stats, state = on_core(
        functools.partial(stats_kernel, tuple(steps), first, last),
        "stats",
        [STATS_SHAPE, STATE_SHAPE],
        operands,
        scalars=len(state) if first else 0,
        flops=4 * BLOCK_FLOPS * len(packets),
    )
    return state, stats


def add_grads(heads, state, stats, packets, distances, acc, dtypes, last=False):
    first = acc is None
    operands = [state, *heads, stats, *packets]
    aliases = {}
    if not first:
        if not last:
            aliases = {len(operands): 0}
        operands.append(acc)
    if last:
        out_shapes = [jax.ShapeDtypeStruct((SEG_LEN, Q_COLS), BF16)]
    else:
        out_shapes = [jax.ShapeDtypeStruct((HEAD, Q_COLS), F32)]
    out_shapes += [jax.ShapeDtypeStruct((KV_COLS, HEAD), dtype) for dtype in dtypes]
    return on_core(
        functools.partial(grads_kernel, tuple(distances), first, last),
        "grads",
        out_shapes,
        operands,
        flops=10 * BLOCK_FLOPS * len(distances),
        aliases=aliases,
    )


def shift_seq(array, k):
    return lax.ppermute(array, "seq", [(i, (i + k) % SEGMENTS) for i in range(SEGMENTS)])


def swap_cores(array):
    return lax.ppermute(array, "dp", [(i, i ^ 1) for i in range(X * Y * CORES)])


def dp_index(y, x, core):
    return (y % Y * X + x % X) * CORES + core


def shift_xy(array, along_x, along_y):
    pairs = [
        (dp_index(y, x, c), dp_index(y + along_y, x + along_x, c))
        for y in range(Y)
        for x in range(X)
        for c in range(CORES)
    ]
    return lax.ppermute(array, "dp", pairs)


def pack_kernel(parent_ref, count_ref, k_ref, v_ref, out_ref, sems):
    copies = []
    for head in range(KV_HEADS):
        for side, ref in enumerate((k_ref, v_ref)):
            copies.append(
                pltpu.make_async_copy(
                    ref.at[:, pl.ds(head * HEAD, HEAD)],
                    out_ref.at[pl.ds((side * KV_HEADS + head) * SEG_LEN, SEG_LEN), :],
                    sems.at[2 * head + side],
                )
            )
    for copy in copies:
        copy.start()
    row = lax.broadcasted_iota(jnp.int32, (LABEL_ROWS, HEAD), 0)
    labels = jnp.where(row < LABEL_ROWS // 2, parent_ref[0, 0], count_ref[0, 0])
    out_ref[PACKET_ROWS:, :] = labels.astype(F32).astype(BF16)
    for copy in copies:
        copy.wait()


def ring_packet(keys, values, parents, counts):
    return pl.pallas_call(
        pack_kernel,
        out_shape=jax.ShapeDtypeStruct((PACKET_ROWS + LABEL_ROWS, HEAD), BF16),
        in_specs=[SMEM_SPEC, SMEM_SPEC] + [pl.BlockSpec(memory_space=pltpu.HBM)] * 2,
        out_specs=VMEM_SPEC,
        scratch_shapes=[pltpu.SemaphoreType.DMA((2 * KV_HEADS,))],
        name="pack",
        compiler_params=pltpu.CompilerParams(vmem_limit_bytes=KERNEL_VMEM),
    )(
        parents,
        counts,
        pltpu.with_memory_space_constraint(keys, pltpu.HBM),
        pltpu.with_memory_space_constraint(values, pltpu.HBM),
    )


def finish_kernel(mine_ref, down_ref, up_ref, *out_refs):
    for head in range(KV_HEADS):
        rows = block_rows(head)
        total = mine_ref[rows, :] + (
            down_ref[rows, :].astype(F32) + up_ref[rows, :].astype(F32)
        )
        for ref in out_refs:
            ref[:, head * HEAD : (head + 1) * HEAD] = total.astype(BF16)


def finish(mine, down, up, copies):
    return on_core(
        finish_kernel,
        "finish",
        [jax.ShapeDtypeStruct((SEG_LEN, KV_COLS), BF16)] * copies,
        [mine, down, up],
    )


def taken(array, index, axis):
    return lax.dynamic_index_in_dim(array, index, axis, keepdims=False)


def places():
    dp = lax.axis_index("dp")
    core = lax.rem(dp, CORES)
    x = lax.rem(lax.div(dp, CORES), X)
    y = lax.div(dp, CORES * X)
    return y, x, core


def load_kernel(q_ref, g_ref, hidden_ref, *refs):
    head_refs, share_refs, (buffer, head_sems, share_sems) = refs[:4], refs[4:-3], refs[-3:]
    copies = [
        pltpu.make_async_copy(ref, buffer.at[i], head_sems.at[i])
        for i, ref in enumerate((q_ref, g_ref))
    ]
    x = places()[1]
    for k, ref in enumerate(share_refs):
        to = lax.rem(x + k, X)
        for y in range(Y):
            first = pl.multiple_of((y * X + to) * SHARE, SHARE)
            copies.append(
                pltpu.make_async_copy(
                    hidden_ref.at[:, pl.ds(first, SHARE)],
                    ref.at[:, pl.ds(y * SHARE, SHARE)],
                    share_sems.at[k * Y + y],
                )
            )
    for copy in copies:
        copy.start()
    for i in range(2):
        copies[i].wait()
        rows_ref, turned_ref = head_refs[2 * i : 2 * i + 2]
        for head in range(KV_HEADS * GROUP):
            part = slice(head * HEAD, (head + 1) * HEAD)
            block = buffer[i, :, part]
            rows_ref[part, :] = block
            turned_ref[:, part] = block.T
    for copy in copies[2:]:
        copy.wait()


def loaded(array_q, array_g, hidden):
    shapes = [(KV_HEADS * GROUP * SEG_LEN, HEAD), (HEAD, KV_HEADS * GROUP * SEG_LEN)] * 2
    shapes += [(SEG_LEN, Y * SHARE)] * X
    outs = pl.pallas_call(
        load_kernel,
        out_shape=[jax.ShapeDtypeStruct(shape, BF16) for shape in shapes],
        in_specs=[pl.BlockSpec(memory_space=pltpu.HBM)] * 3,
        out_specs=[VMEM_SPEC] * len(shapes),
        scratch_shapes=[
            pltpu.VMEM((2, SEG_LEN, Q_COLS), BF16),
            pltpu.SemaphoreType.DMA((2,)),
            pltpu.SemaphoreType.DMA((X * Y,)),
        ],
        name="load",
        compiler_params=pltpu.CompilerParams(vmem_limit_bytes=KERNEL_VMEM),
    )(*[pltpu.with_memory_space_constraint(a, pltpu.HBM) for a in (array_q, array_g, hidden)])
    return outs[:4], outs[4:]


def turn_kernel(*refs):
    part_refs, out_refs = refs[:X], refs[X:]
    here, _, core = places()
    for side, out_ref in enumerate(out_refs):
        for k in range(Y):
            of = lax.rem(here + k, Y) * CORES + lax.rem(core + side, CORES)
            first = pl.multiple_of(of * HEAD, HEAD)
            for i, ref in enumerate(part_refs):
                out_ref[k * HEAD : (k + 1) * HEAD, i * SEG_LEN : (i + 1) * SEG_LEN] = ref[
                    :, pl.ds(first, HEAD)
                ].T


def turned(parts):
    return on_core(
        turn_kernel,
        "turn",
        [jax.ShapeDtypeStruct((Y * HEAD, X * SEG_LEN), BF16)] * CORES,
        list(parts),
    )


def given_kernel(hidden_ref, *refs):
    token_refs, (out_ref,) = refs[:X], refs[X:]
    tokens = jnp.concatenate([ref[...] for ref in token_refs], axis=0)
    out_ref[...] = dot_nn(hidden_ref[...], tokens).astype(BF16)


def kept_kernel(hidden_ref, *refs):
    token_refs, got_ref, own_ref, out_refs = refs[:X], refs[X], refs[X + 1], refs[X + 2 :]
    tokens = jnp.concatenate([ref[...] for ref in token_refs], axis=0)
    total = dot_nn(hidden_ref[...], tokens) + got_ref[...].astype(F32)
    own_ref[...] = total[:HEAD]
    for k, ref in enumerate(out_refs):
        ref[...] = total[(k + 1) * HEAD : (k + 2) * HEAD].astype(BF16)


def all_grads(hidden, queries, keys, values, out_grad, parents, counts):
    barrier = lax.optimization_barrier
    own = ring_packet(
        keys.reshape(SEG_LEN, KV_COLS), values.reshape(SEG_LEN, KV_COLS), parents, counts
    )
    up, down = own, own
    below, above = {}, {}
    state, stats = (parents, counts), None
    for step in range(1, 5):
        if step == 2:
            heads, shares = loaded(
                queries.reshape(SEG_LEN, Q_COLS), out_grad.reshape(SEG_LEN, Q_COLS), hidden
            )
            label = shift_seq(own[PACKET_ROWS:], 4)
            up, down, label, *rest = barrier((up, down, label, *heads, *shares))
            heads, shares = rest[:4], rest[4:]
            hidden_parts = [
                shift_xy(share, k, 0) if k else share for k, share in enumerate(shares)
            ]
        if step == 3:
            state, stats = add_stats(heads, [own], [], state, None)
            up, down, state, stats = barrier((up, down, state, stats))
            stats, hidden_parts[1] = barrier((stats, hidden_parts[1]))
        if step == 4:
            state, stats = add_stats(
                heads, [below[1], below[2]], [(1, False), (2, False)], state, stats
            )
            up, down, state, stats = barrier((up, down, state, stats))
            farthest = [shift_seq(up[:KV_COLS], 1), shift_seq(down[KV_COLS:PACKET_ROWS], -1)]
            break
        down, up = shift_seq(down, -1), shift_seq(up, 1)
        above[step], below[step] = down, up
    state, stats = add_stats(
        heads,
        [below[3], label, above[3], above[2], above[1]],
        [(3, False), (4, True), (5, False), (6, False), (7, False)],
        state,
        stats,
    )
    stats, hidden_parts[2], hidden_parts[3] = barrier(
        (stats, hidden_parts[2], hidden_parts[3])
    )
    state, stats = add_stats(heads, farthest, [(4, False)], state, stats, last=True)

    dvs = {}
    acc, dk, dvs[4] = add_grads(heads, state, stats, farthest, [4], None, [BF16] * 2)
    down, up = shift_seq(dk, -1), None
    for step in range(3, 0, -1):
        starts = BF16 if step == 3 else F32
        acc, low, dvs[step], high, dvs[8 - step] = add_grads(
            heads,
            state,
            stats,
            [below[step], above[step]],
            [step, 8 - step],
            acc,
            [F32, starts, starts, F32],
        )
        if up is None:
            acc, down, low, up = barrier((acc, down, low, high))
        else:
            acc, down, up, low, high = barrier((acc, down, up, low, high))
            up = (high + up.astype(F32)).astype(BF16)
        down, up = shift_seq((low + down.astype(F32)).astype(BF16), -1), shift_seq(up, 1)
    acc, *hidden_parts = barrier((acc, *turned(hidden_parts)))
    value_up = shift_seq(dvs[4], 1)
    dq, mine, dvs[0] = add_grads(heads, state, stats, [own], [0], acc, [F32] * 2, last=True)
    key_grad, near = finish(mine, down, up, 2)
    near, value_up, dvs[3], dvs[5] = barrier((near, value_up, dvs[3], dvs[5]))

    def value_step(step, value_up, value_down):
        value_up = (dvs[8 - step] + value_up.astype(F32)).astype(BF16)
        if value_down is None:
            value_down = dvs[step]
        else:
            value_down = (dvs[step] + value_down.astype(F32)).astype(BF16)
        return shift_seq(value_up, 1), shift_seq(value_down, -1)

    hidden_own, hidden_other = hidden_parts
    flops = 2 * X * SEG_LEN * Y * HEAD * KV_COLS
    tokens = [near] + [shift_xy(near, k, 0) for k in range(1, X)]
    value_up, value_down = value_step(3, value_up, None)
    given = on_core(
        given_kernel,
        "given",
        jax.ShapeDtypeStruct((Y * HEAD, KV_COLS), BF16),
        [hidden_other, *tokens],
        flops=flops,
    )
    kept, *low = on_core(
        kept_kernel,
        "kept",
        [jax.ShapeDtypeStruct((HEAD, KV_COLS), F32)]
        + [jax.ShapeDtypeStruct((HEAD, KV_COLS), BF16)] * (Y - 1),
        [hidden_own, *tokens, swap_cores(given)],
        flops=flops,
    )
    *low, dvs[2], dvs[6] = barrier((*low, dvs[2], dvs[6]))
    others = [shift_xy(low[k - 1], 0, k) for k in range(1, Y)]
    value_up, value_down = value_step(2, value_up, value_down)
    total = kept
    for other in others:
        total = total + other.astype(F32)
    total, dvs[1], dvs[7] = barrier((total.astype(BF16), dvs[1], dvs[7]))
    value_up, value_down = value_step(1, value_up, value_down)
    rows = lax.all_to_all(total, "seq", 0, 0, tiled=True)
    value_grad = finish(dvs[0], value_down, value_up, 1)[0]
    weight_grad = jnp.sum(rows.reshape(SEGMENTS, -1, KV_COLS).astype(F32), axis=0)
    return dq, key_grad, value_grad, weight_grad


def local(hidden_in, queries, keys, values, out_grad, parents, counts):
    dq, key_grad, value_grad, weight_grad = all_grads(
        hidden_in.reshape(SEG_LEN, -1), queries, keys, values, out_grad, parents, counts
    )
    return (
        dq.reshape(1, 1, SEG_LEN, Q_COLS),
        key_grad.reshape(1, 1, SEG_LEN, KV_COLS),
        value_grad.reshape(1, 1, SEG_LEN, KV_COLS),
        weight_grad,
    )


def solution(mesh):
    wide = P("dp", "seq", None, None)
    return jax.shard_map(
        local,
        mesh=mesh,
        in_specs=(wide, wide, wide, wide, wide, P("dp", "seq"), P("dp", "seq")),
        out_specs=(wide, wide, wide, P(("dp", "seq"), None)),
        check_vma=False,
    )
```

```python
import functools
import itertools
import math

import jax
import jax.numpy as jnp
from jax import lax
from jax.experimental import pallas as pl
from jax.experimental.pallas import tpu as pltpu
from jax.sharding import PartitionSpec as P

SEGMENTS = 8
SEG_LEN = 128
KV_HEADS = 4
GROUP = 8
HEAD = 128
KV_COLS = KV_HEADS * HEAD
Q_COLS = KV_HEADS * GROUP * HEAD
GROUP_COLS = GROUP * HEAD
STATS_HEADS = 2
KERNEL_VMEM = 16 << 20
SCALE = 1.0 / math.sqrt(HEAD)
SCALE_LOG2 = SCALE * math.log2(math.e)
NEG_FILL = -1e30
DEAD_LSE = 1e30
LABEL_ROWS = 16
PACKET_ROWS = 2 * KV_HEADS * SEG_LEN
STATE = 16
BF16 = jnp.bfloat16
F32 = jnp.float32

X, Y, CORES = 4, 4, 2
SHARE = CORES * HEAD


def dot_nt(a, b):
    return lax.dot_general(a, b, (((1,), (1,)), ((), ())), preferred_element_type=F32)


def dot_nn(a, b):
    return lax.dot_general(a, b, (((1,), (0,)), ((), ())), preferred_element_type=F32)


def dot_tn(a, b):
    return lax.dot_general(a, b, (((0,), (0,)), ((), ())), preferred_element_type=F32)


def key_bias(live):
    position = lax.broadcasted_iota(jnp.int32, (SEG_LEN, 1), 0)
    return jnp.where(position < live, 0.0, NEG_FILL).astype(F32)


def own_bias(live, heads):
    key_at = lax.broadcasted_iota(jnp.int32, (SEG_LEN, SEG_LEN), 0)
    query_at = lax.broadcasted_iota(jnp.int32, (SEG_LEN, SEG_LEN), 1)
    tile = jnp.where((key_at <= query_at) & (key_at < live), 0.0, NEG_FILL).astype(F32)
    return jnp.concatenate([tile] * heads, axis=1)


def block_rows(group):
    return slice(group * SEG_LEN, (group + 1) * SEG_LEN)


def key_value(refs, group):
    k_ref, v_ref = refs[0], refs[-1]
    first = KV_COLS if len(refs) == 1 else 0
    rows = block_rows(group)
    return k_ref[rows, :], v_ref[first + rows.start : first + rows.stop, :]


def group_cols(group):
    return slice(group * GROUP_COLS, (group + 1) * GROUP_COLS)


def scalar_of(rows):
    return jnp.max(rows.astype(F32)).astype(jnp.int32)


def state_value(ref, index):
    return scalar_of(ref[pl.ds(index, 1), :])


def set_state(ref, index, value):
    ref[pl.ds(index, 1), :] = jnp.full((1, HEAD), value, jnp.int32).astype(F32)


def stats_kernel(steps, first, last, *refs):
    if first:
        parent_ref, count_ref, q_ref, g_ref, packet_ref, out_ref, state_ref = refs
    else:
        q_ref, g_ref = refs[:2]
        packet_refs = refs[2:-4]
        in_ref, old_ref, out_ref, state_ref = refs[-4:]
    me = lax.axis_index("seq")

    def add_segment(packet, bias, start):
        width = STATS_HEADS * HEAD
        for group in range(KV_HEADS):
            k, v = key_value(packet, group)
            for chunk in range(GROUP_COLS // width):
                at = group * GROUP_COLS + chunk * width
                cols = slice(at, at + width)
                scores = dot_nn(k, q_ref[:, cols]) * SCALE_LOG2 + bias
                grad_probs = dot_nn(v, g_ref[:, cols])
                top = jnp.max(scores, axis=0, keepdims=True)
                if not start:
                    old_top = out_ref[0:1, cols]
                    top = jnp.maximum(top, old_top)
                weights = jnp.exp2(scores - top)
                total = jnp.sum(weights, axis=0, keepdims=True)
                mixed = jnp.sum(weights * grad_probs, axis=0, keepdims=True)
                if not start:
                    shrink = jnp.exp2(old_top - top)
                    total = total + out_ref[1:2, cols] * shrink
                    mixed = mixed + out_ref[2:3, cols] * shrink
                out_ref[0:1, cols] = top
                out_ref[1:2, cols] = total
                out_ref[2:3, cols] = mixed

    if first:
        live = count_ref[0, 0]
        state_ref[...] = jnp.zeros_like(state_ref)
        set_state(state_ref, 0, parent_ref[0, 0])
        set_state(state_ref, SEGMENTS, live)
        add_segment([packet_ref], own_bias(live, STATS_HEADS), True)
    else:
        state_ref[...] = old_ref[...]
        out_ref[...] = in_ref[...]
        if last:
            ((distance, _),) = steps
            live_there = state_value(old_ref, distance)

            @pl.when(live_there > 0)
            def _():
                add_segment(packet_refs, key_bias(live_there), False)

        else:
            current = state_value(old_ref, 0)
            for packet_ref, (distance, looked_up) in zip(packet_refs, steps):
                top_row = packet_ref.shape[0] - LABEL_ROWS
                hit = current == me - distance
                parent = scalar_of(packet_ref[top_row:, :][: LABEL_ROWS // 2])
                current = jnp.where(hit, parent, current)

                @pl.when(hit)
                def _():
                    live = scalar_of(packet_ref[top_row:, :][LABEL_ROWS // 2 :])
                    set_state(state_ref, distance, live)
                    if not looked_up:
                        add_segment([packet_ref], key_bias(live), False)

            set_state(state_ref, 0, current)

    if last:
        live = state_value(old_ref, SEGMENTS)
        position = lax.broadcasted_iota(jnp.int32, (1, Q_COLS), 1) & (SEG_LEN - 1)
        total = out_ref[1:2, :]
        row_delta = out_ref[2:3, :] / total
        lse = out_ref[0:1, :] + jnp.log2(total)
        out_ref[0:1, :] = jnp.where(position < live, lse, DEAD_LSE)
        out_ref[1:2, :] = row_delta


def grads_kernel(distances, first, last, *refs):
    state_ref, q_ref, qt_ref, g_ref, gt_ref, stats_ref = refs[:6]
    count = 2 if first else len(distances)
    arrays, rest = refs[6 : 6 + count], refs[6 + count :]
    packets = [arrays] if first else [[ref] for ref in arrays]
    if first:
        in_ref, (acc_ref, *out_refs) = None, rest
    else:
        in_ref, acc_ref, *out_refs = rest

    def run(segments):
        for group in range(KV_HEADS):
            blocks = [key_value(packet, group) for packet, _, _ in segments]
            k = jnp.concatenate([block[0] for block in blocks], axis=0)
            v = jnp.concatenate([block[1] for block in blocks], axis=0)
            bias = jnp.concatenate([bias for _, bias, _ in segments], axis=0)
            cols = group_cols(group)
            scores = dot_nn(k, qt_ref[:, cols]) * SCALE_LOG2 + bias
            probs = jnp.exp2(scores - stats_ref[0:1, cols])
            grad_probs = dot_nn(v, gt_ref[:, cols])
            grad_scores = (probs * (grad_probs - stats_ref[1:2, cols])).astype(BF16)
            dv = dot_nn(probs.astype(BF16), g_ref[cols, :])
            dk = dot_nn(grad_scores, q_ref[cols, :]) * SCALE
            dq = dot_nn(k.T, grad_scores)
            if in_ref is not None:
                dq = dq + in_ref[:, cols]
            if last:
                for head in range(GROUP):
                    part = slice(head * HEAD, (head + 1) * HEAD)
                    at = (group * GROUP + head) * HEAD
                    acc_ref[:, at : at + HEAD] = (dq[:, part] * SCALE).T.astype(BF16)
            else:
                acc_ref[:, cols] = dq
            for i, (_, _, (dk_ref, dv_ref)) in enumerate(segments):
                part = slice(i * SEG_LEN, (i + 1) * SEG_LEN)
                dk_ref[block_rows(group), :] = dk[part].astype(dk_ref.dtype)
                dv_ref[block_rows(group), :] = dv[part].astype(dv_ref.dtype)

    if last:
        bias = own_bias(state_value(state_ref, SEGMENTS), GROUP)
        run([(packets[0], bias, out_refs)])
        return
    lives = [state_value(state_ref, distance) for distance in distances]
    outs = [out_refs[2 * i : 2 * i + 2] for i in range(len(distances))]
    for chosen in itertools.product((False, True), repeat=len(distances)):
        taken_here = functools.reduce(
            jnp.logical_and,
            [(live > 0) if choice else (live == 0) for live, choice in zip(lives, chosen)],
        )

        @pl.when(taken_here)
        def _():
            for choice, pair in zip(chosen, outs):
                if not choice:
                    for ref in pair:
                        ref[...] = jnp.zeros_like(ref)
            if any(chosen):
                run(
                    [
                        (packet, key_bias(live), pair)
                        for packet, live, pair, choice in zip(packets, lives, outs, chosen)
                        if choice
                    ]
                )
            elif in_ref is None:
                acc_ref[...] = jnp.zeros_like(acc_ref)
            else:
                acc_ref[...] = in_ref[...]


SMEM_SPEC = pl.BlockSpec(memory_space=pltpu.SMEM)
VMEM_SPEC = pl.BlockSpec(memory_space=pltpu.VMEM)
STATS_SHAPE = jax.ShapeDtypeStruct((8, Q_COLS), F32)
STATE_SHAPE = jax.ShapeDtypeStruct((STATE, HEAD), F32)
BLOCK_FLOPS = 2 * SEG_LEN * SEG_LEN * HEAD * KV_HEADS * GROUP


def on_core(kernel, name, out_shape, operands, scalars=0, out_specs=None, flops=0, aliases=None):
    many = isinstance(out_shape, list)
    if out_specs is None:
        out_specs = [VMEM_SPEC] * len(out_shape) if many else VMEM_SPEC
    moved = sum(o.size * o.dtype.itemsize for o in operands)
    return pl.pallas_call(
        kernel,
        out_shape=out_shape,
        in_specs=[SMEM_SPEC] * scalars + [VMEM_SPEC] * (len(operands) - scalars),
        out_specs=out_specs,
        name=name,
        input_output_aliases=aliases or {},
        cost_estimate=pl.CostEstimate(flops=flops, bytes_accessed=moved, transcendentals=0),
        compiler_params=pltpu.CompilerParams(vmem_limit_bytes=KERNEL_VMEM),
    )(*operands)


def add_stats(heads, packets, steps, state, stats, last=False):
    _, qt, _, gt = heads
    first = stats is None
    if first:
        operands = [*state, qt, gt, *packets]
    else:
        operands = [qt, gt, *packets, stats, state]
    stats, state = on_core(
        functools.partial(stats_kernel, tuple(steps), first, last),
        "stats",
        [STATS_SHAPE, STATE_SHAPE],
        operands,
        scalars=len(state) if first else 0,
        flops=4 * BLOCK_FLOPS * len(packets),
    )
    return state, stats


def add_grads(heads, state, stats, packets, distances, acc, dtypes, last=False):
    first = acc is None
    operands = [state, *heads, stats, *packets]
    aliases = {}
    if not first:
        if not last:
            aliases = {len(operands): 0}
        operands.append(acc)
    if last:
        out_shapes = [jax.ShapeDtypeStruct((SEG_LEN, Q_COLS), BF16)]
    else:
        out_shapes = [jax.ShapeDtypeStruct((HEAD, Q_COLS), F32)]
    out_shapes += [jax.ShapeDtypeStruct((KV_COLS, HEAD), dtype) for dtype in dtypes]
    return on_core(
        functools.partial(grads_kernel, tuple(distances), first, last),
        "grads",
        out_shapes,
        operands,
        flops=10 * BLOCK_FLOPS * len(distances),
        aliases=aliases,
    )


def shift_seq(array, k):
    return lax.ppermute(array, "seq", [(i, (i + k) % SEGMENTS) for i in range(SEGMENTS)])


def swap_cores(array):
    return lax.ppermute(array, "dp", [(i, i ^ 1) for i in range(X * Y * CORES)])


def dp_index(y, x, core):
    return (y % Y * X + x % X) * CORES + core


def shift_xy(array, along_x, along_y):
    pairs = [
        (dp_index(y, x, c), dp_index(y + along_y, x + along_x, c))
        for y in range(Y)
        for x in range(X)
        for c in range(CORES)
    ]
    return lax.ppermute(array, "dp", pairs)


def pack_kernel(parent_ref, count_ref, k_ref, v_ref, out_ref, sems):
    copies = []
    for head in range(KV_HEADS):
        for side, ref in enumerate((k_ref, v_ref)):
            copies.append(
                pltpu.make_async_copy(
                    ref.at[:, pl.ds(head * HEAD, HEAD)],
                    out_ref.at[pl.ds((side * KV_HEADS + head) * SEG_LEN, SEG_LEN), :],
                    sems.at[2 * head + side],
                )
            )
    for copy in copies:
        copy.start()
    row = lax.broadcasted_iota(jnp.int32, (LABEL_ROWS, HEAD), 0)
    labels = jnp.where(row < LABEL_ROWS // 2, parent_ref[0, 0], count_ref[0, 0])
    out_ref[PACKET_ROWS:, :] = labels.astype(F32).astype(BF16)
    for copy in copies:
        copy.wait()


def ring_packet(keys, values, parents, counts):
    return pl.pallas_call(
        pack_kernel,
        out_shape=jax.ShapeDtypeStruct((PACKET_ROWS + LABEL_ROWS, HEAD), BF16),
        in_specs=[SMEM_SPEC, SMEM_SPEC] + [pl.BlockSpec(memory_space=pltpu.HBM)] * 2,
        out_specs=VMEM_SPEC,
        scratch_shapes=[pltpu.SemaphoreType.DMA((2 * KV_HEADS,))],
        name="pack",
        compiler_params=pltpu.CompilerParams(vmem_limit_bytes=KERNEL_VMEM),
    )(
        parents,
        counts,
        pltpu.with_memory_space_constraint(keys, pltpu.HBM),
        pltpu.with_memory_space_constraint(values, pltpu.HBM),
    )


def finish_kernel(mine_ref, down_ref, up_ref, *out_refs):
    for head in range(KV_HEADS):
        rows = block_rows(head)
        total = mine_ref[rows, :] + (
            down_ref[rows, :].astype(F32) + up_ref[rows, :].astype(F32)
        )
        for ref in out_refs:
            ref[:, head * HEAD : (head + 1) * HEAD] = total.astype(BF16)


def finish(mine, down, up, copies):
    return on_core(
        finish_kernel,
        "finish",
        [jax.ShapeDtypeStruct((SEG_LEN, KV_COLS), BF16)] * copies,
        [mine, down, up],
    )


def taken(array, index, axis):
    return lax.dynamic_index_in_dim(array, index, axis, keepdims=False)


def places():
    dp = lax.axis_index("dp")
    core = lax.rem(dp, CORES)
    x = lax.rem(lax.div(dp, CORES), X)
    y = lax.div(dp, CORES * X)
    return y, x, core


def load_kernel(q_ref, g_ref, hidden_ref, *refs):
    head_refs, share_refs, (buffer, head_sems, share_sems) = refs[:4], refs[4:-3], refs[-3:]
    copies = [
        pltpu.make_async_copy(ref, buffer.at[i], head_sems.at[i])
        for i, ref in enumerate((q_ref, g_ref))
    ]
    x = places()[1]
    for k, ref in enumerate(share_refs):
        to = lax.rem(x + k, X)
        for y in range(Y):
            first = pl.multiple_of((y * X + to) * SHARE, SHARE)
            copies.append(
                pltpu.make_async_copy(
                    hidden_ref.at[:, pl.ds(first, SHARE)],
                    ref.at[:, pl.ds(y * SHARE, SHARE)],
                    share_sems.at[k * Y + y],
                )
            )
    for copy in copies:
        copy.start()
    for i in range(2):
        copies[i].wait()
        rows_ref, turned_ref = head_refs[2 * i : 2 * i + 2]
        for head in range(KV_HEADS * GROUP):
            part = slice(head * HEAD, (head + 1) * HEAD)
            block = buffer[i, :, part]
            rows_ref[part, :] = block
            turned_ref[:, part] = block.T
    for copy in copies[2:]:
        copy.wait()


def loaded(array_q, array_g, hidden):
    shapes = [(KV_HEADS * GROUP * SEG_LEN, HEAD), (HEAD, KV_HEADS * GROUP * SEG_LEN)] * 2
    shapes += [(SEG_LEN, Y * SHARE)] * X
    outs = pl.pallas_call(
        load_kernel,
        out_shape=[jax.ShapeDtypeStruct(shape, BF16) for shape in shapes],
        in_specs=[pl.BlockSpec(memory_space=pltpu.HBM)] * 3,
        out_specs=[VMEM_SPEC] * len(shapes),
        scratch_shapes=[
            pltpu.VMEM((2, SEG_LEN, Q_COLS), BF16),
            pltpu.SemaphoreType.DMA((2,)),
            pltpu.SemaphoreType.DMA((X * Y,)),
        ],
        name="load",
        compiler_params=pltpu.CompilerParams(vmem_limit_bytes=KERNEL_VMEM),
    )(*[pltpu.with_memory_space_constraint(a, pltpu.HBM) for a in (array_q, array_g, hidden)])
    return outs[:4], outs[4:]


def turn_kernel(*refs):
    part_refs, out_refs = refs[:X], refs[X:]
    core = places()[2]
    for side, out_ref in enumerate(out_refs):
        for k in range(Y):
            of = k * CORES + lax.rem(core + side, CORES)
            first = pl.multiple_of(of * HEAD, HEAD)
            for i, ref in enumerate(part_refs):
                out_ref[k * HEAD : (k + 1) * HEAD, i * SEG_LEN : (i + 1) * SEG_LEN] = ref[
                    :, pl.ds(first, HEAD)
                ].T


def turned(parts):
    return on_core(
        turn_kernel,
        "turn",
        [jax.ShapeDtypeStruct((Y * HEAD, X * SEG_LEN), BF16)] * CORES,
        list(parts),
    )


def given_kernel(hidden_ref, *refs):
    token_refs, (out_ref,) = refs[:X], refs[X:]
    tokens = jnp.concatenate([ref[...] for ref in token_refs], axis=0)
    out_ref[...] = dot_nn(hidden_ref[...], tokens).astype(BF16)


def kept_kernel(hidden_ref, *refs):
    token_refs, (got_ref, out_ref) = refs[:X], refs[X:]
    tokens = jnp.concatenate([ref[...] for ref in token_refs], axis=0)
    total = dot_nn(hidden_ref[...], tokens) + got_ref[...].astype(F32)
    out_ref[...] = total.astype(BF16)


def all_grads(hidden, queries, keys, values, out_grad, parents, counts):
    barrier = lax.optimization_barrier
    own = ring_packet(
        keys.reshape(SEG_LEN, KV_COLS), values.reshape(SEG_LEN, KV_COLS), parents, counts
    )
    up, down = own, own
    below, above = {}, {}
    state, stats = (parents, counts), None
    for step in range(1, 5):
        if step == 2:
            heads, shares = loaded(
                queries.reshape(SEG_LEN, Q_COLS), out_grad.reshape(SEG_LEN, Q_COLS), hidden
            )
            label = shift_seq(own[PACKET_ROWS:], 4)
            up, down, label, *rest = barrier((up, down, label, *heads, *shares))
            heads, shares = rest[:4], rest[4:]
            hidden_parts = [
                shift_xy(share, k, 0) if k else share for k, share in enumerate(shares)
            ]
        if step == 3:
            state, stats = add_stats(heads, [own], [], state, None)
            up, down, state, stats = barrier((up, down, state, stats))
            stats, hidden_parts[1] = barrier((stats, hidden_parts[1]))
        if step == 4:
            state, stats = add_stats(
                heads, [below[1], below[2]], [(1, False), (2, False)], state, stats
            )
            up, down, state, stats = barrier((up, down, state, stats))
            farthest = [shift_seq(up[:KV_COLS], 1), shift_seq(down[KV_COLS:PACKET_ROWS], -1)]
            break
        down, up = shift_seq(down, -1), shift_seq(up, 1)
        above[step], below[step] = down, up
    state, stats = add_stats(
        heads,
        [below[3], label, above[3], above[2], above[1]],
        [(3, False), (4, True), (5, False), (6, False), (7, False)],
        state,
        stats,
    )
    stats, hidden_parts[2], hidden_parts[3] = barrier(
        (stats, hidden_parts[2], hidden_parts[3])
    )
    state, stats = add_stats(heads, farthest, [(4, False)], state, stats, last=True)

    dvs = {}
    acc, dk, dvs[4] = add_grads(heads, state, stats, farthest, [4], None, [BF16] * 2)
    down, up = shift_seq(dk, -1), None
    for step in range(3, 0, -1):
        starts = BF16 if step == 3 else F32
        acc, low, dvs[step], high, dvs[8 - step] = add_grads(
            heads,
            state,
            stats,
            [below[step], above[step]],
            [step, 8 - step],
            acc,
            [F32, starts, starts, F32],
        )
        acc, down = barrier((acc, down))
        down = shift_seq((low + down.astype(F32)).astype(BF16), -1)
        up = shift_seq(high if step == 3 else (high + up.astype(F32)).astype(BF16), 1)
    acc, *hidden_parts = barrier((acc, *turned(hidden_parts)))
    value_up = shift_seq(dvs[4], 1)
    dq, mine, dvs[0] = add_grads(heads, state, stats, [own], [0], acc, [F32] * 2, last=True)
    key_grad, near = finish(mine, down, up, 2)
    near, dvs[3], dvs[5] = barrier((near, dvs[3], dvs[5]))

    def value_step(step, value_up, value_down):
        value_up = (dvs[8 - step] + value_up.astype(F32)).astype(BF16)
        if value_down is None:
            value_down = dvs[step]
        else:
            value_down = (dvs[step] + value_down.astype(F32)).astype(BF16)
        return shift_seq(value_up, 1), shift_seq(value_down, -1)

    hidden_own, hidden_other = hidden_parts
    flops = 2 * X * SEG_LEN * Y * HEAD * KV_COLS
    tokens = [near] + [shift_xy(near, k, 0) for k in range(1, X)]
    value_up, value_down = value_step(3, value_up, None)
    given = on_core(
        given_kernel,
        "given",
        jax.ShapeDtypeStruct((Y * HEAD, KV_COLS), BF16),
        [hidden_other, *tokens],
        flops=flops,
    )
    given, value_up, value_down = barrier((given, value_up, value_down))
    value_up, value_down = value_step(2, value_up, value_down)
    kept = on_core(
        kept_kernel,
        "kept",
        jax.ShapeDtypeStruct((Y * HEAD, KV_COLS), BF16),
        [hidden_own, *tokens, swap_cores(given)],
        flops=flops,
    )
    kept, dvs[1], dvs[7] = barrier((kept, dvs[1], dvs[7]))
    value_up, value_down = value_step(1, value_up, value_down)
    groups = [
        [dp_index(y, x, c) * SEGMENTS + z for y in range(Y) for z in range(SEGMENTS)]
        for x in range(X)
        for c in range(CORES)
    ]
    rows = lax.all_to_all(kept, ("dp", "seq"), 0, 0, axis_index_groups=groups, tiled=True)
    value_grad = finish(dvs[0], value_down, value_up, 1)[0]
    weight_grad = jnp.sum(rows.reshape(Y * SEGMENTS, -1, KV_COLS).astype(F32), axis=0)
    return dq, key_grad, value_grad, weight_grad


def local(hidden_in, queries, keys, values, out_grad, parents, counts):
    dq, key_grad, value_grad, weight_grad = all_grads(
        hidden_in.reshape(SEG_LEN, -1), queries, keys, values, out_grad, parents, counts
    )
    return (
        dq.reshape(1, 1, SEG_LEN, Q_COLS),
        key_grad.reshape(1, 1, SEG_LEN, KV_COLS),
        value_grad.reshape(1, 1, SEG_LEN, KV_COLS),
        weight_grad,
    )


def solution(mesh):
    wide = P("dp", "seq", None, None)
    return jax.shard_map(
        local,
        mesh=mesh,
        in_specs=(wide, wide, wide, wide, wide, P("dp", "seq"), P("dp", "seq")),
        out_specs=(wide, wide, wide, P(("dp", "seq"), None)),
        check_vma=False,
    )
```

```python
import functools
import itertools
import math

import jax
import jax.numpy as jnp
from jax import lax
from jax.experimental import pallas as pl
from jax.experimental.pallas import tpu as pltpu
from jax.sharding import PartitionSpec as P

SEGMENTS = 8
SEG_LEN = 128
KV_HEADS = 4
GROUP = 8
HEAD = 128
KV_COLS = KV_HEADS * HEAD
Q_COLS = KV_HEADS * GROUP * HEAD
GROUP_COLS = GROUP * HEAD
STATS_HEADS = 2
KERNEL_VMEM = 16 << 20
SCALE = 1.0 / math.sqrt(HEAD)
SCALE_LOG2 = SCALE * math.log2(math.e)
NEG_FILL = -1e30
DEAD_LSE = 1e30
LABEL_ROWS = 16
PACKET_ROWS = 2 * KV_HEADS * SEG_LEN
STATE = 16
BF16 = jnp.bfloat16
F32 = jnp.float32

X, Y, CORES = 4, 4, 2
SHARE = CORES * HEAD


def dot_nt(a, b):
    return lax.dot_general(a, b, (((1,), (1,)), ((), ())), preferred_element_type=F32)


def dot_nn(a, b):
    return lax.dot_general(a, b, (((1,), (0,)), ((), ())), preferred_element_type=F32)


def dot_tn(a, b):
    return lax.dot_general(a, b, (((0,), (0,)), ((), ())), preferred_element_type=F32)


def key_bias(live):
    position = lax.broadcasted_iota(jnp.int32, (SEG_LEN, 1), 0)
    return jnp.where(position < live, 0.0, NEG_FILL).astype(F32)


def own_bias(live, heads):
    key_at = lax.broadcasted_iota(jnp.int32, (SEG_LEN, SEG_LEN), 0)
    query_at = lax.broadcasted_iota(jnp.int32, (SEG_LEN, SEG_LEN), 1)
    tile = jnp.where((key_at <= query_at) & (key_at < live), 0.0, NEG_FILL).astype(F32)
    return jnp.concatenate([tile] * heads, axis=1)


def block_rows(group):
    return slice(group * SEG_LEN, (group + 1) * SEG_LEN)


def key_value(refs, group):
    k_ref, v_ref = refs[0], refs[-1]
    first = KV_COLS if len(refs) == 1 else 0
    rows = block_rows(group)
    return k_ref[rows, :], v_ref[first + rows.start : first + rows.stop, :]


def group_cols(group):
    return slice(group * GROUP_COLS, (group + 1) * GROUP_COLS)


def scalar_of(rows):
    return jnp.max(rows.astype(F32)).astype(jnp.int32)


def state_value(ref, index):
    return scalar_of(ref[pl.ds(index, 1), :])


def set_state(ref, index, value):
    ref[pl.ds(index, 1), :] = jnp.full((1, HEAD), value, jnp.int32).astype(F32)


def stats_kernel(steps, first, last, *refs):
    if first:
        parent_ref, count_ref, q_ref, g_ref, packet_ref, out_ref, state_ref = refs
    else:
        q_ref, g_ref = refs[:2]
        packet_refs = refs[2:-4]
        in_ref, old_ref, out_ref, state_ref = refs[-4:]
    me = lax.axis_index("seq")

    def add_segment(packet, bias, start):
        width = STATS_HEADS * HEAD
        for group in range(KV_HEADS):
            k, v = key_value(packet, group)
            for chunk in range(GROUP_COLS // width):
                at = group * GROUP_COLS + chunk * width
                cols = slice(at, at + width)
                scores = dot_nn(k, q_ref[:, cols]) * SCALE_LOG2 + bias
                grad_probs = dot_nn(v, g_ref[:, cols])
                top = jnp.max(scores, axis=0, keepdims=True)
                if not start:
                    old_top = out_ref[0:1, cols]
                    top = jnp.maximum(top, old_top)
                weights = jnp.exp2(scores - top)
                total = jnp.sum(weights, axis=0, keepdims=True)
                mixed = jnp.sum(weights * grad_probs, axis=0, keepdims=True)
                if not start:
                    shrink = jnp.exp2(old_top - top)
                    total = total + out_ref[1:2, cols] * shrink
                    mixed = mixed + out_ref[2:3, cols] * shrink
                out_ref[0:1, cols] = top
                out_ref[1:2, cols] = total
                out_ref[2:3, cols] = mixed

    if first:
        live = count_ref[0, 0]
        state_ref[...] = jnp.zeros_like(state_ref)
        set_state(state_ref, 0, parent_ref[0, 0])
        set_state(state_ref, SEGMENTS, live)
        add_segment([packet_ref], own_bias(live, STATS_HEADS), True)
    else:
        state_ref[...] = old_ref[...]
        out_ref[...] = in_ref[...]
        if last:
            ((distance, _),) = steps
            live_there = state_value(old_ref, distance)

            @pl.when(live_there > 0)
            def _():
                add_segment(packet_refs, key_bias(live_there), False)

        else:
            current = state_value(old_ref, 0)
            for packet_ref, (distance, looked_up) in zip(packet_refs, steps):
                top_row = packet_ref.shape[0] - LABEL_ROWS
                hit = current == me - distance
                parent = scalar_of(packet_ref[top_row:, :][: LABEL_ROWS // 2])
                current = jnp.where(hit, parent, current)

                @pl.when(hit)
                def _():
                    live = scalar_of(packet_ref[top_row:, :][LABEL_ROWS // 2 :])
                    set_state(state_ref, distance, live)
                    if not looked_up:
                        add_segment([packet_ref], key_bias(live), False)

            set_state(state_ref, 0, current)

    if last:
        live = state_value(old_ref, SEGMENTS)
        position = lax.broadcasted_iota(jnp.int32, (1, Q_COLS), 1) & (SEG_LEN - 1)
        total = out_ref[1:2, :]
        row_delta = out_ref[2:3, :] / total
        lse = out_ref[0:1, :] + jnp.log2(total)
        out_ref[0:1, :] = jnp.where(position < live, lse, DEAD_LSE)
        out_ref[1:2, :] = row_delta


def grads_kernel(distances, first, last, *refs):
    state_ref, q_ref, qt_ref, g_ref, gt_ref, stats_ref = refs[:6]
    count = 2 if first else len(distances)
    arrays, rest = refs[6 : 6 + count], refs[6 + count :]
    packets = [arrays] if first else [[ref] for ref in arrays]
    if first:
        in_ref, (acc_ref, *out_refs) = None, rest
    else:
        in_ref, acc_ref, *out_refs = rest

    def run(segments):
        for group in range(KV_HEADS):
            blocks = [key_value(packet, group) for packet, _, _ in segments]
            k = jnp.concatenate([block[0] for block in blocks], axis=0)
            v = jnp.concatenate([block[1] for block in blocks], axis=0)
            bias = jnp.concatenate([bias for _, bias, _ in segments], axis=0)
            cols = group_cols(group)
            scores = dot_nn(k, qt_ref[:, cols]) * SCALE_LOG2 + bias
            probs = jnp.exp2(scores - stats_ref[0:1, cols])
            grad_probs = dot_nn(v, gt_ref[:, cols])
            grad_scores = (probs * (grad_probs - stats_ref[1:2, cols])).astype(BF16)
            dv = dot_nn(probs.astype(BF16), g_ref[cols, :])
            dk = dot_nn(grad_scores, q_ref[cols, :]) * SCALE
            dq = dot_nn(k.T, grad_scores)
            if in_ref is not None:
                dq = dq + in_ref[:, cols]
            acc_ref[:, cols] = dq
            for i, (_, _, (dk_ref, dv_ref)) in enumerate(segments):
                part = slice(i * SEG_LEN, (i + 1) * SEG_LEN)
                dk_ref[block_rows(group), :] = dk[part].astype(dk_ref.dtype)
                dv_ref[block_rows(group), :] = dv[part].astype(dv_ref.dtype)

    if last:
        bias = own_bias(state_value(state_ref, SEGMENTS), GROUP)
        run([(packets[0], bias, out_refs)])
        return
    lives = [state_value(state_ref, distance) for distance in distances]
    outs = [out_refs[2 * i : 2 * i + 2] for i in range(len(distances))]
    for chosen in itertools.product((False, True), repeat=len(distances)):
        taken_here = functools.reduce(
            jnp.logical_and,
            [(live > 0) if choice else (live == 0) for live, choice in zip(lives, chosen)],
        )

        @pl.when(taken_here)
        def _():
            for choice, pair in zip(chosen, outs):
                if not choice:
                    for ref in pair:
                        ref[...] = jnp.zeros_like(ref)
            if any(chosen):
                run(
                    [
                        (packet, key_bias(live), pair)
                        for packet, live, pair, choice in zip(packets, lives, outs, chosen)
                        if choice
                    ]
                )
            elif in_ref is None:
                acc_ref[...] = jnp.zeros_like(acc_ref)
            else:
                acc_ref[...] = in_ref[...]


def outputs_kernel(acc_ref, near_ref, query_ref, key_ref):
    for head in range(KV_HEADS * GROUP):
        part = slice(head * HEAD, (head + 1) * HEAD)
        query_ref[:, part] = (acc_ref[:, part] * SCALE).T.astype(BF16)
    key_ref[...] = near_ref[...]


SMEM_SPEC = pl.BlockSpec(memory_space=pltpu.SMEM)
VMEM_SPEC = pl.BlockSpec(memory_space=pltpu.VMEM)
STATS_SHAPE = jax.ShapeDtypeStruct((8, Q_COLS), F32)
STATE_SHAPE = jax.ShapeDtypeStruct((STATE, HEAD), F32)
BLOCK_FLOPS = 2 * SEG_LEN * SEG_LEN * HEAD * KV_HEADS * GROUP


def on_core(kernel, name, out_shape, operands, scalars=0, out_specs=None, flops=0, aliases=None):
    many = isinstance(out_shape, list)
    if out_specs is None:
        out_specs = [VMEM_SPEC] * len(out_shape) if many else VMEM_SPEC
    moved = sum(o.size * o.dtype.itemsize for o in operands)
    return pl.pallas_call(
        kernel,
        out_shape=out_shape,
        in_specs=[SMEM_SPEC] * scalars + [VMEM_SPEC] * (len(operands) - scalars),
        out_specs=out_specs,
        name=name,
        input_output_aliases=aliases or {},
        cost_estimate=pl.CostEstimate(flops=flops, bytes_accessed=moved, transcendentals=0),
        compiler_params=pltpu.CompilerParams(vmem_limit_bytes=KERNEL_VMEM),
    )(*operands)


def add_stats(heads, packets, steps, state, stats, last=False):
    _, qt, _, gt = heads
    first = stats is None
    if first:
        operands = [*state, qt, gt, *packets]
    else:
        operands = [qt, gt, *packets, stats, state]
    stats, state = on_core(
        functools.partial(stats_kernel, tuple(steps), first, last),
        "stats",
        [STATS_SHAPE, STATE_SHAPE],
        operands,
        scalars=len(state) if first else 0,
        flops=4 * BLOCK_FLOPS * len(packets),
    )
    return state, stats


def add_grads(heads, state, stats, packets, distances, acc, dtypes, last=False):
    first = acc is None
    operands = [state, *heads, stats, *packets]
    aliases = {}
    if not first:
        aliases = {len(operands): 0}
        operands.append(acc)
    out_shapes = [jax.ShapeDtypeStruct((HEAD, Q_COLS), F32)]
    out_shapes += [jax.ShapeDtypeStruct((KV_COLS, HEAD), dtype) for dtype in dtypes]
    return on_core(
        functools.partial(grads_kernel, tuple(distances), first, last),
        "grads",
        out_shapes,
        operands,
        flops=10 * BLOCK_FLOPS * len(distances),
        aliases=aliases,
    )


def shift_seq(array, k):
    return lax.ppermute(array, "seq", [(i, (i + k) % SEGMENTS) for i in range(SEGMENTS)])


def swap_cores(array):
    return lax.ppermute(array, "dp", [(i, i ^ 1) for i in range(X * Y * CORES)])


def dp_index(y, x, core):
    return (y % Y * X + x % X) * CORES + core


def shift_xy(array, along_x, along_y):
    pairs = [
        (dp_index(y, x, c), dp_index(y + along_y, x + along_x, c))
        for y in range(Y)
        for x in range(X)
        for c in range(CORES)
    ]
    return lax.ppermute(array, "dp", pairs)


def pack_kernel(parent_ref, count_ref, k_ref, v_ref, out_ref, sems):
    copies = []
    for head in range(KV_HEADS):
        for side, ref in enumerate((k_ref, v_ref)):
            copies.append(
                pltpu.make_async_copy(
                    ref.at[:, pl.ds(head * HEAD, HEAD)],
                    out_ref.at[pl.ds((side * KV_HEADS + head) * SEG_LEN, SEG_LEN), :],
                    sems.at[2 * head + side],
                )
            )
    for copy in copies:
        copy.start()
    row = lax.broadcasted_iota(jnp.int32, (LABEL_ROWS, HEAD), 0)
    labels = jnp.where(row < LABEL_ROWS // 2, parent_ref[0, 0], count_ref[0, 0])
    out_ref[PACKET_ROWS:, :] = labels.astype(F32).astype(BF16)
    for copy in copies:
        copy.wait()


def ring_packet(keys, values, parents, counts):
    return pl.pallas_call(
        pack_kernel,
        out_shape=jax.ShapeDtypeStruct((PACKET_ROWS + LABEL_ROWS, HEAD), BF16),
        in_specs=[SMEM_SPEC, SMEM_SPEC] + [pl.BlockSpec(memory_space=pltpu.HBM)] * 2,
        out_specs=VMEM_SPEC,
        scratch_shapes=[pltpu.SemaphoreType.DMA((2 * KV_HEADS,))],
        name="pack",
        compiler_params=pltpu.CompilerParams(vmem_limit_bytes=KERNEL_VMEM),
    )(
        parents,
        counts,
        pltpu.with_memory_space_constraint(keys, pltpu.HBM),
        pltpu.with_memory_space_constraint(values, pltpu.HBM),
    )


def finish_kernel(mine_ref, down_ref, up_ref, out_ref):
    for head in range(KV_HEADS):
        rows = block_rows(head)
        total = mine_ref[rows, :] + (
            down_ref[rows, :].astype(F32) + up_ref[rows, :].astype(F32)
        )
        out_ref[:, head * HEAD : (head + 1) * HEAD] = total.astype(BF16)


def finish(mine, down, up):
    return on_core(
        finish_kernel,
        "finish",
        jax.ShapeDtypeStruct((SEG_LEN, KV_COLS), BF16),
        [mine, down, up],
    )


def taken(array, index, axis):
    return lax.dynamic_index_in_dim(array, index, axis, keepdims=False)


def places():
    dp = lax.axis_index("dp")
    core = lax.rem(dp, CORES)
    x = lax.rem(lax.div(dp, CORES), X)
    y = lax.div(dp, CORES * X)
    return y, x, core


def load_kernel(q_ref, g_ref, hidden_ref, *refs):
    head_refs, share_refs, (buffer, head_sems, share_sems) = refs[:4], refs[4:-3], refs[-3:]
    copies = [
        pltpu.make_async_copy(ref, buffer.at[i], head_sems.at[i])
        for i, ref in enumerate((q_ref, g_ref))
    ]
    x = places()[1]
    for k, ref in enumerate(share_refs):
        to = lax.rem(x + k, X)
        for y in range(Y):
            first = pl.multiple_of((y * X + to) * SHARE, SHARE)
            copies.append(
                pltpu.make_async_copy(
                    hidden_ref.at[:, pl.ds(first, SHARE)],
                    ref.at[:, pl.ds(y * SHARE, SHARE)],
                    share_sems.at[k * Y + y],
                )
            )
    for copy in copies:
        copy.start()
    for i in range(2):
        copies[i].wait()
        rows_ref, turned_ref = head_refs[2 * i : 2 * i + 2]
        for head in range(KV_HEADS * GROUP):
            part = slice(head * HEAD, (head + 1) * HEAD)
            block = buffer[i, :, part]
            rows_ref[part, :] = block
            turned_ref[:, part] = block.T
    for copy in copies[2:]:
        copy.wait()


def loaded(array_q, array_g, hidden):
    shapes = [(KV_HEADS * GROUP * SEG_LEN, HEAD), (HEAD, KV_HEADS * GROUP * SEG_LEN)] * 2
    shapes += [(SEG_LEN, Y * SHARE)] * X
    outs = pl.pallas_call(
        load_kernel,
        out_shape=[jax.ShapeDtypeStruct(shape, BF16) for shape in shapes],
        in_specs=[pl.BlockSpec(memory_space=pltpu.HBM)] * 3,
        out_specs=[VMEM_SPEC] * len(shapes),
        scratch_shapes=[
            pltpu.VMEM((2, SEG_LEN, Q_COLS), BF16),
            pltpu.SemaphoreType.DMA((2,)),
            pltpu.SemaphoreType.DMA((X * Y,)),
        ],
        name="load",
        compiler_params=pltpu.CompilerParams(vmem_limit_bytes=KERNEL_VMEM),
    )(*[pltpu.with_memory_space_constraint(a, pltpu.HBM) for a in (array_q, array_g, hidden)])
    return outs[:4], outs[4:]


def turn_kernel(*refs):
    part_refs, out_refs = refs[:X], refs[X:]
    here, _, core = places()
    for side, out_ref in enumerate(out_refs):
        for k in range(Y):
            of = lax.rem(here + k, Y) * CORES + lax.rem(core + side, CORES)
            first = pl.multiple_of(of * HEAD, HEAD)
            for i, ref in enumerate(part_refs):
                out_ref[k * HEAD : (k + 1) * HEAD, i * SEG_LEN : (i + 1) * SEG_LEN] = ref[
                    :, pl.ds(first, HEAD)
                ].T


def turned(parts):
    return on_core(
        turn_kernel,
        "turn",
        [jax.ShapeDtypeStruct((Y * HEAD, X * SEG_LEN), BF16)] * CORES,
        list(parts),
    )


def given_kernel(hidden_ref, *refs):
    token_refs, (out_ref,) = refs[:X], refs[X:]
    tokens = jnp.concatenate([ref[...] for ref in token_refs], axis=0)
    out_ref[...] = dot_nn(hidden_ref[...], tokens).astype(BF16)


def kept_kernel(hidden_ref, *refs):
    token_refs, got_ref, own_ref, out_refs = refs[:X], refs[X], refs[X + 1], refs[X + 2 :]
    tokens = jnp.concatenate([ref[...] for ref in token_refs], axis=0)
    total = dot_nn(hidden_ref[...], tokens) + got_ref[...].astype(F32)
    own_ref[...] = total[:HEAD]
    for k, ref in enumerate(out_refs):
        ref[...] = total[(k + 1) * HEAD : (k + 2) * HEAD].astype(BF16)


def all_grads(hidden, queries, keys, values, out_grad, parents, counts):
    barrier = lax.optimization_barrier
    own = ring_packet(
        keys.reshape(SEG_LEN, KV_COLS), values.reshape(SEG_LEN, KV_COLS), parents, counts
    )
    up, down = own, own
    below, above = {}, {}
    state, stats = (parents, counts), None
    for step in range(1, 5):
        if step == 2:
            heads, shares = loaded(
                queries.reshape(SEG_LEN, Q_COLS), out_grad.reshape(SEG_LEN, Q_COLS), hidden
            )
            up, down, *rest = barrier((up, down, *heads, *shares))
            heads, shares = rest[:4], rest[4:]
            hidden_parts = [
                shift_xy(share, k, 0) if k else share for k, share in enumerate(shares)
            ]
        if step == 3:
            state, stats = add_stats(heads, [own], [], state, None)
            up, down, state, stats = barrier((up, down, state, stats))
            label = shift_seq(up[PACKET_ROWS:], 2)
            stats, hidden_parts[1] = barrier((stats, hidden_parts[1]))
        if step == 4:
            state, stats = add_stats(
                heads, [below[1], below[2]], [(1, False), (2, False)], state, stats
            )
            up, down, state, stats = barrier((up, down, state, stats))
            farthest = [shift_seq(up[:KV_COLS], 1), shift_seq(down[KV_COLS:PACKET_ROWS], -1)]
            break
        down, up = shift_seq(down, -1), shift_seq(up, 1)
        above[step], below[step] = down, up
    state, stats = add_stats(
        heads,
        [below[3], label, above[3], above[2], above[1]],
        [(3, False), (4, True), (5, False), (6, False), (7, False)],
        state,
        stats,
    )
    stats, hidden_parts[2], hidden_parts[3] = barrier(
        (stats, hidden_parts[2], hidden_parts[3])
    )
    state, stats = add_stats(heads, farthest, [(4, False)], state, stats, last=True)

    dvs = {}
    acc, dk, dvs[4] = add_grads(heads, state, stats, farthest, [4], None, [BF16] * 2)
    down, up = shift_seq(dk, -1), None
    for step in range(3, 0, -1):
        starts = BF16 if step == 3 else F32
        acc, low, dvs[step], high, dvs[8 - step] = add_grads(
            heads,
            state,
            stats,
            [below[step], above[step]],
            [step, 8 - step],
            acc,
            [F32, starts, starts, F32],
        )
        acc, down = barrier((acc, down))
        down = shift_seq((low + down.astype(F32)).astype(BF16), -1)
        up = shift_seq(high if step == 3 else (high + up.astype(F32)).astype(BF16), 1)
    acc, *hidden_parts = barrier((acc, *turned(hidden_parts)))
    value_up = shift_seq(dvs[4], 1)
    acc, mine, dvs[0] = add_grads(heads, state, stats, [own], [0], acc, [F32] * 2, last=True)
    near = finish(mine, down, up)
    near, dvs[3], dvs[5] = barrier((near, dvs[3], dvs[5]))

    def value_step(step, value_up, value_down):
        value_up = (dvs[8 - step] + value_up.astype(F32)).astype(BF16)
        if value_down is None:
            value_down = dvs[step]
        else:
            value_down = (dvs[step] + value_down.astype(F32)).astype(BF16)
        return shift_seq(value_up, 1), shift_seq(value_down, -1)

    hidden_own, hidden_other = hidden_parts
    flops = 2 * X * SEG_LEN * Y * HEAD * KV_COLS
    tokens = [near] + [shift_xy(near, k, 0) for k in range(1, X)]
    value_up, value_down = value_step(3, value_up, None)
    given = on_core(
        given_kernel,
        "given",
        jax.ShapeDtypeStruct((Y * HEAD, KV_COLS), BF16),
        [hidden_other, *tokens],
        flops=flops,
    )
    given, value_up, value_down = barrier((given, value_up, value_down))
    value_up, value_down = value_step(2, value_up, value_down)
    kept, *low = on_core(
        kept_kernel,
        "kept",
        [jax.ShapeDtypeStruct((HEAD, KV_COLS), F32)]
        + [jax.ShapeDtypeStruct((HEAD, KV_COLS), BF16)] * (Y - 1),
        [hidden_own, *tokens, swap_cores(given)],
        flops=flops,
    )
    *low, dvs[1], dvs[7] = barrier((*low, dvs[1], dvs[7]))
    others = [shift_xy(low[k - 1], 0, k) for k in range(1, Y)]
    value_up, value_down = value_step(1, value_up, value_down)
    total = kept
    for other in others:
        total = total + other.astype(F32)
    total, value_up, value_down, acc = barrier(
        (total.astype(BF16), value_up, value_down, acc)
    )
    rows = lax.all_to_all(total, "seq", 0, 0, tiled=True)
    value_grad = finish(dvs[0], value_down, value_up)
    value_grad, acc = barrier((value_grad, acc))
    dq, key_grad = on_core(
        outputs_kernel,
        "outputs",
        [jax.ShapeDtypeStruct((SEG_LEN, n), BF16) for n in (Q_COLS, KV_COLS)],
        [acc, near],
    )
    weight_grad = jnp.sum(rows.reshape(SEGMENTS, -1, KV_COLS).astype(F32), axis=0)
    return dq, key_grad, value_grad, weight_grad


def local(hidden_in, queries, keys, values, out_grad, parents, counts):
    dq, key_grad, value_grad, weight_grad = all_grads(
        hidden_in.reshape(SEG_LEN, -1), queries, keys, values, out_grad, parents, counts
    )
    return (
        dq.reshape(1, 1, SEG_LEN, Q_COLS),
        key_grad.reshape(1, 1, SEG_LEN, KV_COLS),
        value_grad.reshape(1, 1, SEG_LEN, KV_COLS),
        weight_grad,
    )


def solution(mesh):
    wide = P("dp", "seq", None, None)
    return jax.shard_map(
        local,
        mesh=mesh,
        in_specs=(wide, wide, wide, wide, wide, P("dp", "seq"), P("dp", "seq")),
        out_specs=(wide, wide, wide, P(("dp", "seq"), None)),
        check_vma=False,
    )
```

```python
import functools
import itertools
import math

import jax
import jax.numpy as jnp
from jax import lax
from jax.experimental import pallas as pl
from jax.experimental.pallas import tpu as pltpu
from jax.sharding import PartitionSpec as P

SEGMENTS = 8
SEG_LEN = 128
KV_HEADS = 4
GROUP = 8
HEAD = 128
KV_COLS = KV_HEADS * HEAD
Q_COLS = KV_HEADS * GROUP * HEAD
GROUP_COLS = GROUP * HEAD
STATS_HEADS = 2
KERNEL_VMEM = 16 << 20
SCALE = 1.0 / math.sqrt(HEAD)
SCALE_LOG2 = SCALE * math.log2(math.e)
NEG_FILL = -1e30
DEAD_LSE = 1e30
LABEL_ROWS = 16
PACKET_ROWS = 2 * KV_HEADS * SEG_LEN
STATE = 16
BF16 = jnp.bfloat16
F32 = jnp.float32

X, Y, CORES = 4, 4, 2
SHARE = CORES * HEAD


def dot_nt(a, b):
    return lax.dot_general(a, b, (((1,), (1,)), ((), ())), preferred_element_type=F32)


def dot_nn(a, b):
    return lax.dot_general(a, b, (((1,), (0,)), ((), ())), preferred_element_type=F32)


def dot_tn(a, b):
    return lax.dot_general(a, b, (((0,), (0,)), ((), ())), preferred_element_type=F32)


def key_bias(live):
    position = lax.broadcasted_iota(jnp.int32, (SEG_LEN, 1), 0)
    return jnp.where(position < live, 0.0, NEG_FILL).astype(F32)


def own_bias(live, heads):
    key_at = lax.broadcasted_iota(jnp.int32, (SEG_LEN, SEG_LEN), 0)
    query_at = lax.broadcasted_iota(jnp.int32, (SEG_LEN, SEG_LEN), 1)
    tile = jnp.where((key_at <= query_at) & (key_at < live), 0.0, NEG_FILL).astype(F32)
    return jnp.concatenate([tile] * heads, axis=1)


def aligned(start, size):
    return pl.ds(start if isinstance(start, int) else pl.multiple_of(start, size), size)


def block_rows(group, first=0):
    return aligned(first + group * SEG_LEN, SEG_LEN)


def key_value(refs, group):
    k_ref, v_ref = refs[0], refs[-1]
    first = KV_COLS if len(refs) == 1 else 0
    return k_ref[block_rows(group), :], v_ref[block_rows(group, first), :]


def group_cols(group):
    return aligned(group * GROUP_COLS, GROUP_COLS)


def over(count, body, looped):
    if looped:

        def step(i, carry):
            body(i)
            return carry

        lax.fori_loop(0, count, step, 0)
    else:
        for i in range(count):
            body(i)


def scalar_of(rows):
    return jnp.max(rows.astype(F32)).astype(jnp.int32)


def state_value(ref, index):
    return scalar_of(ref[pl.ds(index, 1), :])


def set_state(ref, index, value):
    ref[pl.ds(index, 1), :] = jnp.full((1, HEAD), value, jnp.int32).astype(F32)


def stats_kernel(steps, first, last, *refs):
    if first:
        parent_ref, count_ref, q_ref, g_ref, packet_ref, out_ref, state_ref = refs
    else:
        q_ref, g_ref = refs[:2]
        packet_refs = refs[2:-4]
        in_ref, old_ref, out_ref, state_ref = refs[-4:]
    me = lax.axis_index("seq")

    def add_segment(packet, bias, start):
        width = STATS_HEADS * HEAD

        def one_group(group):
            k, v = key_value(packet, group)
            for chunk in range(GROUP_COLS // width):
                cols = aligned(group * GROUP_COLS + chunk * width, width)
                scores = dot_nn(k, q_ref[:, cols]) * SCALE_LOG2 + bias
                grad_probs = dot_nn(v, g_ref[:, cols])
                top = jnp.max(scores, axis=0, keepdims=True)
                if not start:
                    old_top = out_ref[0:1, cols]
                    top = jnp.maximum(top, old_top)
                weights = jnp.exp2(scores - top)
                total = jnp.sum(weights, axis=0, keepdims=True)
                mixed = jnp.sum(weights * grad_probs, axis=0, keepdims=True)
                if not start:
                    shrink = jnp.exp2(old_top - top)
                    total = total + out_ref[1:2, cols] * shrink
                    mixed = mixed + out_ref[2:3, cols] * shrink
                out_ref[0:1, cols] = top
                out_ref[1:2, cols] = total
                out_ref[2:3, cols] = mixed

        over(KV_HEADS, one_group, looped=start)

    if first:
        live = count_ref[0, 0]
        state_ref[...] = jnp.zeros_like(state_ref)
        set_state(state_ref, 0, parent_ref[0, 0])
        set_state(state_ref, SEGMENTS, live)
        add_segment([packet_ref], own_bias(live, STATS_HEADS), True)
    else:
        state_ref[...] = old_ref[...]
        out_ref[...] = in_ref[...]
        if last:
            ((distance, _),) = steps
            live_there = state_value(old_ref, distance)

            @pl.when(live_there > 0)
            def _():
                add_segment(packet_refs, key_bias(live_there), False)

        else:
            current = state_value(old_ref, 0)
            for packet_ref, (distance, looked_up) in zip(packet_refs, steps):
                top_row = packet_ref.shape[0] - LABEL_ROWS
                hit = current == me - distance
                parent = scalar_of(packet_ref[top_row:, :][: LABEL_ROWS // 2])
                current = jnp.where(hit, parent, current)

                @pl.when(hit)
                def _():
                    live = scalar_of(packet_ref[top_row:, :][LABEL_ROWS // 2 :])
                    set_state(state_ref, distance, live)
                    if not looked_up:
                        add_segment([packet_ref], key_bias(live), False)

            set_state(state_ref, 0, current)

    if last:
        live = state_value(old_ref, SEGMENTS)
        position = lax.broadcasted_iota(jnp.int32, (1, Q_COLS), 1) & (SEG_LEN - 1)
        total = out_ref[1:2, :]
        row_delta = out_ref[2:3, :] / total
        lse = out_ref[0:1, :] + jnp.log2(total)
        out_ref[0:1, :] = jnp.where(position < live, lse, DEAD_LSE)
        out_ref[1:2, :] = row_delta


def grads_kernel(distances, first, last, *refs):
    state_ref, q_ref, qt_ref, g_ref, gt_ref, stats_ref = refs[:6]
    count = 2 if first else len(distances)
    arrays, rest = refs[6 : 6 + count], refs[6 + count :]
    packets = [arrays] if first else [[ref] for ref in arrays]
    if first:
        in_ref, (acc_ref, *out_refs) = None, rest
    else:
        in_ref, acc_ref, *out_refs = rest

    def run(segments):
        def one_group(group):
            blocks = [key_value(packet, group) for packet, _, _ in segments]
            k = jnp.concatenate([block[0] for block in blocks], axis=0)
            v = jnp.concatenate([block[1] for block in blocks], axis=0)
            bias = jnp.concatenate([bias for _, bias, _ in segments], axis=0)
            cols = group_cols(group)
            scores = dot_nn(k, qt_ref[:, cols]) * SCALE_LOG2 + bias
            probs = jnp.exp2(scores - stats_ref[0:1, cols])
            grad_probs = dot_nn(v, gt_ref[:, cols])
            grad_scores = (probs * (grad_probs - stats_ref[1:2, cols])).astype(BF16)
            dv = dot_nn(probs.astype(BF16), g_ref[cols, :])
            dk = dot_nn(grad_scores, q_ref[cols, :]) * SCALE
            dq = dot_nn(k.T, grad_scores)
            if in_ref is not None:
                dq = dq + in_ref[:, cols]
            acc_ref[:, cols] = dq
            for i, (_, _, (dk_ref, dv_ref)) in enumerate(segments):
                part = slice(i * SEG_LEN, (i + 1) * SEG_LEN)
                dk_ref[block_rows(group), :] = dk[part].astype(dk_ref.dtype)
                dv_ref[block_rows(group), :] = dv[part].astype(dv_ref.dtype)

        over(KV_HEADS, one_group, looped=len(segments) == 1)

    if last:
        bias = own_bias(state_value(state_ref, SEGMENTS), GROUP)
        run([(packets[0], bias, out_refs)])
        return
    lives = [state_value(state_ref, distance) for distance in distances]
    outs = [out_refs[2 * i : 2 * i + 2] for i in range(len(distances))]
    for chosen in itertools.product((False, True), repeat=len(distances)):
        taken_here = functools.reduce(
            jnp.logical_and,
            [(live > 0) if choice else (live == 0) for live, choice in zip(lives, chosen)],
        )

        @pl.when(taken_here)
        def _():
            for choice, pair in zip(chosen, outs):
                if not choice:
                    for ref in pair:
                        ref[...] = jnp.zeros_like(ref)
            if any(chosen):
                run(
                    [
                        (packet, key_bias(live), pair)
                        for packet, live, pair, choice in zip(packets, lives, outs, chosen)
                        if choice
                    ]
                )
            elif in_ref is None:
                acc_ref[...] = jnp.zeros_like(acc_ref)
            else:
                acc_ref[...] = in_ref[...]


def outputs_kernel(acc_ref, near_ref, query_ref, key_ref):
    def one_group(group):
        for head in range(GROUP):
            part = aligned(group * GROUP_COLS + head * HEAD, HEAD)
            query_ref[:, part] = (acc_ref[:, part] * SCALE).T.astype(BF16)

    over(KV_HEADS, one_group, looped=True)
    key_ref[...] = near_ref[...]


SMEM_SPEC = pl.BlockSpec(memory_space=pltpu.SMEM)
VMEM_SPEC = pl.BlockSpec(memory_space=pltpu.VMEM)
STATS_SHAPE = jax.ShapeDtypeStruct((8, Q_COLS), F32)
STATE_SHAPE = jax.ShapeDtypeStruct((STATE, HEAD), F32)
BLOCK_FLOPS = 2 * SEG_LEN * SEG_LEN * HEAD * KV_HEADS * GROUP


def on_core(kernel, name, out_shape, operands, scalars=0, out_specs=None, flops=0, aliases=None):
    many = isinstance(out_shape, list)
    if out_specs is None:
        out_specs = [VMEM_SPEC] * len(out_shape) if many else VMEM_SPEC
    moved = sum(o.size * o.dtype.itemsize for o in operands)
    return pl.pallas_call(
        kernel,
        out_shape=out_shape,
        in_specs=[SMEM_SPEC] * scalars + [VMEM_SPEC] * (len(operands) - scalars),
        out_specs=out_specs,
        name=name,
        input_output_aliases=aliases or {},
        cost_estimate=pl.CostEstimate(flops=flops, bytes_accessed=moved, transcendentals=0),
        compiler_params=pltpu.CompilerParams(vmem_limit_bytes=KERNEL_VMEM),
    )(*operands)


def add_stats(heads, packets, steps, state, stats, last=False):
    _, qt, _, gt = heads
    first = stats is None
    if first:
        operands = [*state, qt, gt, *packets]
    else:
        operands = [qt, gt, *packets, stats, state]
    stats, state = on_core(
        functools.partial(stats_kernel, tuple(steps), first, last),
        "stats",
        [STATS_SHAPE, STATE_SHAPE],
        operands,
        scalars=len(state) if first else 0,
        flops=4 * BLOCK_FLOPS * len(packets),
    )
    return state, stats


def add_grads(heads, state, stats, packets, distances, acc, dtypes, last=False):
    first = acc is None
    operands = [state, *heads, stats, *packets]
    aliases = {}
    if not first:
        aliases = {len(operands): 0}
        operands.append(acc)
    out_shapes = [jax.ShapeDtypeStruct((HEAD, Q_COLS), F32)]
    out_shapes += [jax.ShapeDtypeStruct((KV_COLS, HEAD), dtype) for dtype in dtypes]
    return on_core(
        functools.partial(grads_kernel, tuple(distances), first, last),
        "grads",
        out_shapes,
        operands,
        flops=10 * BLOCK_FLOPS * len(distances),
        aliases=aliases,
    )


def shift_seq(array, k):
    return lax.ppermute(array, "seq", [(i, (i + k) % SEGMENTS) for i in range(SEGMENTS)])


def swap_cores(array):
    return lax.ppermute(array, "dp", [(i, i ^ 1) for i in range(X * Y * CORES)])


def dp_index(y, x, core):
    return (y % Y * X + x % X) * CORES + core


def shift_xy(array, along_x, along_y):
    pairs = [
        (dp_index(y, x, c), dp_index(y + along_y, x + along_x, c))
        for y in range(Y)
        for x in range(X)
        for c in range(CORES)
    ]
    return lax.ppermute(array, "dp", pairs)


def pack_kernel(parent_ref, count_ref, k_ref, v_ref, out_ref, sems):
    copies = []
    for head in range(KV_HEADS):
        for side, ref in enumerate((k_ref, v_ref)):
            copies.append(
                pltpu.make_async_copy(
                    ref.at[:, pl.ds(head * HEAD, HEAD)],
                    out_ref.at[pl.ds((side * KV_HEADS + head) * SEG_LEN, SEG_LEN), :],
                    sems.at[2 * head + side],
                )
            )
    for copy in copies:
        copy.start()
    row = lax.broadcasted_iota(jnp.int32, (LABEL_ROWS, HEAD), 0)
    labels = jnp.where(row < LABEL_ROWS // 2, parent_ref[0, 0], count_ref[0, 0])
    out_ref[PACKET_ROWS:, :] = labels.astype(F32).astype(BF16)
    for copy in copies:
        copy.wait()


def ring_packet(keys, values, parents, counts):
    return pl.pallas_call(
        pack_kernel,
        out_shape=jax.ShapeDtypeStruct((PACKET_ROWS + LABEL_ROWS, HEAD), BF16),
        in_specs=[SMEM_SPEC, SMEM_SPEC] + [pl.BlockSpec(memory_space=pltpu.HBM)] * 2,
        out_specs=VMEM_SPEC,
        scratch_shapes=[pltpu.SemaphoreType.DMA((2 * KV_HEADS,))],
        name="pack",
        compiler_params=pltpu.CompilerParams(vmem_limit_bytes=KERNEL_VMEM),
    )(
        parents,
        counts,
        pltpu.with_memory_space_constraint(keys, pltpu.HBM),
        pltpu.with_memory_space_constraint(values, pltpu.HBM),
    )


def finish_kernel(mine_ref, down_ref, up_ref, out_ref):
    for head in range(KV_HEADS):
        rows = block_rows(head)
        total = mine_ref[rows, :] + (
            down_ref[rows, :].astype(F32) + up_ref[rows, :].astype(F32)
        )
        out_ref[:, head * HEAD : (head + 1) * HEAD] = total.astype(BF16)


def finish(mine, down, up):
    return on_core(
        finish_kernel,
        "finish",
        jax.ShapeDtypeStruct((SEG_LEN, KV_COLS), BF16),
        [mine, down, up],
    )


def taken(array, index, axis):
    return lax.dynamic_index_in_dim(array, index, axis, keepdims=False)


def places():
    dp = lax.axis_index("dp")
    core = lax.rem(dp, CORES)
    x = lax.rem(lax.div(dp, CORES), X)
    y = lax.div(dp, CORES * X)
    return y, x, core


def load_kernel(q_ref, g_ref, hidden_ref, *refs):
    head_refs, share_refs, (buffer, head_sems, share_sems) = refs[:4], refs[4:-3], refs[-3:]
    copies = [
        pltpu.make_async_copy(ref, buffer.at[i], head_sems.at[i])
        for i, ref in enumerate((q_ref, g_ref))
    ]
    x = places()[1]
    for k, ref in enumerate(share_refs):
        to = lax.rem(x + k, X)
        for y in range(Y):
            first = pl.multiple_of((y * X + to) * SHARE, SHARE)
            copies.append(
                pltpu.make_async_copy(
                    hidden_ref.at[:, pl.ds(first, SHARE)],
                    ref.at[:, pl.ds(y * SHARE, SHARE)],
                    share_sems.at[k * Y + y],
                )
            )
    for copy in copies:
        copy.start()
    for i in range(2):
        copies[i].wait()
        rows_ref, turned_ref = head_refs[2 * i : 2 * i + 2]

        def one_group(group):
            for head in range(GROUP):
                part = aligned(group * GROUP_COLS + head * HEAD, HEAD)
                block = buffer[i, :, part]
                rows_ref[part, :] = block
                turned_ref[:, part] = block.T

        over(KV_HEADS, one_group, looped=True)
    for copy in copies[2:]:
        copy.wait()


def loaded(array_q, array_g, hidden):
    shapes = [(KV_HEADS * GROUP * SEG_LEN, HEAD), (HEAD, KV_HEADS * GROUP * SEG_LEN)] * 2
    shapes += [(SEG_LEN, Y * SHARE)] * X
    outs = pl.pallas_call(
        load_kernel,
        out_shape=[jax.ShapeDtypeStruct(shape, BF16) for shape in shapes],
        in_specs=[pl.BlockSpec(memory_space=pltpu.HBM)] * 3,
        out_specs=[VMEM_SPEC] * len(shapes),
        scratch_shapes=[
            pltpu.VMEM((2, SEG_LEN, Q_COLS), BF16),
            pltpu.SemaphoreType.DMA((2,)),
            pltpu.SemaphoreType.DMA((X * Y,)),
        ],
        name="load",
        compiler_params=pltpu.CompilerParams(vmem_limit_bytes=KERNEL_VMEM),
    )(*[pltpu.with_memory_space_constraint(a, pltpu.HBM) for a in (array_q, array_g, hidden)])
    return outs[:4], outs[4:]


def turn_kernel(*refs):
    part_refs, out_refs = refs[:X], refs[X:]
    here, _, core = places()
    for side, out_ref in enumerate(out_refs):
        for k in range(Y):
            of = lax.rem(here + k, Y) * CORES + lax.rem(core + side, CORES)
            first = pl.multiple_of(of * HEAD, HEAD)
            for i, ref in enumerate(part_refs):
                out_ref[k * HEAD : (k + 1) * HEAD, i * SEG_LEN : (i + 1) * SEG_LEN] = ref[
                    :, pl.ds(first, HEAD)
                ].T


def turned(parts):
    return on_core(
        turn_kernel,
        "turn",
        [jax.ShapeDtypeStruct((Y * HEAD, X * SEG_LEN), BF16)] * CORES,
        list(parts),
    )


def given_kernel(hidden_ref, *refs):
    token_refs, (out_ref,) = refs[:X], refs[X:]
    tokens = jnp.concatenate([ref[...] for ref in token_refs], axis=0)
    out_ref[...] = dot_nn(hidden_ref[...], tokens).astype(BF16)


def kept_kernel(hidden_ref, *refs):
    token_refs, got_ref, own_ref, out_refs = refs[:X], refs[X], refs[X + 1], refs[X + 2 :]
    tokens = jnp.concatenate([ref[...] for ref in token_refs], axis=0)
    total = dot_nn(hidden_ref[...], tokens) + got_ref[...].astype(F32)
    own_ref[...] = total[:HEAD]
    for k, ref in enumerate(out_refs):
        ref[...] = total[(k + 1) * HEAD : (k + 2) * HEAD].astype(BF16)


def all_grads(hidden, queries, keys, values, out_grad, parents, counts):
    barrier = lax.optimization_barrier
    own = ring_packet(
        keys.reshape(SEG_LEN, KV_COLS), values.reshape(SEG_LEN, KV_COLS), parents, counts
    )
    up, down = own, own
    below, above = {}, {}
    state, stats = (parents, counts), None
    for step in range(1, 5):
        if step == 2:
            heads, shares = loaded(
                queries.reshape(SEG_LEN, Q_COLS), out_grad.reshape(SEG_LEN, Q_COLS), hidden
            )
            up, down, *rest = barrier((up, down, *heads, *shares))
            heads, shares = rest[:4], rest[4:]
            hidden_parts = [
                shift_xy(share, k, 0) if k else share for k, share in enumerate(shares)
            ]
        if step == 3:
            state, stats = add_stats(heads, [own], [], state, None)
            up, down, state, stats = barrier((up, down, state, stats))
            label = shift_seq(up[PACKET_ROWS:], 2)
            stats, hidden_parts[1] = barrier((stats, hidden_parts[1]))
        if step == 4:
            state, stats = add_stats(
                heads, [below[1], below[2]], [(1, False), (2, False)], state, stats
            )
            up, down, state, stats = barrier((up, down, state, stats))
            farthest = [shift_seq(up[:KV_COLS], 1), shift_seq(down[KV_COLS:PACKET_ROWS], -1)]
            break
        down, up = shift_seq(down, -1), shift_seq(up, 1)
        above[step], below[step] = down, up
    state, stats = add_stats(
        heads,
        [below[3], label, above[3], above[2], above[1]],
        [(3, False), (4, True), (5, False), (6, False), (7, False)],
        state,
        stats,
    )
    stats, hidden_parts[2], hidden_parts[3] = barrier(
        (stats, hidden_parts[2], hidden_parts[3])
    )
    state, stats = add_stats(heads, farthest, [(4, False)], state, stats, last=True)

    dvs = {}
    acc, dk, dvs[4] = add_grads(heads, state, stats, farthest, [4], None, [BF16] * 2)
    down, up = shift_seq(dk, -1), None
    for step in range(3, 0, -1):
        starts = BF16 if step == 3 else F32
        acc, low, dvs[step], high, dvs[8 - step] = add_grads(
            heads,
            state,
            stats,
            [below[step], above[step]],
            [step, 8 - step],
            acc,
            [F32, starts, starts, F32],
        )
        acc, down = barrier((acc, down))
        down = shift_seq((low + down.astype(F32)).astype(BF16), -1)
        up = shift_seq(high if step == 3 else (high + up.astype(F32)).astype(BF16), 1)
    acc, *hidden_parts = barrier((acc, *turned(hidden_parts)))
    value_up = shift_seq(dvs[4], 1)
    acc, mine, dvs[0] = add_grads(heads, state, stats, [own], [0], acc, [F32] * 2, last=True)
    near = finish(mine, down, up)
    near, dvs[3], dvs[5] = barrier((near, dvs[3], dvs[5]))

    def value_step(step, value_up, value_down):
        value_up = (dvs[8 - step] + value_up.astype(F32)).astype(BF16)
        if value_down is None:
            value_down = dvs[step]
        else:
            value_down = (dvs[step] + value_down.astype(F32)).astype(BF16)
        return shift_seq(value_up, 1), shift_seq(value_down, -1)

    hidden_own, hidden_other = hidden_parts
    flops = 2 * X * SEG_LEN * Y * HEAD * KV_COLS
    tokens = [near] + [shift_xy(near, k, 0) for k in range(1, X)]
    value_up, value_down = value_step(3, value_up, None)
    given = on_core(
        given_kernel,
        "given",
        jax.ShapeDtypeStruct((Y * HEAD, KV_COLS), BF16),
        [hidden_other, *tokens],
        flops=flops,
    )
    given, value_up, value_down = barrier((given, value_up, value_down))
    value_up, value_down = value_step(2, value_up, value_down)
    kept, *low = on_core(
        kept_kernel,
        "kept",
        [jax.ShapeDtypeStruct((HEAD, KV_COLS), F32)]
        + [jax.ShapeDtypeStruct((HEAD, KV_COLS), BF16)] * (Y - 1),
        [hidden_own, *tokens, swap_cores(given)],
        flops=flops,
    )
    *low, dvs[1], dvs[7] = barrier((*low, dvs[1], dvs[7]))
    others = [shift_xy(low[k - 1], 0, k) for k in range(1, Y)]
    value_up, value_down = value_step(1, value_up, value_down)
    total = kept
    for other in others:
        total = total + other.astype(F32)
    total, value_up, value_down, acc = barrier(
        (total.astype(BF16), value_up, value_down, acc)
    )
    rows = lax.all_to_all(total, "seq", 0, 0, tiled=True)
    value_grad = finish(dvs[0], value_down, value_up)
    value_grad, acc = barrier((value_grad, acc))
    dq, key_grad = on_core(
        outputs_kernel,
        "outputs",
        [jax.ShapeDtypeStruct((SEG_LEN, n), BF16) for n in (Q_COLS, KV_COLS)],
        [acc, near],
    )
    weight_grad = jnp.sum(rows.reshape(SEGMENTS, -1, KV_COLS).astype(F32), axis=0)
    return dq, key_grad, value_grad, weight_grad


def local(hidden_in, queries, keys, values, out_grad, parents, counts):
    dq, key_grad, value_grad, weight_grad = all_grads(
        hidden_in.reshape(SEG_LEN, -1), queries, keys, values, out_grad, parents, counts
    )
    return (
        dq.reshape(1, 1, SEG_LEN, Q_COLS),
        key_grad.reshape(1, 1, SEG_LEN, KV_COLS),
        value_grad.reshape(1, 1, SEG_LEN, KV_COLS),
        weight_grad,
    )


def solution(mesh):
    wide = P("dp", "seq", None, None)
    return jax.shard_map(
        local,
        mesh=mesh,
        in_specs=(wide, wide, wide, wide, wide, P("dp", "seq"), P("dp", "seq")),
        out_specs=(wide, wide, wide, P(("dp", "seq"), None)),
        check_vma=False,
    )
```

```python
import functools
import itertools
import math

import jax
import jax.numpy as jnp
from jax import lax
from jax.experimental import pallas as pl
from jax.experimental.pallas import tpu as pltpu
from jax.sharding import PartitionSpec as P

SEGMENTS = 8
SEG_LEN = 128
KV_HEADS = 4
GROUP = 8
HEAD = 128
KV_COLS = KV_HEADS * HEAD
Q_COLS = KV_HEADS * GROUP * HEAD
GROUP_COLS = GROUP * HEAD
STATS_HEADS = 2
KERNEL_VMEM = 16 << 20
SCALE = 1.0 / math.sqrt(HEAD)
SCALE_LOG2 = SCALE * math.log2(math.e)
NEG_FILL = -1e30
DEAD_LSE = 1e30
LABEL_ROWS = 16
PACKET_ROWS = 2 * KV_HEADS * SEG_LEN
STATE = 16
BF16 = jnp.bfloat16
F32 = jnp.float32

X, Y, CORES = 4, 4, 2
SHARE = CORES * HEAD


def dot_nt(a, b):
    return lax.dot_general(a, b, (((1,), (1,)), ((), ())), preferred_element_type=F32)


def dot_nn(a, b):
    return lax.dot_general(a, b, (((1,), (0,)), ((), ())), preferred_element_type=F32)


def dot_tn(a, b):
    return lax.dot_general(a, b, (((0,), (0,)), ((), ())), preferred_element_type=F32)


def key_bias(live):
    position = lax.broadcasted_iota(jnp.int32, (SEG_LEN, 1), 0)
    return jnp.where(position < live, 0.0, NEG_FILL).astype(F32)


def own_bias(live, heads):
    key_at = lax.broadcasted_iota(jnp.int32, (SEG_LEN, SEG_LEN), 0)
    query_at = lax.broadcasted_iota(jnp.int32, (SEG_LEN, SEG_LEN), 1)
    tile = jnp.where((key_at <= query_at) & (key_at < live), 0.0, NEG_FILL).astype(F32)
    return jnp.concatenate([tile] * heads, axis=1)


def aligned(start, size):
    return pl.ds(start if isinstance(start, int) else pl.multiple_of(start, size), size)


def block_rows(group, first=0):
    return aligned(first + group * SEG_LEN, SEG_LEN)


def key_value(refs, group):
    k_ref, v_ref = refs[0], refs[-1]
    first = KV_COLS if len(refs) == 1 else 0
    return k_ref[block_rows(group), :], v_ref[block_rows(group, first), :]


def group_cols(group):
    return aligned(group * GROUP_COLS, GROUP_COLS)


def over(count, body, looped):
    if looped:

        def step(i, carry):
            body(i)
            return carry

        lax.fori_loop(0, count, step, 0)
    else:
        for i in range(count):
            body(i)


def scalar_of(rows):
    return jnp.max(rows.astype(F32)).astype(jnp.int32)


def state_value(ref, index):
    return scalar_of(ref[pl.ds(index, 1), :])


def set_state(ref, index, value):
    ref[pl.ds(index, 1), :] = jnp.full((1, HEAD), value, jnp.int32).astype(F32)


def stats_kernel(steps, first, last, *refs):
    if first:
        parent_ref, count_ref, q_ref, g_ref, packet_ref, out_ref, state_ref = refs
    else:
        q_ref, g_ref = refs[:2]
        packet_refs = refs[2:-4]
        in_ref, old_ref, out_ref, state_ref = refs[-4:]
    me = lax.axis_index("seq")

    def add_segment(packet, bias, start):
        width = STATS_HEADS * HEAD

        def one_group(group):
            k, v = key_value(packet, group)
            for chunk in range(GROUP_COLS // width):
                cols = aligned(group * GROUP_COLS + chunk * width, width)
                scores = dot_nn(k, q_ref[:, cols]) * SCALE_LOG2 + bias
                grad_probs = dot_nn(v, g_ref[:, cols])
                top = jnp.max(scores, axis=0, keepdims=True)
                if not start:
                    old_top = out_ref[0:1, cols]
                    top = jnp.maximum(top, old_top)
                weights = jnp.exp2(scores - top)
                total = jnp.sum(weights, axis=0, keepdims=True)
                mixed = jnp.sum(weights * grad_probs, axis=0, keepdims=True)
                if not start:
                    shrink = jnp.exp2(old_top - top)
                    total = total + out_ref[1:2, cols] * shrink
                    mixed = mixed + out_ref[2:3, cols] * shrink
                out_ref[0:1, cols] = top
                out_ref[1:2, cols] = total
                out_ref[2:3, cols] = mixed

        over(KV_HEADS, one_group, looped=start)

    if first:
        live = count_ref[0, 0]
        state_ref[...] = jnp.zeros_like(state_ref)
        set_state(state_ref, 0, parent_ref[0, 0])
        set_state(state_ref, SEGMENTS, live)
        add_segment([packet_ref], own_bias(live, STATS_HEADS), True)
    else:
        state_ref[...] = old_ref[...]
        out_ref[...] = in_ref[...]
        if last:
            ((distance, _),) = steps
            live_there = state_value(old_ref, distance)

            @pl.when(live_there > 0)
            def _():
                add_segment(packet_refs, key_bias(live_there), False)

        else:
            current = state_value(old_ref, 0)
            for packet_ref, (distance, looked_up) in zip(packet_refs, steps):
                top_row = packet_ref.shape[0] - LABEL_ROWS
                hit = current == me - distance
                parent = scalar_of(packet_ref[top_row:, :][: LABEL_ROWS // 2])
                current = jnp.where(hit, parent, current)

                @pl.when(hit)
                def _():
                    live = scalar_of(packet_ref[top_row:, :][LABEL_ROWS // 2 :])
                    set_state(state_ref, distance, live)
                    if not looked_up:
                        add_segment([packet_ref], key_bias(live), False)

            set_state(state_ref, 0, current)

    if last:
        live = state_value(old_ref, SEGMENTS)
        position = lax.broadcasted_iota(jnp.int32, (1, Q_COLS), 1) & (SEG_LEN - 1)
        total = out_ref[1:2, :]
        row_delta = out_ref[2:3, :] / total
        lse = out_ref[0:1, :] + jnp.log2(total)
        out_ref[0:1, :] = jnp.where(position < live, lse, DEAD_LSE)
        out_ref[1:2, :] = row_delta


def grads_kernel(distances, first, last, *refs):
    state_ref, q_ref, qt_ref, g_ref, gt_ref, stats_ref = refs[:6]
    count = 2 if first else len(distances)
    arrays, rest = refs[6 : 6 + count], refs[6 + count :]
    packets = [arrays] if first else [[ref] for ref in arrays]
    if first:
        in_ref, (acc_ref, *out_refs) = None, rest
    else:
        in_ref, acc_ref, *out_refs = rest

    def run(segments):
        def one_group(group):
            blocks = [key_value(packet, group) for packet, _, _ in segments]
            k = jnp.concatenate([block[0] for block in blocks], axis=0)
            v = jnp.concatenate([block[1] for block in blocks], axis=0)
            bias = jnp.concatenate([bias for _, bias, _ in segments], axis=0)
            cols = group_cols(group)
            scores = dot_nn(k, qt_ref[:, cols]) * SCALE_LOG2 + bias
            probs = jnp.exp2(scores - stats_ref[0:1, cols])
            grad_probs = dot_nn(v, gt_ref[:, cols])
            grad_scores = (probs * (grad_probs - stats_ref[1:2, cols])).astype(BF16)
            dv = dot_nn(probs.astype(BF16), g_ref[cols, :])
            dk = dot_nn(grad_scores, q_ref[cols, :]) * SCALE
            dq = dot_nn(k.T, grad_scores)
            if in_ref is not None:
                dq = dq + in_ref[:, cols]
            acc_ref[:, cols] = dq
            for i, (_, _, (dk_ref, dv_ref)) in enumerate(segments):
                part = slice(i * SEG_LEN, (i + 1) * SEG_LEN)
                dk_ref[block_rows(group), :] = dk[part].astype(dk_ref.dtype)
                dv_ref[block_rows(group), :] = dv[part].astype(dv_ref.dtype)

        over(KV_HEADS, one_group, looped=len(segments) == 1 and not last)

    if last:
        bias = own_bias(state_value(state_ref, SEGMENTS), GROUP)
        run([(packets[0], bias, out_refs)])
        return
    lives = [state_value(state_ref, distance) for distance in distances]
    outs = [out_refs[2 * i : 2 * i + 2] for i in range(len(distances))]
    for chosen in itertools.product((False, True), repeat=len(distances)):
        taken_here = functools.reduce(
            jnp.logical_and,
            [(live > 0) if choice else (live == 0) for live, choice in zip(lives, chosen)],
        )

        @pl.when(taken_here)
        def _():
            for choice, pair in zip(chosen, outs):
                if not choice:
                    for ref in pair:
                        ref[...] = jnp.zeros_like(ref)
            if any(chosen):
                run(
                    [
                        (packet, key_bias(live), pair)
                        for packet, live, pair, choice in zip(packets, lives, outs, chosen)
                        if choice
                    ]
                )
            elif in_ref is None:
                acc_ref[...] = jnp.zeros_like(acc_ref)
            else:
                acc_ref[...] = in_ref[...]


def outputs_kernel(acc_ref, near_ref, query_ref, key_ref):
    def one_group(group):
        for head in range(GROUP):
            part = aligned(group * GROUP_COLS + head * HEAD, HEAD)
            query_ref[:, part] = (acc_ref[:, part] * SCALE).T.astype(BF16)

    over(KV_HEADS, one_group, looped=True)
    key_ref[...] = near_ref[...]


SMEM_SPEC = pl.BlockSpec(memory_space=pltpu.SMEM)
VMEM_SPEC = pl.BlockSpec(memory_space=pltpu.VMEM)
STATS_SHAPE = jax.ShapeDtypeStruct((8, Q_COLS), F32)
STATE_SHAPE = jax.ShapeDtypeStruct((STATE, HEAD), F32)
BLOCK_FLOPS = 2 * SEG_LEN * SEG_LEN * HEAD * KV_HEADS * GROUP


def on_core(kernel, name, out_shape, operands, scalars=0, out_specs=None, flops=0, aliases=None):
    many = isinstance(out_shape, list)
    if out_specs is None:
        out_specs = [VMEM_SPEC] * len(out_shape) if many else VMEM_SPEC
    moved = sum(o.size * o.dtype.itemsize for o in operands)
    return pl.pallas_call(
        kernel,
        out_shape=out_shape,
        in_specs=[SMEM_SPEC] * scalars + [VMEM_SPEC] * (len(operands) - scalars),
        out_specs=out_specs,
        name=name,
        input_output_aliases=aliases or {},
        cost_estimate=pl.CostEstimate(flops=flops, bytes_accessed=moved, transcendentals=0),
        compiler_params=pltpu.CompilerParams(vmem_limit_bytes=KERNEL_VMEM),
    )(*operands)


def add_stats(heads, packets, steps, state, stats, last=False):
    _, qt, _, gt = heads
    first = stats is None
    if first:
        operands = [*state, qt, gt, *packets]
    else:
        operands = [qt, gt, *packets, stats, state]
    stats, state = on_core(
        functools.partial(stats_kernel, tuple(steps), first, last),
        "stats",
        [STATS_SHAPE, STATE_SHAPE],
        operands,
        scalars=len(state) if first else 0,
        flops=4 * BLOCK_FLOPS * len(packets),
    )
    return state, stats


def add_grads(heads, state, stats, packets, distances, acc, dtypes, last=False):
    first = acc is None
    operands = [state, *heads, stats, *packets]
    aliases = {}
    if not first:
        aliases = {len(operands): 0}
        operands.append(acc)
    out_shapes = [jax.ShapeDtypeStruct((HEAD, Q_COLS), F32)]
    out_shapes += [jax.ShapeDtypeStruct((KV_COLS, HEAD), dtype) for dtype in dtypes]
    return on_core(
        functools.partial(grads_kernel, tuple(distances), first, last),
        "grads",
        out_shapes,
        operands,
        flops=10 * BLOCK_FLOPS * len(distances),
        aliases=aliases,
    )


def shift_seq(array, k):
    return lax.ppermute(array, "seq", [(i, (i + k) % SEGMENTS) for i in range(SEGMENTS)])


def swap_cores(array):
    return lax.ppermute(array, "dp", [(i, i ^ 1) for i in range(X * Y * CORES)])


def dp_index(y, x, core):
    return (y % Y * X + x % X) * CORES + core


def shift_xy(array, along_x, along_y):
    pairs = [
        (dp_index(y, x, c), dp_index(y + along_y, x + along_x, c))
        for y in range(Y)
        for x in range(X)
        for c in range(CORES)
    ]
    return lax.ppermute(array, "dp", pairs)


def pack_kernel(parent_ref, count_ref, k_ref, v_ref, out_ref, sems):
    copies = []
    for head in range(KV_HEADS):
        for side, ref in enumerate((k_ref, v_ref)):
            copies.append(
                pltpu.make_async_copy(
                    ref.at[:, pl.ds(head * HEAD, HEAD)],
                    out_ref.at[pl.ds((side * KV_HEADS + head) * SEG_LEN, SEG_LEN), :],
                    sems.at[2 * head + side],
                )
            )
    for copy in copies:
        copy.start()
    row = lax.broadcasted_iota(jnp.int32, (LABEL_ROWS, HEAD), 0)
    labels = jnp.where(row < LABEL_ROWS // 2, parent_ref[0, 0], count_ref[0, 0])
    out_ref[PACKET_ROWS:, :] = labels.astype(F32).astype(BF16)
    for copy in copies:
        copy.wait()


def ring_packet(keys, values, parents, counts):
    return pl.pallas_call(
        pack_kernel,
        out_shape=jax.ShapeDtypeStruct((PACKET_ROWS + LABEL_ROWS, HEAD), BF16),
        in_specs=[SMEM_SPEC, SMEM_SPEC] + [pl.BlockSpec(memory_space=pltpu.HBM)] * 2,
        out_specs=VMEM_SPEC,
        scratch_shapes=[pltpu.SemaphoreType.DMA((2 * KV_HEADS,))],
        name="pack",
        compiler_params=pltpu.CompilerParams(vmem_limit_bytes=KERNEL_VMEM),
    )(
        parents,
        counts,
        pltpu.with_memory_space_constraint(keys, pltpu.HBM),
        pltpu.with_memory_space_constraint(values, pltpu.HBM),
    )


def finish_kernel(mine_ref, down_ref, up_ref, out_ref):
    for head in range(KV_HEADS):
        rows = block_rows(head)
        total = mine_ref[rows, :] + (
            down_ref[rows, :].astype(F32) + up_ref[rows, :].astype(F32)
        )
        out_ref[:, head * HEAD : (head + 1) * HEAD] = total.astype(BF16)


def finish(mine, down, up):
    return on_core(
        finish_kernel,
        "finish",
        jax.ShapeDtypeStruct((SEG_LEN, KV_COLS), BF16),
        [mine, down, up],
    )


def taken(array, index, axis):
    return lax.dynamic_index_in_dim(array, index, axis, keepdims=False)


def places():
    dp = lax.axis_index("dp")
    core = lax.rem(dp, CORES)
    x = lax.rem(lax.div(dp, CORES), X)
    y = lax.div(dp, CORES * X)
    return y, x, core


def load_kernel(q_ref, g_ref, hidden_ref, *refs):
    head_refs, share_refs, (buffer, head_sems, share_sems) = refs[:4], refs[4:-3], refs[-3:]
    copies = [
        pltpu.make_async_copy(ref, buffer.at[i], head_sems.at[i])
        for i, ref in enumerate((q_ref, g_ref))
    ]
    x = places()[1]
    for k, ref in enumerate(share_refs):
        to = lax.rem(x + k, X)
        for y in range(Y):
            first = pl.multiple_of((y * X + to) * SHARE, SHARE)
            copies.append(
                pltpu.make_async_copy(
                    hidden_ref.at[:, pl.ds(first, SHARE)],
                    ref.at[:, pl.ds(y * SHARE, SHARE)],
                    share_sems.at[k * Y + y],
                )
            )
    for copy in copies:
        copy.start()
    for i in range(2):
        copies[i].wait()
        rows_ref, turned_ref = head_refs[2 * i : 2 * i + 2]

        def one_group(group):
            for head in range(GROUP):
                part = aligned(group * GROUP_COLS + head * HEAD, HEAD)
                block = buffer[i, :, part]
                rows_ref[part, :] = block
                turned_ref[:, part] = block.T

        over(KV_HEADS, one_group, looped=True)
    for copy in copies[2:]:
        copy.wait()


def loaded(array_q, array_g, hidden):
    shapes = [(KV_HEADS * GROUP * SEG_LEN, HEAD), (HEAD, KV_HEADS * GROUP * SEG_LEN)] * 2
    shapes += [(SEG_LEN, Y * SHARE)] * X
    outs = pl.pallas_call(
        load_kernel,
        out_shape=[jax.ShapeDtypeStruct(shape, BF16) for shape in shapes],
        in_specs=[pl.BlockSpec(memory_space=pltpu.HBM)] * 3,
        out_specs=[VMEM_SPEC] * len(shapes),
        scratch_shapes=[
            pltpu.VMEM((2, SEG_LEN, Q_COLS), BF16),
            pltpu.SemaphoreType.DMA((2,)),
            pltpu.SemaphoreType.DMA((X * Y,)),
        ],
        name="load",
        compiler_params=pltpu.CompilerParams(vmem_limit_bytes=KERNEL_VMEM),
    )(*[pltpu.with_memory_space_constraint(a, pltpu.HBM) for a in (array_q, array_g, hidden)])
    return outs[:4], outs[4:]


def turn_kernel(*refs):
    part_refs, out_refs = refs[:X], refs[X:]
    here, _, core = places()
    for side, out_ref in enumerate(out_refs):
        for k in range(Y):
            of = lax.rem(here + k, Y) * CORES + lax.rem(core + side, CORES)
            first = pl.multiple_of(of * HEAD, HEAD)
            for i, ref in enumerate(part_refs):
                out_ref[k * HEAD : (k + 1) * HEAD, i * SEG_LEN : (i + 1) * SEG_LEN] = ref[
                    :, pl.ds(first, HEAD)
                ].T


def turned(parts):
    return on_core(
        turn_kernel,
        "turn",
        [jax.ShapeDtypeStruct((Y * HEAD, X * SEG_LEN), BF16)] * CORES,
        list(parts),
    )


def given_kernel(hidden_ref, *refs):
    token_refs, (out_ref,) = refs[:X], refs[X:]
    tokens = jnp.concatenate([ref[...] for ref in token_refs], axis=0)
    out_ref[...] = dot_nn(hidden_ref[...], tokens).astype(BF16)


def kept_kernel(hidden_ref, *refs):
    token_refs, got_ref, own_ref, out_refs = refs[:X], refs[X], refs[X + 1], refs[X + 2 :]
    tokens = jnp.concatenate([ref[...] for ref in token_refs], axis=0)
    total = dot_nn(hidden_ref[...], tokens) + got_ref[...].astype(F32)
    own_ref[...] = total[:HEAD]
    for k, ref in enumerate(out_refs):
        ref[...] = total[(k + 1) * HEAD : (k + 2) * HEAD].astype(BF16)


def all_grads(hidden, queries, keys, values, out_grad, parents, counts):
    barrier = lax.optimization_barrier
    own = ring_packet(
        keys.reshape(SEG_LEN, KV_COLS), values.reshape(SEG_LEN, KV_COLS), parents, counts
    )
    up, down = own, own
    below, above = {}, {}
    state, stats = (parents, counts), None
    for step in range(1, 5):
        if step == 2:
            heads, shares = loaded(
                queries.reshape(SEG_LEN, Q_COLS), out_grad.reshape(SEG_LEN, Q_COLS), hidden
            )
            up, down, *rest = barrier((up, down, *heads, *shares))
            heads, shares = rest[:4], rest[4:]
            hidden_parts = [
                shift_xy(share, k, 0) if k else share for k, share in enumerate(shares)
            ]
        if step == 3:
            state, stats = add_stats(heads, [own], [], state, None)
            up, down, state, stats = barrier((up, down, state, stats))
            label = shift_seq(up[PACKET_ROWS:], 2)
            stats, hidden_parts[1] = barrier((stats, hidden_parts[1]))
        if step == 4:
            state, stats = add_stats(
                heads, [below[1], below[2]], [(1, False), (2, False)], state, stats
            )
            up, down, state, stats = barrier((up, down, state, stats))
            farthest = [shift_seq(up[:KV_COLS], 1), shift_seq(down[KV_COLS:PACKET_ROWS], -1)]
            break
        down, up = shift_seq(down, -1), shift_seq(up, 1)
        above[step], below[step] = down, up
    state, stats = add_stats(
        heads,
        [below[3], label, above[3], above[2], above[1]],
        [(3, False), (4, True), (5, False), (6, False), (7, False)],
        state,
        stats,
    )
    stats, hidden_parts[2], hidden_parts[3] = barrier(
        (stats, hidden_parts[2], hidden_parts[3])
    )
    state, stats = add_stats(heads, farthest, [(4, False)], state, stats, last=True)

    dvs = {}
    acc, dk, dvs[4] = add_grads(heads, state, stats, farthest, [4], None, [BF16] * 2)
    down, up = shift_seq(dk, -1), None
    value_up = shift_seq(dvs[4], 1)
    for step in range(3, 0, -1):
        starts = BF16 if step == 3 else F32
        acc, low, dvs[step], high, dvs[8 - step] = add_grads(
            heads,
            state,
            stats,
            [below[step], above[step]],
            [step, 8 - step],
            acc,
            [F32, starts, starts, F32],
        )
        if step == 3:
            acc, down, value_up = barrier((acc, down, value_up))
        else:
            acc, down = barrier((acc, down))
        down = (low + down.astype(F32)).astype(BF16)
        if step == 1:
            down, dvs[5] = barrier((down, dvs[5]))
        down = shift_seq(down, -1)
        up = shift_seq(high if step == 3 else (high + up.astype(F32)).astype(BF16), 1)

    def value_step(step, value_up, value_down):
        value_up = (dvs[8 - step] + value_up.astype(F32)).astype(BF16)
        value_down = (dvs[step] + value_down.astype(F32)).astype(BF16)
        return shift_seq(value_up, 1), shift_seq(value_down, -1)

    acc, value_up, *hidden_parts = barrier((acc, value_up, *turned(hidden_parts)))
    value_up = (dvs[5] + value_up.astype(F32)).astype(BF16)
    value_up, dvs[3] = barrier((value_up, dvs[3]))
    value_up, value_down = shift_seq(value_up, 1), shift_seq(dvs[3], -1)
    acc, mine, dvs[0] = add_grads(heads, state, stats, [own], [0], acc, [F32] * 2, last=True)
    near = finish(mine, down, up)
    near, dvs[2], dvs[6] = barrier((near, dvs[2], dvs[6]))
    hidden_own, hidden_other = hidden_parts
    flops = 2 * X * SEG_LEN * Y * HEAD * KV_COLS
    tokens = [near] + [shift_xy(near, k, 0) for k in range(1, X)]
    value_up, value_down = value_step(2, value_up, value_down)
    given = on_core(
        given_kernel,
        "given",
        jax.ShapeDtypeStruct((Y * HEAD, KV_COLS), BF16),
        [hidden_other, *tokens],
        flops=flops,
    )
    given, value_up, value_down = barrier((given, value_up, value_down))
    value_up, value_down = value_step(1, value_up, value_down)
    kept, *low = on_core(
        kept_kernel,
        "kept",
        [jax.ShapeDtypeStruct((HEAD, KV_COLS), F32)]
        + [jax.ShapeDtypeStruct((HEAD, KV_COLS), BF16)] * (Y - 1),
        [hidden_own, *tokens, swap_cores(given)],
        flops=flops,
    )
    others = [shift_xy(low[k - 1], 0, k) for k in range(1, Y)]
    total = kept
    for other in others:
        total = total + other.astype(F32)
    total, value_up, value_down, acc = barrier(
        (total.astype(BF16), value_up, value_down, acc)
    )
    rows = lax.all_to_all(total, "seq", 0, 0, tiled=True)
    value_grad = finish(dvs[0], value_down, value_up)
    value_grad, acc = barrier((value_grad, acc))
    dq, key_grad = on_core(
        outputs_kernel,
        "outputs",
        [jax.ShapeDtypeStruct((SEG_LEN, n), BF16) for n in (Q_COLS, KV_COLS)],
        [acc, near],
    )
    weight_grad = jnp.sum(rows.reshape(SEGMENTS, -1, KV_COLS).astype(F32), axis=0)
    return dq, key_grad, value_grad, weight_grad


def local(hidden_in, queries, keys, values, out_grad, parents, counts):
    dq, key_grad, value_grad, weight_grad = all_grads(
        hidden_in.reshape(SEG_LEN, -1), queries, keys, values, out_grad, parents, counts
    )
    return (
        dq.reshape(1, 1, SEG_LEN, Q_COLS),
        key_grad.reshape(1, 1, SEG_LEN, KV_COLS),
        value_grad.reshape(1, 1, SEG_LEN, KV_COLS),
        weight_grad,
    )


def solution(mesh):
    wide = P("dp", "seq", None, None)
    return jax.shard_map(
        local,
        mesh=mesh,
        in_specs=(wide, wide, wide, wide, wide, P("dp", "seq"), P("dp", "seq")),
        out_specs=(wide, wide, wide, P(("dp", "seq"), None)),
        check_vma=False,
    )
```

```python
import functools
import itertools
import math

import jax
import jax.numpy as jnp
from jax import lax
from jax.experimental import pallas as pl
from jax.experimental.pallas import tpu as pltpu
from jax.sharding import PartitionSpec as P

SEGMENTS = 8
SEG_LEN = 128
KV_HEADS = 4
GROUP = 8
HEAD = 128
KV_COLS = KV_HEADS * HEAD
Q_COLS = KV_HEADS * GROUP * HEAD
GROUP_COLS = GROUP * HEAD
STATS_HEADS = 2
KERNEL_VMEM = 16 << 20
SCALE = 1.0 / math.sqrt(HEAD)
SCALE_LOG2 = SCALE * math.log2(math.e)
NEG_FILL = -1e30
DEAD_LSE = 1e30
LABEL_ROWS = 16
PACKET_ROWS = 2 * KV_HEADS * SEG_LEN
STATE = 16
BF16 = jnp.bfloat16
F32 = jnp.float32

X, Y, CORES = 4, 4, 2
SHARE = CORES * HEAD


def dot_nt(a, b):
    return lax.dot_general(a, b, (((1,), (1,)), ((), ())), preferred_element_type=F32)


def dot_nn(a, b):
    return lax.dot_general(a, b, (((1,), (0,)), ((), ())), preferred_element_type=F32)


def dot_tn(a, b):
    return lax.dot_general(a, b, (((0,), (0,)), ((), ())), preferred_element_type=F32)


def key_bias(live):
    position = lax.broadcasted_iota(jnp.int32, (SEG_LEN, 1), 0)
    return jnp.where(position < live, 0.0, NEG_FILL).astype(F32)


def own_bias(live, heads):
    key_at = lax.broadcasted_iota(jnp.int32, (SEG_LEN, SEG_LEN), 0)
    query_at = lax.broadcasted_iota(jnp.int32, (SEG_LEN, SEG_LEN), 1)
    tile = jnp.where((key_at <= query_at) & (key_at < live), 0.0, NEG_FILL).astype(F32)
    return jnp.concatenate([tile] * heads, axis=1)


def aligned(start, size):
    return pl.ds(start if isinstance(start, int) else pl.multiple_of(start, size), size)


def block_rows(group, first=0):
    return aligned(first + group * SEG_LEN, SEG_LEN)


def key_value(refs, group):
    k_ref, v_ref = refs[0], refs[-1]
    first = KV_COLS if len(refs) == 1 else 0
    return k_ref[block_rows(group), :], v_ref[block_rows(group, first), :]


def group_cols(group):
    return aligned(group * GROUP_COLS, GROUP_COLS)


def over(count, body, looped):
    if looped:

        def step(i, carry):
            body(i)
            return carry

        lax.fori_loop(0, count, step, 0)
    else:
        for i in range(count):
            body(i)


def scalar_of(rows):
    return jnp.max(rows.astype(F32)).astype(jnp.int32)


def state_value(ref, index):
    return scalar_of(ref[pl.ds(index, 1), :])


def set_state(ref, index, value):
    ref[pl.ds(index, 1), :] = jnp.full((1, HEAD), value, jnp.int32).astype(F32)


def stats_kernel(steps, first, last, *refs):
    if first:
        parent_ref, count_ref, q_ref, g_ref, packet_ref, out_ref, state_ref = refs
    else:
        q_ref, g_ref = refs[:2]
        packet_refs = refs[2:-4]
        in_ref, old_ref, out_ref, state_ref = refs[-4:]
    me = lax.axis_index("seq")

    def add_segment(packet, bias, start):
        width = STATS_HEADS * HEAD

        def one_group(group):
            k, v = key_value(packet, group)
            for chunk in range(GROUP_COLS // width):
                cols = aligned(group * GROUP_COLS + chunk * width, width)
                scores = dot_nn(k, q_ref[:, cols]) * SCALE_LOG2 + bias
                grad_probs = dot_nn(v, g_ref[:, cols])
                top = jnp.max(scores, axis=0, keepdims=True)
                if not start:
                    old_top = out_ref[0:1, cols]
                    top = jnp.maximum(top, old_top)
                weights = jnp.exp2(scores - top)
                total = jnp.sum(weights, axis=0, keepdims=True)
                mixed = jnp.sum(weights * grad_probs, axis=0, keepdims=True)
                if not start:
                    shrink = jnp.exp2(old_top - top)
                    total = total + out_ref[1:2, cols] * shrink
                    mixed = mixed + out_ref[2:3, cols] * shrink
                out_ref[0:1, cols] = top
                out_ref[1:2, cols] = total
                out_ref[2:3, cols] = mixed

        over(KV_HEADS, one_group, looped=start)

    if first:
        live = count_ref[0, 0]
        state_ref[...] = jnp.zeros_like(state_ref)
        set_state(state_ref, 0, parent_ref[0, 0])
        set_state(state_ref, SEGMENTS, live)
        add_segment([packet_ref], own_bias(live, STATS_HEADS), True)
    else:
        state_ref[...] = old_ref[...]
        out_ref[...] = in_ref[...]
        if last:
            ((distance, _),) = steps
            live_there = state_value(old_ref, distance)

            @pl.when(live_there > 0)
            def _():
                add_segment(packet_refs, key_bias(live_there), False)

        else:
            current = state_value(old_ref, 0)
            for packet_ref, (distance, looked_up) in zip(packet_refs, steps):
                top_row = packet_ref.shape[0] - LABEL_ROWS
                hit = current == me - distance
                parent = scalar_of(packet_ref[top_row:, :][: LABEL_ROWS // 2])
                current = jnp.where(hit, parent, current)

                @pl.when(hit)
                def _():
                    live = scalar_of(packet_ref[top_row:, :][LABEL_ROWS // 2 :])
                    set_state(state_ref, distance, live)
                    if not looked_up:
                        add_segment([packet_ref], key_bias(live), False)

            set_state(state_ref, 0, current)

    if last:
        live = state_value(old_ref, SEGMENTS)
        position = lax.broadcasted_iota(jnp.int32, (1, Q_COLS), 1) & (SEG_LEN - 1)
        total = out_ref[1:2, :]
        row_delta = out_ref[2:3, :] / total
        lse = out_ref[0:1, :] + jnp.log2(total)
        out_ref[0:1, :] = jnp.where(position < live, lse, DEAD_LSE)
        out_ref[1:2, :] = row_delta


def grads_kernel(distances, first, last, *refs):
    state_ref, q_ref, qt_ref, g_ref, gt_ref, stats_ref = refs[:6]
    count = 2 if first else len(distances)
    arrays, rest = refs[6 : 6 + count], refs[6 + count :]
    packets = [arrays] if first else [[ref] for ref in arrays]
    if first:
        in_ref, (acc_ref, *out_refs) = None, rest
    else:
        in_ref, acc_ref, *out_refs = rest

    def run(segments):
        def one_group(group):
            blocks = [key_value(packet, group) for packet, _, _ in segments]
            k = jnp.concatenate([block[0] for block in blocks], axis=0)
            v = jnp.concatenate([block[1] for block in blocks], axis=0)
            bias = jnp.concatenate([bias for _, bias, _ in segments], axis=0)
            cols = group_cols(group)
            scores = dot_nn(k, qt_ref[:, cols]) * SCALE_LOG2 + bias
            probs = jnp.exp2(scores - stats_ref[0:1, cols])
            grad_probs = dot_nn(v, gt_ref[:, cols])
            grad_scores = (probs * (grad_probs - stats_ref[1:2, cols])).astype(BF16)
            dv = dot_nn(probs.astype(BF16), g_ref[cols, :])
            dk = dot_nn(grad_scores, q_ref[cols, :]) * SCALE
            dq = dot_nn(k.T, grad_scores)
            if in_ref is not None:
                dq = dq + in_ref[:, cols]
            acc_ref[:, cols] = dq
            for i, (_, _, (dk_ref, dv_ref)) in enumerate(segments):
                part = slice(i * SEG_LEN, (i + 1) * SEG_LEN)
                dk_ref[block_rows(group), :] = dk[part].astype(dk_ref.dtype)
                dv_ref[block_rows(group), :] = dv[part].astype(dv_ref.dtype)

        over(KV_HEADS, one_group, looped=len(segments) == 1 and not (first or last))

    if last:
        bias = own_bias(state_value(state_ref, SEGMENTS), GROUP)
        run([(packets[0], bias, out_refs)])
        return
    lives = [state_value(state_ref, distance) for distance in distances]
    outs = [out_refs[2 * i : 2 * i + 2] for i in range(len(distances))]
    for chosen in itertools.product((False, True), repeat=len(distances)):
        taken_here = functools.reduce(
            jnp.logical_and,
            [(live > 0) if choice else (live == 0) for live, choice in zip(lives, chosen)],
        )

        @pl.when(taken_here)
        def _():
            for choice, pair in zip(chosen, outs):
                if not choice:
                    for ref in pair:
                        ref[...] = jnp.zeros_like(ref)
            if any(chosen):
                run(
                    [
                        (packet, key_bias(live), pair)
                        for packet, live, pair, choice in zip(packets, lives, outs, chosen)
                        if choice
                    ]
                )
            elif in_ref is None:
                acc_ref[...] = jnp.zeros_like(acc_ref)
            else:
                acc_ref[...] = in_ref[...]


def outputs_kernel(acc_ref, near_ref, query_ref, key_ref):
    def one_group(group):
        for head in range(GROUP):
            part = aligned(group * GROUP_COLS + head * HEAD, HEAD)
            query_ref[:, part] = (acc_ref[:, part] * SCALE).T.astype(BF16)

    over(KV_HEADS, one_group, looped=True)
    key_ref[...] = near_ref[...]


SMEM_SPEC = pl.BlockSpec(memory_space=pltpu.SMEM)
VMEM_SPEC = pl.BlockSpec(memory_space=pltpu.VMEM)
STATS_SHAPE = jax.ShapeDtypeStruct((8, Q_COLS), F32)
STATE_SHAPE = jax.ShapeDtypeStruct((STATE, HEAD), F32)
BLOCK_FLOPS = 2 * SEG_LEN * SEG_LEN * HEAD * KV_HEADS * GROUP


def on_core(kernel, name, out_shape, operands, scalars=0, out_specs=None, flops=0, aliases=None):
    many = isinstance(out_shape, list)
    if out_specs is None:
        out_specs = [VMEM_SPEC] * len(out_shape) if many else VMEM_SPEC
    moved = sum(o.size * o.dtype.itemsize for o in operands)
    return pl.pallas_call(
        kernel,
        out_shape=out_shape,
        in_specs=[SMEM_SPEC] * scalars + [VMEM_SPEC] * (len(operands) - scalars),
        out_specs=out_specs,
        name=name,
        input_output_aliases=aliases or {},
        cost_estimate=pl.CostEstimate(flops=flops, bytes_accessed=moved, transcendentals=0),
        compiler_params=pltpu.CompilerParams(vmem_limit_bytes=KERNEL_VMEM),
    )(*operands)


def add_stats(heads, packets, steps, state, stats, last=False):
    _, qt, _, gt = heads
    first = stats is None
    if first:
        operands = [*state, qt, gt, *packets]
    else:
        operands = [qt, gt, *packets, stats, state]
    stats, state = on_core(
        functools.partial(stats_kernel, tuple(steps), first, last),
        "stats",
        [STATS_SHAPE, STATE_SHAPE],
        operands,
        scalars=len(state) if first else 0,
        flops=4 * BLOCK_FLOPS * len(packets),
    )
    return state, stats


def add_grads(heads, state, stats, packets, distances, acc, dtypes, last=False):
    first = acc is None
    operands = [state, *heads, stats, *packets]
    aliases = {}
    if not first:
        aliases = {len(operands): 0}
        operands.append(acc)
    out_shapes = [jax.ShapeDtypeStruct((HEAD, Q_COLS), F32)]
    out_shapes += [jax.ShapeDtypeStruct((KV_COLS, HEAD), dtype) for dtype in dtypes]
    return on_core(
        functools.partial(grads_kernel, tuple(distances), first, last),
        "grads",
        out_shapes,
        operands,
        flops=10 * BLOCK_FLOPS * len(distances),
        aliases=aliases,
    )


def shift_seq(array, k):
    return lax.ppermute(array, "seq", [(i, (i + k) % SEGMENTS) for i in range(SEGMENTS)])


def swap_cores(array):
    return lax.ppermute(array, "dp", [(i, i ^ 1) for i in range(X * Y * CORES)])


def dp_index(y, x, core):
    return (y % Y * X + x % X) * CORES + core


def shift_xy(array, along_x, along_y):
    pairs = [
        (dp_index(y, x, c), dp_index(y + along_y, x + along_x, c))
        for y in range(Y)
        for x in range(X)
        for c in range(CORES)
    ]
    return lax.ppermute(array, "dp", pairs)


def pack_kernel(parent_ref, count_ref, k_ref, v_ref, out_ref, sems):
    copies = []
    for head in range(KV_HEADS):
        for side, ref in enumerate((k_ref, v_ref)):
            copies.append(
                pltpu.make_async_copy(
                    ref.at[:, pl.ds(head * HEAD, HEAD)],
                    out_ref.at[pl.ds((side * KV_HEADS + head) * SEG_LEN, SEG_LEN), :],
                    sems.at[2 * head + side],
                )
            )
    for copy in copies:
        copy.start()
    row = lax.broadcasted_iota(jnp.int32, (LABEL_ROWS, HEAD), 0)
    labels = jnp.where(row < LABEL_ROWS // 2, parent_ref[0, 0], count_ref[0, 0])
    out_ref[PACKET_ROWS:, :] = labels.astype(F32).astype(BF16)
    for copy in copies:
        copy.wait()


def ring_packet(keys, values, parents, counts):
    return pl.pallas_call(
        pack_kernel,
        out_shape=jax.ShapeDtypeStruct((PACKET_ROWS + LABEL_ROWS, HEAD), BF16),
        in_specs=[SMEM_SPEC, SMEM_SPEC] + [pl.BlockSpec(memory_space=pltpu.HBM)] * 2,
        out_specs=VMEM_SPEC,
        scratch_shapes=[pltpu.SemaphoreType.DMA((2 * KV_HEADS,))],
        name="pack",
        compiler_params=pltpu.CompilerParams(vmem_limit_bytes=KERNEL_VMEM),
    )(
        parents,
        counts,
        pltpu.with_memory_space_constraint(keys, pltpu.HBM),
        pltpu.with_memory_space_constraint(values, pltpu.HBM),
    )


def finish_kernel(mine_ref, down_ref, up_ref, out_ref):
    for head in range(KV_HEADS):
        rows = block_rows(head)
        total = mine_ref[rows, :] + (
            down_ref[rows, :].astype(F32) + up_ref[rows, :].astype(F32)
        )
        out_ref[:, head * HEAD : (head + 1) * HEAD] = total.astype(BF16)


def finish(mine, down, up):
    return on_core(
        finish_kernel,
        "finish",
        jax.ShapeDtypeStruct((SEG_LEN, KV_COLS), BF16),
        [mine, down, up],
    )


def taken(array, index, axis):
    return lax.dynamic_index_in_dim(array, index, axis, keepdims=False)


def places():
    dp = lax.axis_index("dp")
    core = lax.rem(dp, CORES)
    x = lax.rem(lax.div(dp, CORES), X)
    y = lax.div(dp, CORES * X)
    return y, x, core


def load_kernel(q_ref, g_ref, hidden_ref, *refs):
    head_refs, share_refs, (buffer, head_sems, share_sems) = refs[:4], refs[4:-3], refs[-3:]
    copies = [
        pltpu.make_async_copy(ref, buffer.at[i], head_sems.at[i])
        for i, ref in enumerate((q_ref, g_ref))
    ]
    x = places()[1]
    for k, ref in enumerate(share_refs):
        to = lax.rem(x + k, X)
        for y in range(Y):
            first = pl.multiple_of((y * X + to) * SHARE, SHARE)
            copies.append(
                pltpu.make_async_copy(
                    hidden_ref.at[:, pl.ds(first, SHARE)],
                    ref.at[:, pl.ds(y * SHARE, SHARE)],
                    share_sems.at[k * Y + y],
                )
            )
    for copy in copies:
        copy.start()
    for i in range(2):
        copies[i].wait()
        rows_ref, turned_ref = head_refs[2 * i : 2 * i + 2]

        def one_group(group):
            for head in range(GROUP):
                part = aligned(group * GROUP_COLS + head * HEAD, HEAD)
                block = buffer[i, :, part]
                rows_ref[part, :] = block
                turned_ref[:, part] = block.T

        over(KV_HEADS, one_group, looped=True)
    for copy in copies[2:]:
        copy.wait()


def loaded(array_q, array_g, hidden):
    shapes = [(KV_HEADS * GROUP * SEG_LEN, HEAD), (HEAD, KV_HEADS * GROUP * SEG_LEN)] * 2
    shapes += [(SEG_LEN, Y * SHARE)] * X
    outs = pl.pallas_call(
        load_kernel,
        out_shape=[jax.ShapeDtypeStruct(shape, BF16) for shape in shapes],
        in_specs=[pl.BlockSpec(memory_space=pltpu.HBM)] * 3,
        out_specs=[VMEM_SPEC] * len(shapes),
        scratch_shapes=[
            pltpu.VMEM((2, SEG_LEN, Q_COLS), BF16),
            pltpu.SemaphoreType.DMA((2,)),
            pltpu.SemaphoreType.DMA((X * Y,)),
        ],
        name="load",
        compiler_params=pltpu.CompilerParams(vmem_limit_bytes=KERNEL_VMEM),
    )(*[pltpu.with_memory_space_constraint(a, pltpu.HBM) for a in (array_q, array_g, hidden)])
    return outs[:4], outs[4:]


def turn_kernel(*refs):
    part_refs, out_refs = refs[:X], refs[X:]
    here, _, core = places()
    for side, out_ref in enumerate(out_refs):
        for k in range(Y):
            of = lax.rem(here + k, Y) * CORES + lax.rem(core + side, CORES)
            first = pl.multiple_of(of * HEAD, HEAD)
            for i, ref in enumerate(part_refs):
                out_ref[k * HEAD : (k + 1) * HEAD, i * SEG_LEN : (i + 1) * SEG_LEN] = ref[
                    :, pl.ds(first, HEAD)
                ].T


def turned(parts):
    return on_core(
        turn_kernel,
        "turn",
        [jax.ShapeDtypeStruct((Y * HEAD, X * SEG_LEN), BF16)] * CORES,
        list(parts),
    )


def given_kernel(hidden_ref, *refs):
    token_refs, (out_ref,) = refs[:X], refs[X:]
    tokens = jnp.concatenate([ref[...] for ref in token_refs], axis=0)
    out_ref[...] = dot_nn(hidden_ref[...], tokens).astype(BF16)


def kept_kernel(hidden_ref, *refs):
    token_refs, got_ref, own_ref, out_refs = refs[:X], refs[X], refs[X + 1], refs[X + 2 :]
    tokens = jnp.concatenate([ref[...] for ref in token_refs], axis=0)
    total = dot_nn(hidden_ref[...], tokens) + got_ref[...].astype(F32)
    own_ref[...] = total[:HEAD]
    for k, ref in enumerate(out_refs):
        ref[...] = total[(k + 1) * HEAD : (k + 2) * HEAD].astype(BF16)


def all_grads(hidden, queries, keys, values, out_grad, parents, counts):
    barrier = lax.optimization_barrier
    own = ring_packet(
        keys.reshape(SEG_LEN, KV_COLS), values.reshape(SEG_LEN, KV_COLS), parents, counts
    )
    up, down = own, own
    below, above = {}, {}
    state, stats = (parents, counts), None
    for step in range(1, 5):
        if step == 2:
            heads, shares = loaded(
                queries.reshape(SEG_LEN, Q_COLS), out_grad.reshape(SEG_LEN, Q_COLS), hidden
            )
            up, down, *rest = barrier((up, down, *heads, *shares))
            heads, shares = rest[:4], rest[4:]
            hidden_parts = [
                shift_xy(share, k, 0) if k else share for k, share in enumerate(shares)
            ]
        if step == 3:
            state, stats = add_stats(heads, [own], [], state, None)
            up, down, state, stats = barrier((up, down, state, stats))
            label = shift_seq(up[PACKET_ROWS:], 2)
            stats, hidden_parts[1] = barrier((stats, hidden_parts[1]))
        if step == 4:
            state, stats = add_stats(
                heads, [below[1], below[2]], [(1, False), (2, False)], state, stats
            )
            up, down, state, stats = barrier((up, down, state, stats))
            farthest = [shift_seq(up[:KV_COLS], 1), shift_seq(down[KV_COLS:PACKET_ROWS], -1)]
            break
        down, up = shift_seq(down, -1), shift_seq(up, 1)
        above[step], below[step] = down, up
    state, stats = add_stats(
        heads,
        [below[3], label, above[3], above[2], above[1]],
        [(3, False), (4, True), (5, False), (6, False), (7, False)],
        state,
        stats,
    )
    stats, hidden_parts[2], hidden_parts[3] = barrier(
        (stats, hidden_parts[2], hidden_parts[3])
    )
    state, stats = add_stats(heads, farthest, [(4, False)], state, stats, last=True)

    dvs = {}
    acc, dk, dvs[4] = add_grads(heads, state, stats, farthest, [4], None, [BF16] * 2)
    down, up = shift_seq(dk, -1), None
    for step in range(3, 0, -1):
        starts = BF16 if step == 3 else F32
        acc, low, dvs[step], high, dvs[8 - step] = add_grads(
            heads,
            state,
            stats,
            [below[step], above[step]],
            [step, 8 - step],
            acc,
            [F32, starts, starts, F32],
        )
        acc, down = barrier((acc, down))
        down = shift_seq((low + down.astype(F32)).astype(BF16), -1)
        up = shift_seq(high if step == 3 else (high + up.astype(F32)).astype(BF16), 1)
    acc, *hidden_parts = barrier((acc, *turned(hidden_parts)))
    value_up = shift_seq(dvs[4], 1)
    acc, mine, dvs[0] = add_grads(heads, state, stats, [own], [0], acc, [F32] * 2, last=True)
    near = finish(mine, down, up)
    near, dvs[3], dvs[5] = barrier((near, dvs[3], dvs[5]))

    def value_step(step, value_up, value_down):
        value_up = (dvs[8 - step] + value_up.astype(F32)).astype(BF16)
        if value_down is None:
            value_down = dvs[step]
        else:
            value_down = (dvs[step] + value_down.astype(F32)).astype(BF16)
        return shift_seq(value_up, 1), shift_seq(value_down, -1)

    hidden_own, hidden_other = hidden_parts
    flops = 2 * X * SEG_LEN * Y * HEAD * KV_COLS
    tokens = [near] + [shift_xy(near, k, 0) for k in range(1, X)]
    value_up, value_down = value_step(3, value_up, None)
    given = on_core(
        given_kernel,
        "given",
        jax.ShapeDtypeStruct((Y * HEAD, KV_COLS), BF16),
        [hidden_other, *tokens],
        flops=flops,
    )
    given, value_up, value_down = barrier((given, value_up, value_down))
    value_up, value_down = value_step(2, value_up, value_down)
    kept, *low = on_core(
        kept_kernel,
        "kept",
        [jax.ShapeDtypeStruct((HEAD, KV_COLS), F32)]
        + [jax.ShapeDtypeStruct((HEAD, KV_COLS), BF16)] * (Y - 1),
        [hidden_own, *tokens, swap_cores(given)],
        flops=flops,
    )
    *low, dvs[1], dvs[7] = barrier((*low, dvs[1], dvs[7]))
    others = [shift_xy(low[k - 1], 0, k) for k in range(1, Y)]
    value_up, value_down = value_step(1, value_up, value_down)
    total = kept
    for other in others:
        total = total + other.astype(F32)
    total, value_up, value_down, acc = barrier(
        (total.astype(BF16), value_up, value_down, acc)
    )
    rows = lax.all_to_all(total, "seq", 0, 0, tiled=True)
    value_grad = finish(dvs[0], value_down, value_up)
    value_grad, acc = barrier((value_grad, acc))
    dq, key_grad = on_core(
        outputs_kernel,
        "outputs",
        [jax.ShapeDtypeStruct((SEG_LEN, n), BF16) for n in (Q_COLS, KV_COLS)],
        [acc, near],
    )
    weight_grad = jnp.sum(rows.reshape(SEGMENTS, -1, KV_COLS).astype(F32), axis=0)
    return dq, key_grad, value_grad, weight_grad


def local(hidden_in, queries, keys, values, out_grad, parents, counts):
    dq, key_grad, value_grad, weight_grad = all_grads(
        hidden_in.reshape(SEG_LEN, -1), queries, keys, values, out_grad, parents, counts
    )
    return (
        dq.reshape(1, 1, SEG_LEN, Q_COLS),
        key_grad.reshape(1, 1, SEG_LEN, KV_COLS),
        value_grad.reshape(1, 1, SEG_LEN, KV_COLS),
        weight_grad,
    )


def solution(mesh):
    wide = P("dp", "seq", None, None)
    return jax.shard_map(
        local,
        mesh=mesh,
        in_specs=(wide, wide, wide, wide, wide, P("dp", "seq"), P("dp", "seq")),
        out_specs=(wide, wide, wide, P(("dp", "seq"), None)),
        check_vma=False,
    )
```

```python
import functools
import itertools
import math

import jax
import jax.numpy as jnp
from jax import lax
from jax.experimental import pallas as pl
from jax.experimental.pallas import tpu as pltpu
from jax.sharding import PartitionSpec as P

SEGMENTS = 8
SEG_LEN = 128
KV_HEADS = 4
GROUP = 8
HEAD = 128
KV_COLS = KV_HEADS * HEAD
Q_COLS = KV_HEADS * GROUP * HEAD
GROUP_COLS = GROUP * HEAD
STATS_HEADS = 2
KERNEL_VMEM = 16 << 20
SCALE = 1.0 / math.sqrt(HEAD)
SCALE_LOG2 = SCALE * math.log2(math.e)
NEG_FILL = -1e30
DEAD_LSE = 1e30
LABEL_ROWS = 16
PACKET_ROWS = 2 * KV_HEADS * SEG_LEN
STATE = 16
BF16 = jnp.bfloat16
F32 = jnp.float32

X, Y, CORES = 4, 4, 2
SHARE = CORES * HEAD


def dot_nt(a, b):
    return lax.dot_general(a, b, (((1,), (1,)), ((), ())), preferred_element_type=F32)


def dot_nn(a, b):
    return lax.dot_general(a, b, (((1,), (0,)), ((), ())), preferred_element_type=F32)


def dot_tn(a, b):
    return lax.dot_general(a, b, (((0,), (0,)), ((), ())), preferred_element_type=F32)


def key_bias(live):
    position = lax.broadcasted_iota(jnp.int32, (SEG_LEN, 1), 0)
    return jnp.where(position < live, 0.0, NEG_FILL).astype(F32)


def own_bias(live, heads):
    key_at = lax.broadcasted_iota(jnp.int32, (SEG_LEN, SEG_LEN), 0)
    query_at = lax.broadcasted_iota(jnp.int32, (SEG_LEN, SEG_LEN), 1)
    tile = jnp.where((key_at <= query_at) & (key_at < live), 0.0, NEG_FILL).astype(F32)
    return jnp.concatenate([tile] * heads, axis=1)


def aligned(start, size):
    return pl.ds(start if isinstance(start, int) else pl.multiple_of(start, size), size)


def block_rows(group, first=0):
    return aligned(first + group * SEG_LEN, SEG_LEN)


def key_value(refs, group):
    k_ref, v_ref = refs[0], refs[-1]
    first = KV_COLS if len(refs) == 1 else 0
    return k_ref[block_rows(group), :], v_ref[block_rows(group, first), :]


def group_cols(group):
    return aligned(group * GROUP_COLS, GROUP_COLS)


def over(count, body, looped):
    if looped:

        def step(i, carry):
            body(i)
            return carry

        lax.fori_loop(0, count, step, 0)
    else:
        for i in range(count):
            body(i)


def scalar_of(rows):
    return jnp.max(rows.astype(F32)).astype(jnp.int32)


def state_value(ref, index):
    return scalar_of(ref[pl.ds(index, 1), :])


def set_state(ref, index, value):
    ref[pl.ds(index, 1), :] = jnp.full((1, HEAD), value, jnp.int32).astype(F32)


def stats_kernel(steps, first, last, *refs):
    if first:
        parent_ref, count_ref, q_ref, g_ref, packet_ref, out_ref, state_ref = refs
    else:
        q_ref, g_ref = refs[:2]
        packet_refs = refs[2:-4]
        in_ref, old_ref, out_ref, state_ref = refs[-4:]
    me = lax.axis_index("seq")

    def add_segment(packet, bias, start):
        width = STATS_HEADS * HEAD

        def one_group(group):
            k, v = key_value(packet, group)
            for chunk in range(GROUP_COLS // width):
                cols = aligned(group * GROUP_COLS + chunk * width, width)
                scores = dot_nn(k, q_ref[:, cols]) * SCALE_LOG2 + bias
                grad_probs = dot_nn(v, g_ref[:, cols])
                top = jnp.max(scores, axis=0, keepdims=True)
                if not start:
                    old_top = out_ref[0:1, cols]
                    top = jnp.maximum(top, old_top)
                weights = jnp.exp2(scores - top)
                total = jnp.sum(weights, axis=0, keepdims=True)
                mixed = jnp.sum(weights * grad_probs, axis=0, keepdims=True)
                if not start:
                    shrink = jnp.exp2(old_top - top)
                    total = total + out_ref[1:2, cols] * shrink
                    mixed = mixed + out_ref[2:3, cols] * shrink
                out_ref[0:1, cols] = top
                out_ref[1:2, cols] = total
                out_ref[2:3, cols] = mixed

        over(KV_HEADS, one_group, looped=start)

    if first:
        live = count_ref[0, 0]
        state_ref[...] = jnp.zeros_like(state_ref)
        set_state(state_ref, 0, parent_ref[0, 0])
        set_state(state_ref, SEGMENTS, live)
        add_segment([packet_ref], own_bias(live, STATS_HEADS), True)
    else:
        state_ref[...] = old_ref[...]
        out_ref[...] = in_ref[...]
        if last:
            ((distance, _),) = steps
            live_there = state_value(old_ref, distance)

            @pl.when(live_there > 0)
            def _():
                add_segment(packet_refs, key_bias(live_there), False)

        else:
            current = state_value(old_ref, 0)
            for packet_ref, (distance, looked_up) in zip(packet_refs, steps):
                top_row = packet_ref.shape[0] - LABEL_ROWS
                hit = current == me - distance
                parent = scalar_of(packet_ref[top_row:, :][: LABEL_ROWS // 2])
                current = jnp.where(hit, parent, current)

                @pl.when(hit)
                def _():
                    live = scalar_of(packet_ref[top_row:, :][LABEL_ROWS // 2 :])
                    set_state(state_ref, distance, live)
                    if not looked_up:
                        add_segment([packet_ref], key_bias(live), False)

            set_state(state_ref, 0, current)

    if last:
        live = state_value(old_ref, SEGMENTS)
        position = lax.broadcasted_iota(jnp.int32, (1, Q_COLS), 1) & (SEG_LEN - 1)
        total = out_ref[1:2, :]
        row_delta = out_ref[2:3, :] / total
        lse = out_ref[0:1, :] + jnp.log2(total)
        out_ref[0:1, :] = jnp.where(position < live, lse, DEAD_LSE)
        out_ref[1:2, :] = row_delta


def grads_kernel(distances, first, last, *refs):
    state_ref, q_ref, qt_ref, g_ref, gt_ref, stats_ref = refs[:6]
    count = 2 if first else len(distances)
    arrays, rest = refs[6 : 6 + count], refs[6 + count :]
    packets = [arrays] if first else [[ref] for ref in arrays]
    if first:
        in_ref, (acc_ref, *out_refs) = None, rest
    else:
        in_ref, acc_ref, *out_refs = rest

    def run(segments):
        def one_group(group):
            blocks = [key_value(packet, group) for packet, _, _ in segments]
            k = jnp.concatenate([block[0] for block in blocks], axis=0)
            v = jnp.concatenate([block[1] for block in blocks], axis=0)
            bias = jnp.concatenate([bias for _, bias, _ in segments], axis=0)
            cols = group_cols(group)
            scores = dot_nn(k, qt_ref[:, cols]) * SCALE_LOG2 + bias
            probs = jnp.exp2(scores - stats_ref[0:1, cols])
            grad_probs = dot_nn(v, gt_ref[:, cols])
            grad_scores = (probs * (grad_probs - stats_ref[1:2, cols])).astype(BF16)
            dv = dot_nn(probs.astype(BF16), g_ref[cols, :])
            dk = dot_nn(grad_scores, q_ref[cols, :]) * SCALE
            dq = dot_nn(k.T, grad_scores)
            if in_ref is not None:
                dq = dq + in_ref[:, cols]
            acc_ref[:, cols] = dq
            for i, (_, _, (dk_ref, dv_ref)) in enumerate(segments):
                part = slice(i * SEG_LEN, (i + 1) * SEG_LEN)
                dk_ref[block_rows(group), :] = dk[part].astype(dk_ref.dtype)
                dv_ref[block_rows(group), :] = dv[part].astype(dv_ref.dtype)

        over(KV_HEADS, one_group, looped=len(segments) == 1)

    if last:
        bias = own_bias(state_value(state_ref, SEGMENTS), GROUP)
        run([(packets[0], bias, out_refs)])
        return
    lives = [state_value(state_ref, distance) for distance in distances]
    outs = [out_refs[2 * i : 2 * i + 2] for i in range(len(distances))]
    for chosen in itertools.product((False, True), repeat=len(distances)):
        taken_here = functools.reduce(
            jnp.logical_and,
            [(live > 0) if choice else (live == 0) for live, choice in zip(lives, chosen)],
        )

        @pl.when(taken_here)
        def _():
            for choice, pair in zip(chosen, outs):
                if not choice:
                    for ref in pair:
                        ref[...] = jnp.zeros_like(ref)
            if any(chosen):
                run(
                    [
                        (packet, key_bias(live), pair)
                        for packet, live, pair, choice in zip(packets, lives, outs, chosen)
                        if choice
                    ]
                )
            elif in_ref is None:
                acc_ref[...] = jnp.zeros_like(acc_ref)
            else:
                acc_ref[...] = in_ref[...]


def outputs_kernel(acc_ref, near_ref, query_ref, key_ref):
    def one_group(group):
        for head in range(GROUP):
            part = aligned(group * GROUP_COLS + head * HEAD, HEAD)
            query_ref[:, part] = (acc_ref[:, part] * SCALE).T.astype(BF16)

    over(KV_HEADS, one_group, looped=True)
    key_ref[...] = near_ref[...]


SMEM_SPEC = pl.BlockSpec(memory_space=pltpu.SMEM)
VMEM_SPEC = pl.BlockSpec(memory_space=pltpu.VMEM)
STATS_SHAPE = jax.ShapeDtypeStruct((8, Q_COLS), F32)
STATE_SHAPE = jax.ShapeDtypeStruct((STATE, HEAD), F32)
BLOCK_FLOPS = 2 * SEG_LEN * SEG_LEN * HEAD * KV_HEADS * GROUP


def on_core(kernel, name, out_shape, operands, scalars=0, out_specs=None, flops=0, aliases=None):
    many = isinstance(out_shape, list)
    if out_specs is None:
        out_specs = [VMEM_SPEC] * len(out_shape) if many else VMEM_SPEC
    moved = sum(o.size * o.dtype.itemsize for o in operands)
    return pl.pallas_call(
        kernel,
        out_shape=out_shape,
        in_specs=[SMEM_SPEC] * scalars + [VMEM_SPEC] * (len(operands) - scalars),
        out_specs=out_specs,
        name=name,
        input_output_aliases=aliases or {},
        cost_estimate=pl.CostEstimate(flops=flops, bytes_accessed=moved, transcendentals=0),
        compiler_params=pltpu.CompilerParams(vmem_limit_bytes=KERNEL_VMEM),
    )(*operands)


def add_stats(heads, packets, steps, state, stats, last=False):
    _, qt, _, gt = heads
    first = stats is None
    if first:
        operands = [*state, qt, gt, *packets]
    else:
        operands = [qt, gt, *packets, stats, state]
    stats, state = on_core(
        functools.partial(stats_kernel, tuple(steps), first, last),
        "stats",
        [STATS_SHAPE, STATE_SHAPE],
        operands,
        scalars=len(state) if first else 0,
        flops=4 * BLOCK_FLOPS * len(packets),
    )
    return state, stats


def add_grads(heads, state, stats, packets, distances, acc, dtypes, last=False):
    first = acc is None
    operands = [state, *heads, stats, *packets]
    aliases = {}
    if not first:
        aliases = {len(operands): 0}
        operands.append(acc)
    out_shapes = [jax.ShapeDtypeStruct((HEAD, Q_COLS), F32)]
    out_shapes += [jax.ShapeDtypeStruct((KV_COLS, HEAD), dtype) for dtype in dtypes]
    return on_core(
        functools.partial(grads_kernel, tuple(distances), first, last),
        "grads",
        out_shapes,
        operands,
        flops=10 * BLOCK_FLOPS * len(distances),
        aliases=aliases,
    )


def shift_seq(array, k):
    return lax.ppermute(array, "seq", [(i, (i + k) % SEGMENTS) for i in range(SEGMENTS)])


def swap_cores(array):
    return lax.ppermute(array, "dp", [(i, i ^ 1) for i in range(X * Y * CORES)])


def dp_index(y, x, core):
    return (y % Y * X + x % X) * CORES + core


def shift_xy(array, along_x, along_y):
    pairs = [
        (dp_index(y, x, c), dp_index(y + along_y, x + along_x, c))
        for y in range(Y)
        for x in range(X)
        for c in range(CORES)
    ]
    return lax.ppermute(array, "dp", pairs)


def pack_kernel(parent_ref, count_ref, k_ref, v_ref, out_ref, sems):
    copies = []
    for head in range(KV_HEADS):
        for side, ref in enumerate((k_ref, v_ref)):
            copies.append(
                pltpu.make_async_copy(
                    ref.at[:, pl.ds(head * HEAD, HEAD)],
                    out_ref.at[pl.ds((side * KV_HEADS + head) * SEG_LEN, SEG_LEN), :],
                    sems.at[2 * head + side],
                )
            )
    for copy in copies:
        copy.start()
    row = lax.broadcasted_iota(jnp.int32, (LABEL_ROWS, HEAD), 0)
    labels = jnp.where(row < LABEL_ROWS // 2, parent_ref[0, 0], count_ref[0, 0])
    out_ref[PACKET_ROWS:, :] = labels.astype(F32).astype(BF16)
    for copy in copies:
        copy.wait()


def ring_packet(keys, values, parents, counts):
    return pl.pallas_call(
        pack_kernel,
        out_shape=jax.ShapeDtypeStruct((PACKET_ROWS + LABEL_ROWS, HEAD), BF16),
        in_specs=[SMEM_SPEC, SMEM_SPEC] + [pl.BlockSpec(memory_space=pltpu.HBM)] * 2,
        out_specs=VMEM_SPEC,
        scratch_shapes=[pltpu.SemaphoreType.DMA((2 * KV_HEADS,))],
        name="pack",
        compiler_params=pltpu.CompilerParams(vmem_limit_bytes=KERNEL_VMEM),
    )(
        parents,
        counts,
        pltpu.with_memory_space_constraint(keys, pltpu.HBM),
        pltpu.with_memory_space_constraint(values, pltpu.HBM),
    )


def finish_kernel(mine_ref, down_ref, up_ref, out_ref):
    for head in range(KV_HEADS):
        rows = block_rows(head)
        total = mine_ref[rows, :] + (
            down_ref[rows, :].astype(F32) + up_ref[rows, :].astype(F32)
        )
        out_ref[:, head * HEAD : (head + 1) * HEAD] = total.astype(BF16)


def finish(mine, down, up):
    return on_core(
        finish_kernel,
        "finish",
        jax.ShapeDtypeStruct((SEG_LEN, KV_COLS), BF16),
        [mine, down, up],
    )


def taken(array, index, axis):
    return lax.dynamic_index_in_dim(array, index, axis, keepdims=False)


def places():
    dp = lax.axis_index("dp")
    core = lax.rem(dp, CORES)
    x = lax.rem(lax.div(dp, CORES), X)
    y = lax.div(dp, CORES * X)
    return y, x, core


def load_kernel(q_ref, g_ref, hidden_ref, *refs):
    head_refs, share_refs, (buffer, head_sems, share_sems) = refs[:4], refs[4:-3], refs[-3:]
    copies = [
        pltpu.make_async_copy(ref, buffer.at[i], head_sems.at[i])
        for i, ref in enumerate((q_ref, g_ref))
    ]
    x = places()[1]
    for k, ref in enumerate(share_refs):
        to = lax.rem(x + k, X)
        for y in range(Y):
            first = pl.multiple_of((y * X + to) * SHARE, SHARE)
            copies.append(
                pltpu.make_async_copy(
                    hidden_ref.at[:, pl.ds(first, SHARE)],
                    ref.at[:, pl.ds(y * SHARE, SHARE)],
                    share_sems.at[k * Y + y],
                )
            )
    for copy in copies:
        copy.start()
    for i in range(2):
        copies[i].wait()
        rows_ref, turned_ref = head_refs[2 * i : 2 * i + 2]

        def one_group(group):
            for head in range(GROUP):
                part = aligned(group * GROUP_COLS + head * HEAD, HEAD)
                block = buffer[i, :, part]
                rows_ref[part, :] = block
                turned_ref[:, part] = block.T

        over(KV_HEADS, one_group, looped=True)
    for copy in copies[2:]:
        copy.wait()


def loaded(array_q, array_g, hidden):
    shapes = [(KV_HEADS * GROUP * SEG_LEN, HEAD), (HEAD, KV_HEADS * GROUP * SEG_LEN)] * 2
    shapes += [(SEG_LEN, Y * SHARE)] * X
    outs = pl.pallas_call(
        load_kernel,
        out_shape=[jax.ShapeDtypeStruct(shape, BF16) for shape in shapes],
        in_specs=[pl.BlockSpec(memory_space=pltpu.HBM)] * 3,
        out_specs=[VMEM_SPEC] * len(shapes),
        scratch_shapes=[
            pltpu.VMEM((2, SEG_LEN, Q_COLS), BF16),
            pltpu.SemaphoreType.DMA((2,)),
            pltpu.SemaphoreType.DMA((X * Y,)),
        ],
        name="load",
        compiler_params=pltpu.CompilerParams(vmem_limit_bytes=KERNEL_VMEM),
    )(*[pltpu.with_memory_space_constraint(a, pltpu.HBM) for a in (array_q, array_g, hidden)])
    return outs[:4], outs[4:]


def turn_kernel(*refs):
    part_refs, out_refs = refs[:X], refs[X:]
    here, _, core = places()
    for side, out_ref in enumerate(out_refs):
        for k in range(Y):
            of = lax.rem(here + k, Y) * CORES + lax.rem(core + side, CORES)
            first = pl.multiple_of(of * HEAD, HEAD)
            for i, ref in enumerate(part_refs):
                out_ref[k * HEAD : (k + 1) * HEAD, i * SEG_LEN : (i + 1) * SEG_LEN] = ref[
                    :, pl.ds(first, HEAD)
                ].T


def turned(parts):
    return on_core(
        turn_kernel,
        "turn",
        [jax.ShapeDtypeStruct((Y * HEAD, X * SEG_LEN), BF16)] * CORES,
        list(parts),
    )


def given_kernel(hidden_ref, *refs):
    token_refs, (out_ref,) = refs[:X], refs[X:]
    tokens = jnp.concatenate([ref[...] for ref in token_refs], axis=0)
    out_ref[...] = dot_nn(hidden_ref[...], tokens).astype(BF16)


def kept_kernel(hidden_ref, *refs):
    token_refs, got_ref, own_ref, out_refs = refs[:X], refs[X], refs[X + 1], refs[X + 2 :]
    tokens = jnp.concatenate([ref[...] for ref in token_refs], axis=0)
    total = dot_nn(hidden_ref[...], tokens) + got_ref[...].astype(F32)
    own_ref[...] = total[:HEAD]
    for k, ref in enumerate(out_refs):
        ref[...] = total[(k + 1) * HEAD : (k + 2) * HEAD].astype(BF16)


def all_grads(hidden, queries, keys, values, out_grad, parents, counts):
    barrier = lax.optimization_barrier
    own = ring_packet(
        keys.reshape(SEG_LEN, KV_COLS), values.reshape(SEG_LEN, KV_COLS), parents, counts
    )
    up, down = own, own
    below, above = {}, {}
    state, stats = (parents, counts), None
    for step in range(1, 5):
        if step == 2:
            heads, shares = loaded(
                queries.reshape(SEG_LEN, Q_COLS), out_grad.reshape(SEG_LEN, Q_COLS), hidden
            )
            up, down, *rest = barrier((up, down, *heads, *shares))
            heads, shares = rest[:4], rest[4:]
            hidden_parts = [
                shift_xy(share, k, 0) if k else share for k, share in enumerate(shares)
            ]
        if step == 3:
            state, stats = add_stats(heads, [own], [], state, None)
            up, down, state, stats = barrier((up, down, state, stats))
            label = shift_seq(up[PACKET_ROWS:], 2)
            stats, hidden_parts[1], hidden_parts[3] = barrier(
                (stats, hidden_parts[1], hidden_parts[3])
            )
        if step == 4:
            state, stats = add_stats(
                heads, [below[1], below[2]], [(1, False), (2, False)], state, stats
            )
            up, down, state, stats = barrier((up, down, state, stats))
            farthest = [shift_seq(up[:KV_COLS], 1), shift_seq(down[KV_COLS:PACKET_ROWS], -1)]
            break
        down, up = shift_seq(down, -1), shift_seq(up, 1)
        above[step], below[step] = down, up
    state, stats = add_stats(
        heads,
        [below[3], label, above[3], above[2], above[1]],
        [(3, False), (4, True), (5, False), (6, False), (7, False)],
        state,
        stats,
    )
    stats, hidden_parts[2] = barrier((stats, hidden_parts[2]))
    state, stats = add_stats(heads, farthest, [(4, False)], state, stats, last=True)

    dvs = {}
    acc, dk, dvs[4] = add_grads(heads, state, stats, farthest, [4], None, [BF16] * 2)
    down, up = shift_seq(dk, -1), None
    for step in range(3, 0, -1):
        starts = BF16 if step == 3 else F32
        acc, low, dvs[step], high, dvs[8 - step] = add_grads(
            heads,
            state,
            stats,
            [below[step], above[step]],
            [step, 8 - step],
            acc,
            [F32, starts, starts, F32],
        )
        acc, down = barrier((acc, down))
        down = shift_seq((low + down.astype(F32)).astype(BF16), -1)
        up = shift_seq(high if step == 3 else (high + up.astype(F32)).astype(BF16), 1)
    acc, *hidden_parts = barrier((acc, *turned(hidden_parts)))
    value_up = shift_seq(dvs[4], 1)
    acc, mine, dvs[0] = add_grads(heads, state, stats, [own], [0], acc, [F32] * 2, last=True)
    near = finish(mine, down, up)
    near, dvs[3], dvs[5] = barrier((near, dvs[3], dvs[5]))

    def value_step(step, value_up, value_down):
        value_up = (dvs[8 - step] + value_up.astype(F32)).astype(BF16)
        if value_down is None:
            value_down = dvs[step]
        else:
            value_down = (dvs[step] + value_down.astype(F32)).astype(BF16)
        return shift_seq(value_up, 1), shift_seq(value_down, -1)

    hidden_own, hidden_other = hidden_parts
    flops = 2 * X * SEG_LEN * Y * HEAD * KV_COLS
    tokens = [near] + [shift_xy(near, k, 0) for k in range(1, X)]
    value_up, value_down = value_step(3, value_up, None)
    given = on_core(
        given_kernel,
        "given",
        jax.ShapeDtypeStruct((Y * HEAD, KV_COLS), BF16),
        [hidden_other, *tokens],
        flops=flops,
    )
    given, value_up, value_down = barrier((given, value_up, value_down))
    value_up, value_down = value_step(2, value_up, value_down)
    kept, *low = on_core(
        kept_kernel,
        "kept",
        [jax.ShapeDtypeStruct((HEAD, KV_COLS), F32)]
        + [jax.ShapeDtypeStruct((HEAD, KV_COLS), BF16)] * (Y - 1),
        [hidden_own, *tokens, swap_cores(given)],
        flops=flops,
    )
    *low, dvs[1], dvs[7] = barrier((*low, dvs[1], dvs[7]))
    others = [shift_xy(low[k - 1], 0, k) for k in range(1, Y)]
    value_up, value_down = value_step(1, value_up, value_down)
    total = kept
    for other in others:
        total = total + other.astype(F32)
    total, value_up, value_down, acc = barrier(
        (total.astype(BF16), value_up, value_down, acc)
    )
    rows = lax.all_to_all(total, "seq", 0, 0, tiled=True)
    value_grad = finish(dvs[0], value_down, value_up)
    value_grad, acc = barrier((value_grad, acc))
    dq, key_grad = on_core(
        outputs_kernel,
        "outputs",
        [jax.ShapeDtypeStruct((SEG_LEN, n), BF16) for n in (Q_COLS, KV_COLS)],
        [acc, near],
    )
    weight_grad = jnp.sum(rows.reshape(SEGMENTS, -1, KV_COLS).astype(F32), axis=0)
    return dq, key_grad, value_grad, weight_grad


def local(hidden_in, queries, keys, values, out_grad, parents, counts):
    dq, key_grad, value_grad, weight_grad = all_grads(
        hidden_in.reshape(SEG_LEN, -1), queries, keys, values, out_grad, parents, counts
    )
    return (
        dq.reshape(1, 1, SEG_LEN, Q_COLS),
        key_grad.reshape(1, 1, SEG_LEN, KV_COLS),
        value_grad.reshape(1, 1, SEG_LEN, KV_COLS),
        weight_grad,
    )


def solution(mesh):
    wide = P("dp", "seq", None, None)
    return jax.shard_map(
        local,
        mesh=mesh,
        in_specs=(wide, wide, wide, wide, wide, P("dp", "seq"), P("dp", "seq")),
        out_specs=(wide, wide, wide, P(("dp", "seq"), None)),
        check_vma=False,
    )
```
